32 devices in a mesh: rows: 8 (over y, x, core), blk: 4 (over z).
Axes of the slice: x: 2, y: 2, z: 4, core: 2. Of those that a mesh axis runs over, the one named last changes fastest.
Arguments:
- tokens: bfloat16 [8, 512, 2048], P('rows', 'blk'), may hold values from -6 to 6
- segment_ids: int32 [8, 512], P('rows'), may hold values from 0 to 3, as said below
- mixer_gain: bfloat16 [2048], P(('rows', 'blk')), may hold values from 0.5 to 1.5
- branch_weight: bfloat16 [2048, 2736], P(('rows', 'blk')), may hold values from -0.125 to 0.125
- input_weight: bfloat16 [2048, 2736], P(('rows', 'blk')), may hold values from -0.125 to 0.125
- output_weight: bfloat16 [2048, 2736], P(('rows', 'blk')), may hold values from -0.3125 to 0.3125
- conv_weight: float32 [4, 2736], P(None, 'blk'), may hold values from -3 to 3
- conv_bias: float32 [2736], P('blk'), may hold values from -2 to 2
- decay_gate: float32 [16, 171, 171], P('blk'), may hold values from -0.4375 to 0.4375
- decay_bias: float32 [2736], P('blk'), may hold values from -3 to 3
- input_gate: float32 [16, 171, 171], P('blk'), may hold values from -0.4375 to 0.4375
- input_bias: float32 [2736], P('blk'), may hold values from -3 to 3
- decay_param: float32 [2736], P('blk')
- mlp_gain: bfloat16 [2048], P(('rows', 'blk')), may hold values from 0.5 to 1.5
- hidden_gate: bfloat16 [6144, 2048], P(('rows', 'blk')), may hold values from -0.125 to 0.125
- hidden_up: bfloat16 [6144, 2048], P(('rows', 'blk')), may hold values from -0.125 to 0.125
- hidden_down: bfloat16 [6144, 2048], P(('rows', 'blk')), may hold values from -0.109375 to 0.109375
- cotangent: bfloat16 [8, 512, 2048], P('rows', 'blk'), may hold values from -6 to 6
Outputs:
- block_out: bfloat16 [8, 512, 2048], P('rows', 'blk')
- token_grad: float32 [8, 512, 2048], P('rows', 'blk')
- mixer_gain_grad: float32 [2048], P(('rows', 'blk'))
- branch_weight_grad: float32 [2048, 2736], P(('rows', 'blk'))
- input_weight_grad: float32 [2048, 2736], P(('rows', 'blk'))
- output_weight_grad: float32 [2048, 2736], P(('rows', 'blk'))
- conv_weight_grad: float32 [4, 2736], P(None, 'blk')
- conv_bias_grad: float32 [2736], P('blk')
- decay_gate_grad: float32 [16, 171, 171], P('blk')
- decay_bias_grad: float32 [2736], P('blk')
- input_gate_grad: float32 [16, 171, 171], P('blk')
- input_bias_grad: float32 [2736], P('blk')
- decay_param_grad: float32 [2736], P('blk')
- mlp_gain_grad: float32 [2048], P(('rows', 'blk'))
- hidden_gate_grad: float32 [6144, 2048], P(('rows', 'blk'))
- hidden_up_grad: float32 [6144, 2048], P(('rows', 'blk'))
- hidden_down_grad: float32 [6144, 2048], P(('rows', 'blk'))
The draws below stay inside these ranges and needn't reach their ends.
Inputs may be any that keep to these rules, and one draw needn't show every extreme that they name: `segment_ids`: segment ids never fall along a row.
All inputs are finite; a program needn't handle non-finite values.
Results may differ from the reference program's by a relative error of at most 0.01.
Values may be sent and summed in bfloat16 or wider, within the bound.
No kernel may reach another device: no remote copies, remote signals or barrier semaphores. Data moves between devices by JAX's collectives and lax.ppermute only.
A program may use at most 832 MiB of HBM per device.

```python
import jax
import jax.numpy as jnp
from jax import lax

D = 2048
FF = 6144
HEADS = 16
BW = 171
CONV = 4
TOK_DEV = 128
R = 2736
SEQ = 512
BATCH = 8


def draw_segment_ids(key, part):
    key = jax.random.fold_in(key, 11)
    lead_key, tail_key, extra_key = jax.random.split(key, 3)
    lead = jax.random.randint(lead_key, (BATCH, 1), 1, TOK_DEV // 2)
    tail = SEQ - jax.random.randint(tail_key, (BATCH, 1), 2, TOK_DEV // 2 + 2)
    extra = jax.random.randint(extra_key, (BATCH, 1), 1, SEQ - tail)
    places = jnp.arange(SEQ, dtype=jnp.int32)[None, :]
    return (places >= lead).astype(jnp.int32) + (places >= tail).astype(jnp.int32) + (places >= tail + extra).astype(jnp.int32)


def draw_decay_param(key, part):
    key = jax.random.fold_in(key, 23)
    rate_key = jax.random.fold_in(key, 1)
    spread = jax.random.uniform(rate_key, (R,), jnp.float32)
    rate = jnp.exp(jnp.log(0.01 / SEQ) + spread * jnp.log(2.0 * SEQ))
    return -jnp.log(jnp.expm1(rate))


def levels(rng, dims, cuts, smallest, largest):
    level, own = 1.0, jax.random.fold_in(rng, 6)
    for dim, parts in cuts:
        steps = jnp.exp(jax.random.uniform(jax.random.fold_in(own, dim), (parts,), jnp.float32, smallest / len(cuts), largest / len(cuts)))
        level = level * jnp.repeat(steps, dims[dim] // parts).reshape([-1 if axis == dim else 1 for axis in range(len(dims))])
    return level


def normal_values(own_key, dims, deviation, reach, cuts=(), kind=jnp.bfloat16):
    array = jax.random.normal(own_key, dims, jnp.float32) * deviation
    if len(cuts) > 0:
        array = levels(own_key, dims, cuts, -0.22, 0.18) * array
    return jnp.clip(array, min=-reach, max=reach).astype(kind)


def setup_inputs(seed: int = 0) -> dict:
    seeds = jax.random.split(jax.random.key(seed), 19)
    return {
        "tokens": normal_values(seeds[0], (BATCH, SEQ, D), 1.0, 6.0, ((0, 8), (1, 4))),
        "segment_ids": draw_segment_ids(jax.random.fold_in(seeds[18], 71), 0),
        "mixer_gain": jnp.clip(1.0 + 0.1 * jax.random.normal(seeds[2], (D,), jnp.float32), 0.5, 1.5).astype(jnp.bfloat16),
        "branch_weight": normal_values(seeds[3], (D, R), D ** -0.5, 0.125, ((0, 32),)),
        "input_weight": normal_values(seeds[4], (D, R), D ** -0.5, 0.125, ((0, 32),)),
        "output_weight": normal_values(seeds[5], (D, R), (R // 9) ** -0.5, 0.3125, ((0, 32),)),
        "conv_weight": normal_values(seeds[6], (CONV, R), 0.5, 3.0, ((1, 4),), jnp.float32),
        "conv_bias": normal_values(seeds[7], (R,), 0.3, 2.0, ((0, 4),), jnp.float32),
        "decay_gate": normal_values(seeds[8], (HEADS, BW, BW), BW ** -0.5, 0.4375, ((0, 4),), jnp.float32),
        "decay_bias": normal_values(seeds[9], (R,), 0.5, 3.0, ((0, 4),), jnp.float32),
        "input_gate": normal_values(seeds[10], (HEADS, BW, BW), BW ** -0.5, 0.4375, ((0, 4),), jnp.float32),
        "input_bias": normal_values(seeds[11], (R,), 0.5, 3.0, ((0, 4),), jnp.float32),
        "decay_param": draw_decay_param(jax.random.fold_in(seeds[18], 71), 0),
        "mlp_gain": jnp.clip(1.0 + 0.1 * jax.random.normal(seeds[13], (D,), jnp.float32), 0.5, 1.5).astype(jnp.bfloat16),
        "hidden_gate": normal_values(seeds[14], (FF, D), D ** -0.5, 0.125, ((0, 32),)),
        "hidden_up": normal_values(seeds[15], (FF, D), D ** -0.5, 0.125, ((0, 32),)),
        "hidden_down": normal_values(seeds[16], (FF, D), (FF // 2) ** -0.5, 0.109375, ((0, 32),)),
        "cotangent": normal_values(seeds[17], (BATCH, SEQ, D), 1.0, 6.0, ((0, 8), (1, 4))),
    }


@jax.custom_vjp
def low(v):
    return lax.optimization_barrier(v.astype(jnp.bfloat16)).astype(jnp.float32)

@jax.custom_vjp
def low_back(v):
    return v

def low_keep(v):
    return (low(v), None)

def low_pass(kept, grad):
    return (grad,)

def back_keep(v):
    return (v, None)

def back_low(kept, grad):
    return (low(grad),)
low.defvjp(low_keep, low_pass)
low_back.defvjp(back_keep, back_low)
epsilon = 1e-06
scale_c = 8.0
highest = lax.Precision.HIGHEST

def rms_unit(values):
    return values * lax.rsqrt(lax.optimization_barrier(jnp.mean(values * values, axis=-1, keepdims=True)) + epsilon)

def gelu_tanh(values):
    return jax.nn.gelu(values, approximate=True)

def matmul(left, right):
    return jnp.dot(left, right, preferred_element_type=jnp.float32, precision=highest)

def gated_terms(signal, segments, params):
    conv_weight, conv_bias, decay_gate, decay_bias, input_gate, input_bias, decay_param = params
    length, channels = signal.shape
    tap_count = conv_weight.shape[0]
    conv_out = conv_bias[None, :] + conv_weight[0][None, :] * signal
    for offset in range(1, tap_count):
        shifted = jnp.concatenate([jnp.zeros((offset, channels), jnp.float32), signal[:-offset]], axis=0)
        earlier_ids = jnp.concatenate([jnp.full((offset,), -1, jnp.int32), segments[:-offset]], axis=0)
        matches = (earlier_ids == segments).astype(jnp.float32)
        conv_out = conv_out + conv_weight[offset][None, :] * shifted * matches[:, None]
    blocks = conv_out.reshape(length, decay_gate.shape[0], decay_gate.shape[1])
    decay_pre = jnp.einsum('shc,hcd->shd', blocks, decay_gate, precision=highest).reshape(length, channels) + decay_bias[None, :]
    input_pre = jnp.einsum('shc,hcd->shd', blocks, input_gate, precision=highest).reshape(length, channels) + input_bias[None, :]
    decay_rate = jax.nn.sigmoid(decay_pre)
    input_rate = jax.nn.sigmoid(input_pre)
    restart = jnp.concatenate([jnp.ones((1,), jnp.float32), (segments[1:] != segments[:-1]).astype(jnp.float32)])[:, None]
    log_decay = -scale_c * jax.nn.softplus(-decay_param)[None, :] * decay_rate
    scaled = restart + (1.0 - restart) * jnp.sqrt(-jnp.expm1(2.0 * log_decay))
    carried = (1.0 - restart) * jnp.exp(log_decay)
    return (carried, scaled * input_rate * conv_out)

def forward(residual_in, segments, params):
    mixer_gain, branch_weight, input_weight, output_weight, conv_weight, conv_bias, decay_gate, decay_bias, input_gate, input_bias, decay_param, mlp_gain, hidden_gate, hidden_up, hidden_down = params
    mixer_normed = low(rms_unit(residual_in) * mixer_gain[None, :])
    branch_pre = low_back(matmul(mixer_normed, branch_weight))
    signal = low_back(low(matmul(mixer_normed, input_weight)))
    carried, driven = gated_terms(signal, segments, (conv_weight, conv_bias, decay_gate, decay_bias, input_gate, input_bias, decay_param))

    def advance(hidden_state, factors):
        hidden_state = factors[0] * hidden_state + factors[1]
        return (hidden_state, hidden_state)
    _, states = lax.scan(advance, jnp.zeros((signal.shape[1],), jnp.float32), (carried, driven))
    state_values = low_back(low(states))
    mixed = low(gelu_tanh(branch_pre) * state_values)
    residual_mid = residual_in + low_back(matmul(mixed, output_weight.T))
    mlp_normed = low(rms_unit(residual_mid) * mlp_gain[None, :])
    gate_vals = low_back(matmul(mlp_normed, hidden_gate.T))
    up_vals = low_back(matmul(mlp_normed, hidden_up.T))
    hidden_vals = low(gelu_tanh(gate_vals) * up_vals)
    return residual_mid + low_back(matmul(hidden_vals, hidden_down))

def reference(tokens, segment_ids, mixer_gain, branch_weight, input_weight, output_weight, conv_weight, conv_bias, decay_gate, decay_bias, input_gate, input_bias, decay_param, mlp_gain, hidden_gate, hidden_up, hidden_down, cotangent):
    params = (mixer_gain.astype(jnp.float32), branch_weight.astype(jnp.float32), input_weight.astype(jnp.float32), output_weight.astype(jnp.float32), conv_weight.astype(jnp.float32), conv_bias.astype(jnp.float32), decay_gate.astype(jnp.float32), decay_bias.astype(jnp.float32), input_gate.astype(jnp.float32), input_bias.astype(jnp.float32), decay_param.astype(jnp.float32), mlp_gain.astype(jnp.float32), hidden_gate.astype(jnp.float32), hidden_up.astype(jnp.float32), hidden_down.astype(jnp.float32))

    def one_row(totals, row_data):
        row_tokens, row_segments, row_cotangent = row_data
        row_out, pullback = jax.vjp(lambda values, weights: forward(values, row_segments, weights), row_tokens.astype(jnp.float32), params)
        row_grad, weight_grads = pullback(row_cotangent.astype(jnp.float32))
        totals = jax.tree.map(jnp.add, totals, weight_grads)
        return (totals, (row_out.astype(jnp.bfloat16), row_grad))
    sums, (block_out, token_grad) = lax.scan(one_row, jax.tree.map(jnp.zeros_like, params), (tokens, segment_ids, cotangent))
    return (block_out, token_grad, sums[0], sums[1], sums[2], sums[3], sums[4], sums[5], sums[6], sums[7], sums[8], sums[9], sums[10], sums[11], sums[12], sums[13], sums[14])
```

```python
import functools

import jax
import jax.numpy as jnp
from jax import lax
from jax.experimental import pallas as pl
from jax.experimental.pallas import tpu as pltpu
from jax.sharding import PartitionSpec as P

epsilon = 1e-06
scale_c = 8.0
bf16 = jnp.bfloat16
f32 = jnp.float32
chunk = 64
vmem_limit = 48 * 1024 * 1024


def rms_scale(values):
    return lax.rsqrt(jnp.mean(values * values, axis=-1, keepdims=True) + epsilon)


def gelu_tanh(values):
    return jax.nn.gelu(values, approximate=True)


def mm(left, right, dims):
    return lax.dot_general(left, right, (dims, ((), ())), preferred_element_type=f32)


def tie(*values):
    return lax.optimization_barrier(values)


def flip(size, bit):
    return [(place, place ^ bit) for place in range(size)]


def bits_of(size):
    found, bit = [], 1
    while bit < size:
        found.append(bit)
        bit *= 2
    return found


def swap_blk(parts):
    return lax.all_to_all(parts, "blk", split_axis=0, concat_axis=0, tiled=True)


def gather_blk(part, size):
    return swap_blk(jnp.broadcast_to(part[None], (size,) + part.shape))


def halve(total, size, bit, left):
    axis = left.index(bit)
    left.remove(bit)
    mine = (lax.axis_index("rows") // bit) % 2
    away = lax.dynamic_index_in_dim(total, 1 - mine, axis, keepdims=False)
    keep = lax.dynamic_index_in_dim(total, mine, axis, keepdims=False)
    got = lax.ppermute(away.astype(bf16), "rows", flip(size, bit))
    return keep.astype(f32) + got.astype(f32), got


def by_bits(total, size):
    left = list(reversed(bits_of(size)))
    return total.reshape((2,) * len(left) + (total.shape[0] // size,) + total.shape[1:]), left


def sum_rows(value, size, wire=f32):
    for bit in bits_of(size):
        value = value + lax.ppermute(value.astype(wire), "rows", flip(size, bit)).astype(f32)
    return value


def sum_blk(value, size):
    for bit in bits_of(size):
        value = value + lax.ppermute(value, "blk", flip(size, bit))
    return value


def split_columns_kernel(
    width, wide, input_ref, branch_ref, output_ref, mixer_ref, mlp_ref, both_ref
):
    parts = both_ref.shape[0]
    both_ref[...] = jnp.zeros_like(both_ref)
    for part in range(parts):
        cut = slice(part * width, (part + 1) * width)
        both_ref[part, :, :width] = input_ref[:, cut]
        both_ref[part, :, wide : wide + width] = branch_ref[:, cut]
        both_ref[part, :, 2 * wide : 2 * wide + width] = output_ref[:, cut]
        both_ref[part, :, width : width + 1] = mixer_ref[...]
        both_ref[part, :, width + 1 : width + 2] = mlp_ref[...]


def join_columns_kernel(width, wide, parts_ref, *out_refs):
    for part in range(parts_ref.shape[0]):
        cut = slice(part * width, (part + 1) * width)
        for number, out_ref in enumerate(out_refs):
            begin = number * wide
            out_ref[:, cut] = parts_ref[part, :, begin : begin + width].astype(f32)


def mixer_norm_kernel(gain_ref, tokens_ref, out_ref):
    step = 32

    def rows_step(index, carry):
        here = pl.ds(pl.multiple_of(index * step, step), step)
        values = tokens_ref[here, :].astype(f32)
        out_ref[here, :] = (values * rms_scale(values) * gain_ref[...]).astype(bf16)
        return carry

    lax.fori_loop(0, tokens_ref.shape[0] // step, rows_step, 0)


def sum_parts(parts_ref, here):
    total = parts_ref[0, here, :].astype(f32)
    for part in range(1, parts_ref.shape[0]):
        total = total + parts_ref[part, here, :].astype(f32)
    return total


def mid_norm_kernel(gain_ref, tokens_ref, parts_ref, mid_ref, normed_ref):
    step = 32

    def rows_step(index, carry):
        here = pl.ds(pl.multiple_of(index * step, step), step)
        values = tokens_ref[here, :].astype(f32) + sum_parts(parts_ref, here)
        mid_ref[here, :] = values
        normed_ref[here, :] = (values * rms_scale(values) * gain_ref[...]).astype(bf16)
        return carry

    lax.fori_loop(0, tokens_ref.shape[0] // step, rows_step, 0)


def fold8(value):
    return value.reshape(value.shape[0] // 8, 8, value.shape[1]).sum(axis=0)


def norm_back(grad, values, gain):
    scale = rms_scale(values)
    product = grad * values
    factor = scale * scale * scale * jnp.mean(product * gain, axis=-1, keepdims=True)
    return scale * (grad * gain) - values * factor, product * scale


def mid_grad_kernel(gain_ref, mid_ref, cotangent_ref, parts_ref, grad_ref, sent_ref, sums_ref):
    step = 32
    sums_ref[...] = jnp.zeros_like(sums_ref)

    def rows_step(index, carry):
        here = pl.ds(pl.multiple_of(index * step, step), step)
        change, terms = norm_back(sum_parts(parts_ref, here), mid_ref[here, :], gain_ref[...])
        sums_ref[...] += fold8(terms)
        result = cotangent_ref[here, :].astype(f32) + change
        grad_ref[here, :] = result
        sent_ref[here, :] = result.astype(bf16)
        return carry

    lax.fori_loop(0, mid_ref.shape[0] // step, rows_step, 0)


def pack_grad_kernel(partial_ref, tokens_ref, sent_ref, sums_ref):
    step = 32
    sums_ref[...] = jnp.zeros_like(sums_ref)

    def rows_step(index, carry):
        here = pl.ds(pl.multiple_of(index * step, step), step)
        values = tokens_ref[here, :].astype(f32)
        grad = partial_ref[here, :]
        sums_ref[...] += fold8(values * rms_scale(values) * grad)
        sent_ref[here, :] = grad.astype(bf16)
        return carry

    lax.fori_loop(0, partial_ref.shape[0] // step, rows_step, 0)


def token_grad_kernel(gain_ref, tokens_ref, mid_grad_ref, parts_ref, grad_ref):
    step = 32

    def rows_step(index, carry):
        here = pl.ds(pl.multiple_of(index * step, step), step)
        values = tokens_ref[here, :].astype(f32)
        change, _ = norm_back(sum_parts(parts_ref, here), values, gain_ref[...])
        grad_ref[here, :] = mid_grad_ref[here, :] + change
        return carry

    lax.fori_loop(0, tokens_ref.shape[0] // step, rows_step, 0)


def local_kernel(kernel, name, operands, outs, scratch=()):
    return pl.pallas_call(
        kernel,
        out_shape=[jax.ShapeDtypeStruct(shape, kind) for shape, kind in outs],
        in_specs=[pl.BlockSpec(memory_space=pltpu.VMEM)] * len(operands),
        out_specs=[pl.BlockSpec(memory_space=pltpu.VMEM)] * len(outs),
        scratch_shapes=list(scratch),
        compiler_params=pltpu.CompilerParams(vmem_limit_bytes=vmem_limit),
        name=name,
    )(*operands)


def round_up(value):
    return -(-value // 128) * 128


def column_tiles(width, wide, block):
    tiles = []
    for start in range(0, wide, 256):
        stop = min(start + 256, wide)
        low = (start // block) * block
        high = ((min(stop, width) - 1) // block + 1) * block
        tiles.append((start, stop, low // 128 * 128, min(round_up(high), wide)))
    return tiles


def split_bf16(value):
    high = value.astype(bf16)
    return high, (value - high.astype(f32)).astype(bf16)


def one_minus_exp(value):
    series = 1.0 + value * (1.0 / 8.0)
    for term in (7.0, 6.0, 5.0, 4.0, 3.0, 2.0):
        series = 1.0 + value * (1.0 / term) * series
    return jnp.where(value > -0.3, -value * series, 1.0 - jnp.exp(value))


def shift_down(tile, count, fill):
    moved = pltpu.roll(tile, count, 0)
    row = lax.broadcasted_iota(jnp.int32, tile.shape, 0)
    return jnp.where(row < count, fill, moved)


def shift_up(tile, count, fill):
    moved = pltpu.roll(tile, tile.shape[0] - count, 0)
    row = lax.broadcasted_iota(jnp.int32, tile.shape, 0)
    return jnp.where(row >= tile.shape[0] - count, fill, moved)


def blocked_product(first, second, weights, tiles, store, length, turned=False):
    step = 256

    def rows_step(index, carry):
        rows = pl.ds(pl.multiple_of(index * step, step), step)
        for start, stop, low, high in tiles:
            total = None
            for (high_ref, low_ref), (w_high, w_low) in zip((first, second), weights):
                if high_ref is None:
                    continue
                a_high = high_ref[rows, low:high]
                a_low = low_ref[rows, low:high]
                cut = (slice(start, stop), slice(low, high))
                cut = cut if turned else cut[::-1]
                b_high, b_low = w_high[cut], w_low[cut]
                dims = ((1,), (1,)) if turned else ((1,), (0,))
                part = mm(a_high, b_high, dims) + mm(a_high, b_low, dims) + mm(a_low, b_high, dims)
                total = part if total is None else total + part
            store(rows, slice(start, stop), total)
        return carry

    lax.fori_loop(0, length // step, rows_step, 0)


def recur_forward_kernel(
    tiles,
    signal_ref,
    masks_ref,
    vectors_ref,
    decay_high,
    decay_low,
    input_high,
    input_low,
    states_ref,
    values_ref,
    conv_ref,
    decay_rate_ref,
    input_rate_ref,
    padded,
    conv_high,
    conv_low,
):
    length, width = signal_ref.shape
    count = length // chunk
    padded[0:8, :] = jnp.zeros((8, width), f32)

    def pad_step(index, carry):
        begin = pl.multiple_of(index * chunk, chunk)
        here = pl.ds(begin, chunk)
        padded[pl.ds(begin + 8, chunk), :] = signal_ref[here, :].astype(f32)
        return carry

    lax.fori_loop(0, count, pad_step, 0)

    def conv_step(index, carry):
        begin = pl.multiple_of(index * chunk, chunk)
        rows = pl.ds(begin, chunk)
        window = padded[pl.ds(begin, chunk + 8), :]
        total = vectors_ref[4:5, :] + vectors_ref[0:1, :] * window[8:, :]
        for tap in range(1, 4):
            total = total + vectors_ref[tap : tap + 1, :] * (
                window[8 - tap : 8 - tap + chunk, :] * masks_ref[rows, tap : tap + 1]
            )
        conv_ref[rows, :] = total
        high, low = split_bf16(total)
        conv_high[rows, :] = high
        conv_low[rows, :] = low
        return carry

    lax.fori_loop(0, count, conv_step, 0)

    def store_decay(rows, columns, value):
        decay_rate_ref[rows, columns] = jax.nn.sigmoid(value + vectors_ref[5:6, columns])

    def store_input(rows, columns, value):
        input_rate_ref[rows, columns] = jax.nn.sigmoid(value + vectors_ref[6:7, columns])

    nothing = (None, None)
    blocked_product(
        (conv_high, conv_low), nothing, ((decay_high, decay_low), nothing), tiles, store_decay, length
    )
    blocked_product(
        (conv_high, conv_low), nothing, ((input_high, input_low), nothing), tiles, store_input, length
    )

    def scan_step(index, state):
        begin = pl.multiple_of(index * 8, 8)
        rows = pl.ds(begin, 8)
        restart = masks_ref[rows, 4:5]
        keep = 1.0 - restart
        log_decay = -vectors_ref[7:8, :] * decay_rate_ref[rows, :]
        mult = restart + keep * jnp.sqrt(one_minus_exp(2.0 * log_decay))
        carried = keep * jnp.exp(log_decay)
        total = mult * input_rate_ref[rows, :] * conv_ref[rows, :]
        for count_rows in (1, 2, 4):
            total = total + carried * shift_down(total, count_rows, 0.0)
            carried = carried * shift_down(carried, count_rows, 1.0)
        total = total + carried * state
        states_ref[rows, :] = total
        return total[7:8, :]

    lax.fori_loop(0, length // 8, scan_step, jnp.zeros((1, width), f32), unroll=4)

    def values_step(index, carry):
        begin = pl.multiple_of(index * chunk, chunk)
        here = pl.ds(begin, chunk)
        values_ref[here, :] = states_ref[pl.ds(begin, chunk), :].astype(bf16)
        return carry

    lax.fori_loop(0, count, values_step, 0)


def recur_backward_kernel(
    tiles,
    grad_ref,
    signal_ref,
    masks_ref,
    vectors_ref,
    decay_high,
    decay_low,
    input_high,
    input_low,
    states_ref,
    conv_ref,
    decay_rate_ref,
    input_rate_ref,
    signal_grad_ref,
    decay_pre_ref,
    input_pre_ref,
    sums_ref,
    padded,
    grads,
    earlier,
    decay_pre_high,
    decay_pre_low,
    input_pre_high,
    input_pre_low,
):
    length, width = signal_ref.shape
    count = length // chunk
    padded[0:8, :] = jnp.zeros((8, width), f32)
    earlier[0:8, :] = jnp.zeros((8, width), f32)

    def pad_step(index, carry):
        begin = pl.multiple_of(index * chunk, chunk)
        here = pl.ds(begin, chunk)
        padded[pl.ds(begin + 8, chunk), :] = signal_ref[here, :].astype(f32)
        earlier[pl.ds(begin + 8, chunk), :] = states_ref[pl.ds(begin, chunk), :]
        grads[pl.ds(begin, chunk), :] = grad_ref[here, :].astype(f32)
        return carry

    lax.fori_loop(0, count, pad_step, 0)
    grads[length:, :] = jnp.zeros((8, width), f32)
    sums_ref[...] = jnp.zeros_like(sums_ref)

    def scan_step(index, later):
        begin = pl.multiple_of(length - 8 - index * 8, 8)
        rows = pl.ds(begin, 8)
        restart = masks_ref[rows, 4:5]
        keep = 1.0 - restart
        decay_rate = decay_rate_ref[rows, :]
        input_rate = input_rate_ref[rows, :]
        conv_out = conv_ref[rows, :]
        log_decay = -vectors_ref[7:8, :] * decay_rate
        decay = jnp.exp(log_decay)
        root = jnp.sqrt(one_minus_exp(2.0 * log_decay))
        mult = restart + keep * root
        carried = keep * decay
        flow = grads[rows, :]
        reach = shift_up(carried, 1, 1.0)
        for count_rows in (1, 2, 4):
            flow = flow + reach * shift_up(flow, count_rows, 0.0)
            reach = reach * shift_up(reach, count_rows, 1.0)
        flow = flow + reach * later
        window = earlier[pl.ds(begin, 16), :]
        before = window[7:15, :]
        flow_rate = flow * input_rate
        mult_grad = flow_rate * conv_out
        log_grad = keep * (flow * before * decay - mult_grad * decay * decay / root)
        rate_log = decay_rate * log_grad
        decay_pre = -vectors_ref[7:8, :] * rate_log * (1.0 - decay_rate)
        input_pre = mult_grad * mult * (1.0 - input_rate)
        grads[rows, :] = flow_rate * mult
        decay_pre_ref[rows, :] = decay_pre
        input_pre_ref[rows, :] = input_pre
        sums_ref[0:8, :] += rate_log
        sums_ref[8:16, :] += decay_pre
        sums_ref[16:24, :] += input_pre
        return carried[0:1, :] * flow[0:1, :]

    lax.fori_loop(0, length // 8, scan_step, jnp.zeros((1, width), f32), unroll=4)

    def split_step(index, carry):
        rows = pl.ds(pl.multiple_of(index * chunk, chunk), chunk)
        decay_pre_high[rows, :], decay_pre_low[rows, :] = split_bf16(decay_pre_ref[rows, :])
        input_pre_high[rows, :], input_pre_low[rows, :] = split_bf16(input_pre_ref[rows, :])
        return carry

    lax.fori_loop(0, count, split_step, 0)

    def store(rows, columns, value):
        grads[rows, columns] += value

    blocked_product(
        (decay_pre_high, decay_pre_low),
        (input_pre_high, input_pre_low),
        ((decay_high, decay_low), (input_high, input_low)),
        tiles,
        store,
        length,
        True,
    )

    def conv_step(index, carry):
        begin = pl.multiple_of(index * chunk, chunk)
        rows = pl.ds(begin, chunk)
        grad_window = grads[pl.ds(begin, chunk + 8), :]
        mask_window = masks_ref[pl.ds(begin, chunk + 8), :]
        signal_window = padded[pl.ds(begin, chunk + 8), :]
        here = grad_window[:chunk, :]
        result = vectors_ref[0:1, :] * here
        sums_ref[24:32, :] += fold8(here)
        sums_ref[32:40, :] += fold8(here * signal_window[8:, :])
        for tap in range(1, 4):
            masked = grad_window * mask_window[:, tap : tap + 1]
            result = result + vectors_ref[tap : tap + 1, :] * masked[tap : tap + chunk, :]
            sums_ref[32 + 8 * tap : 40 + 8 * tap, :] += fold8(
                masked[:chunk, :] * signal_window[8 - tap : 8 - tap + chunk, :]
            )
        here = pl.ds(begin, chunk)
        signal_grad_ref[here, :] = result.astype(bf16)
        return carry

    lax.fori_loop(0, count, conv_step, 0)


def recur_forward(signal, masks, vectors, weights, tiles):
    length, width = signal.shape
    whole = ((length, width), f32)
    return local_kernel(
        functools.partial(recur_forward_kernel, tiles),
        "recur_forward",
        (signal, masks, vectors, *weights),
        [whole, ((length, width), bf16), whole, whole, whole],
        [
            pltpu.VMEM((length + 8, width), f32),
            pltpu.VMEM((length, width), bf16),
            pltpu.VMEM((length, width), bf16),
        ],
    )


def recur_backward(state_grad, signal, masks, vectors, weights, saved, tiles):
    length, width = signal.shape
    whole = ((length, width), f32)
    pair = pltpu.VMEM((length, width), bf16)
    padded = pltpu.VMEM((length + 8, width), f32)
    return local_kernel(
        functools.partial(recur_backward_kernel, tiles),
        "recur_backward",
        (state_grad, signal, masks, vectors, *weights, *saved),
        [((length, width), bf16), whole, whole, ((64, width), f32)],
        [padded] * 3 + [pair] * 4,
    )


def dense_kernel(decay_ref, input_ref, decay_high, decay_low, input_high, input_low):
    heads, block, _ = decay_ref.shape
    for ref, high, low in (
        (decay_ref, decay_high, decay_low),
        (input_ref, input_high, input_low),
    ):
        high[...] = jnp.zeros_like(high)
        low[...] = jnp.zeros_like(low)
        for head in range(heads):
            cut = slice(head * block, (head + 1) * block)
            high[cut, cut], low[cut, cut] = split_bf16(ref[head])


def diagonal_blocks(left, right, heads, block):
    dense = lax.dot_general(
        left,
        right,
        (((0,), (0,)), ((), ())),
        precision=lax.Precision.HIGH,
        preferred_element_type=f32,
    )
    cuts = [slice(head * block, (head + 1) * block) for head in range(heads)]
    return jnp.stack([dense[cut, cut] for cut in cuts])


def unit_grads_kernel(*refs):
    count = (len(refs) - 1) // 2
    out_ref = refs[-1]
    for number in range(count):
        left_ref, right_ref = refs[number], refs[count + number]
        value = mm(left_ref[...], right_ref[...], ((0,), (0,))).astype(bf16)
        out_ref[:, number] = value.reshape(out_ref.shape[0], *out_ref.shape[2:])


def unit_grads(lefts, rights, parts):
    length, total = lefts[0].shape
    units = total // parts
    model_width = rights[0].shape[1]
    group = 1
    while group * units % 128:
        group *= 2
    count = len(lefts)
    return pl.pallas_call(
        unit_grads_kernel,
        grid=(parts // group,),
        out_shape=jax.ShapeDtypeStruct((parts, count, units, model_width), bf16),
        in_specs=[pl.BlockSpec((length, group * units), lambda i: (0, i))] * count
        + [pl.BlockSpec((length, model_width), lambda i: (0, 0))] * count,
        out_specs=pl.BlockSpec((group, count, units, model_width), lambda i: (i, 0, 0, 0)),
        compiler_params=pltpu.CompilerParams(vmem_limit_bytes=vmem_limit),
        cost_estimate=pl.CostEstimate(flops=1024, bytes_accessed=1024, transcendentals=0),
        name="unit_grads",
    )(*lefts, *rights)


def body(
    sizes,
    tokens,
    segment_ids,
    mixer_gain,
    branch_weight,
    input_weight,
    output_weight,
    conv_weight,
    conv_bias,
    decay_gate,
    decay_bias,
    input_gate,
    input_bias,
    decay_param,
    mlp_gain,
    hidden_gate,
    hidden_up,
    hidden_down,
    cotangent,
):
    n_rows, n_blk = sizes
    own_tokens, own_grad = tokens[0], cotangent[0]
    segments = segment_ids[0]
    tok_count, model_width = own_tokens.shape
    width = conv_weight.shape[1]
    wide = round_up(width + 2)
    heads, block, _ = decay_gate.shape
    tiles = column_tiles(width, wide, block)
    row, blk = lax.axis_index("rows"), lax.axis_index("blk")
    square = (tok_count, model_width)
    shard = branch_weight.shape[0]
    units = hidden_gate.shape[0]

    (column_parts,) = local_kernel(
        functools.partial(split_columns_kernel, width, wide),
        "split_columns",
        (input_weight, branch_weight, output_weight, mixer_gain[:, None], mlp_gain[:, None]),
        [((n_blk, shard, 3 * wide), bf16)],
    )
    columns = swap_blk(column_parts).reshape(n_blk * shard, 3 * wide)
    columns, token_own = tie(columns, own_tokens)
    both_columns = lax.all_gather(columns[:, : 2 * wide], "rows", axis=0, tiled=True)
    output_columns = lax.all_gather(columns[:, 2 * wide :], "rows", axis=0, tiled=True)
    tokens_all = gather_blk(token_own, n_blk).reshape(n_blk * tok_count, model_width)
    tokens_all, hidden_gate, hidden_up, hidden_down = tie(
        tokens_all, hidden_gate, hidden_up, hidden_down
    )
    gate_units = lax.all_gather(hidden_gate, "rows", axis=0, tiled=True)
    up_units = lax.all_gather(hidden_up, "rows", axis=0, tiled=True)
    down_units = lax.all_gather(hidden_down, "rows", axis=0, tiled=True)

    gains = both_columns[:, width : width + 2].astype(f32).T
    mixer_gains, mlp_gains = gains[0:1], gains[1:2]

    masks = [jnp.ones_like(segments, dtype=f32)]
    for tap in range(1, 4):
        masks.append(
            jnp.concatenate(
                [jnp.zeros((tap,), f32), (segments[tap:] == segments[:-tap]).astype(f32)]
            )
        )
    masks.append(1.0 - masks[1])
    masks = jnp.pad(jnp.stack(masks, axis=1), ((0, 8), (0, 3)))
    vectors = jnp.concatenate(
        [
            conv_weight,
            conv_bias[None],
            decay_bias[None],
            input_bias[None],
            scale_c * jax.nn.softplus(-decay_param)[None],
        ],
        axis=0,
    )
    vectors = jnp.pad(vectors, ((0, 0), (0, wide - width)), constant_values=1.0)
    weights = local_kernel(
        dense_kernel, "dense_gates", (decay_gate, input_gate), [((wide, wide), bf16)] * 4
    )
    (mixer_normed,) = local_kernel(
        mixer_norm_kernel,
        "mixer_norm",
        (mixer_gains, tokens_all),
        [((n_blk * tok_count, model_width), bf16)],
    )
    mixer_normed, grad_own = tie(mixer_normed, own_grad)
    out_grad = gather_blk(grad_own, n_blk).reshape(n_blk * tok_count, model_width)
    both_pre = mm(mixer_normed, both_columns, ((1,), (0,)))
    signal, branch_pre = both_pre[:, :wide].astype(bf16), both_pre[:, wide:]
    states, state_values, conv_out, decay_rate, input_rate = recur_forward(
        signal, masks, vectors, weights, tiles
    )
    branch_act, branch_pullback = jax.vjp(gelu_tanh, branch_pre)
    mixed = (branch_act * state_values.astype(f32)).astype(bf16)
    mixed, out_grad = tie(mixed, out_grad)

    def scatter_blk(partial):
        return swap_blk(partial.astype(bf16).reshape(n_blk, tok_count, model_width))

    mid_parts = scatter_blk(mm(mixed, output_columns, ((1,), (1,))))
    residual_mid, own_normed = local_kernel(
        mid_norm_kernel,
        "mid_norm",
        (mlp_gains, own_tokens, mid_parts),
        [(square, f32), (square, bf16)],
    )

    mlp_normed = gather_blk(own_normed, n_blk).reshape(n_blk * tok_count, model_width)
    gate_vals = mm(mlp_normed, gate_units, ((1,), (1,)))
    up_vals = mm(mlp_normed, up_units, ((1,), (1,)))
    gate_act, gate_pullback = jax.vjp(gelu_tanh, gate_vals)
    hidden_vals = (gate_act * up_vals).astype(bf16)
    hidden_grad = mm(out_grad, down_units, ((1,), (1,)))
    gate_grad = gate_pullback(hidden_grad * up_vals)[0].astype(bf16)
    up_grad = (hidden_grad * gate_act).astype(bf16)

    normed_partial = (
        mm(gate_grad, gate_units, ((1,), (0,))) + mm(up_grad, up_units, ((1,), (0,)))
    ).astype(bf16)
    normed_partial, gate_grad, up_grad, hidden_vals = tie(
        normed_partial, gate_grad, up_grad, hidden_vals
    )
    normed_parts = scatter_blk(normed_partial)
    unit_sums = unit_grads(
        (gate_grad, up_grad, hidden_vals), (mlp_normed, mlp_normed, out_grad), n_rows
    )
    out_partial = mm(hidden_vals, down_units, ((1,), (0,))).astype(bf16)
    normed_parts, _, out_partial = tie(normed_parts, unit_sums, out_partial)
    unit_sums = lax.psum_scatter(
        unit_sums.reshape(n_rows * 3 * units, model_width),
        "rows",
        scatter_dimension=0,
        tiled=True,
    )

    mid_grad, own_sent, mlp_gain_part = local_kernel(
        mid_grad_kernel,
        "mid_grad",
        (mlp_gains, residual_mid, own_grad, normed_parts),
        [(square, f32), (square, bf16), ((8, model_width), f32)],
    )
    mid_sent = gather_blk(own_sent, n_blk).reshape(n_blk * tok_count, model_width)

    mid_sent, out_partial = tie(mid_sent, out_partial)
    out_parts = scatter_blk(out_partial)
    mixed_grad = mm(mid_sent, output_columns, ((1,), (0,)))
    state_grad = (mixed_grad * branch_act).astype(bf16)
    branch_grad = branch_pullback(mixed_grad * state_values.astype(f32))[0].astype(bf16)

    def column_grads(left, right):
        partial = mm(left, right, ((0,), (0,))).astype(bf16)
        return partial.reshape(n_rows, 1, n_blk * shard, -1)

    early_sum = jnp.concatenate(
        [column_grads(mid_sent, mixed), column_grads(mixer_normed, branch_grad)], axis=1
    )
    signal_grad, decay_pre_grad, input_pre_grad, sums = recur_backward(
        state_grad,
        signal,
        masks,
        vectors,
        weights,
        (states, conv_out, decay_rate, input_rate),
        tiles,
    )
    signal_grad, out_parts = tie(signal_grad, out_parts)
    both_grad = jnp.concatenate([signal_grad, branch_grad], axis=1)
    partial = mm(both_grad, both_columns, ((1,), (1,)))
    token_sent, mixer_gain_part = local_kernel(
        pack_grad_kernel,
        "pack_grad",
        (partial, tokens_all),
        [((n_blk * tok_count, model_width), bf16), ((8, model_width), f32)],
    )
    token_parts = scatter_blk(token_sent)
    early_sum, unit_sums = tie(early_sum, unit_sums)
    early_sum = lax.psum_scatter(
        early_sum.reshape(n_rows * 2 * n_blk * shard, wide),
        "rows",
        scatter_dimension=0,
        tiled=True,
    ).reshape(2, n_blk * shard, wide)
    late_sum, late_left = by_bits(column_grads(mixer_normed, signal_grad)[:, 0], n_rows)
    gate_sums = jnp.stack(
        [
            diagonal_blocks(conv_out, decay_pre_grad, heads, block),
            diagonal_blocks(conv_out, input_pre_grad, heads, block),
        ]
    )
    vector_sums = sums.reshape(8, 8, wide).sum(axis=1)
    gain_sums = jnp.stack([mixer_gain_part.sum(axis=0), mlp_gain_part.sum(axis=0)])

    def add_from(value, bit, axis="rows", size=n_rows, wire=f32):
        return value + lax.ppermute(value.astype(wire), axis, flip(size, bit)).astype(f32)

    for bit in bits_of(n_rows):
        late_sum, _ = halve(late_sum, n_rows, bit, late_left)
        gate_sums = add_from(gate_sums, bit, wire=bf16)
        vector_sums = add_from(vector_sums, bit)
        gain_sums = add_from(gain_sums, bit)
        late_sum, gate_sums, vector_sums, gain_sums = tie(
            late_sum, gate_sums, vector_sums, gain_sums
        )
    for bit in bits_of(n_blk):
        gain_sums = add_from(gain_sums, bit, "blk", n_blk)
    vector_sums = vector_sums[:, :width]

    def join_columns(total):
        count = total.shape[0]
        parts = total.reshape(count, n_blk, shard, wide).transpose(1, 2, 0, 3)
        return local_kernel(
            functools.partial(join_columns_kernel, width, wide),
            "join_columns",
            (swap_blk(parts.reshape(n_blk, shard, count * wide)),),
            [((shard, n_blk * width), f32)] * count,
        )

    output_weight_grad, branch_weight_grad, input_weight_grad = join_columns(
        jnp.concatenate([early_sum, late_sum.astype(bf16)], axis=0)
    )
    block_out = (residual_mid + out_parts.astype(f32).sum(axis=0)).astype(bf16)

    (token_grad,) = local_kernel(
        token_grad_kernel,
        "token_grad",
        (mixer_gains, own_tokens, mid_grad, token_parts),
        [(square, f32)],
    )
    gain_sums = lax.dynamic_slice_in_dim(
        gain_sums, (row * n_blk + blk) * mixer_gain.shape[0], mixer_gain.shape[0], axis=1
    )

    return (
        block_out[None],
        token_grad[None],
        gain_sums[0],
        branch_weight_grad,
        input_weight_grad,
        output_weight_grad,
        vector_sums[4:8],
        vector_sums[3],
        gate_sums[0],
        vector_sums[1],
        gate_sums[1],
        vector_sums[2],
        scale_c * jax.nn.sigmoid(-decay_param) * vector_sums[0],
        gain_sums[1],
        unit_sums[:units].astype(f32),
        unit_sums[units : 2 * units].astype(f32),
        unit_sums[2 * units :].astype(f32),
    )


def solution(mesh):
    by_all = P(("rows", "blk"))
    by_all_rows = P(("rows", "blk"), None)
    tokens_spec = P("rows", "blk", None)
    by_blk = P("blk")
    by_blk_heads = P("blk", None, None)
    taps = P(None, "blk")
    recurrence = (taps, by_blk, by_blk_heads, by_blk, by_blk_heads, by_blk, by_blk)
    return jax.shard_map(
        functools.partial(body, (mesh.shape["rows"], mesh.shape["blk"])),
        mesh=mesh,
        in_specs=(tokens_spec, P("rows", None), by_all)
        + (by_all_rows,) * 3
        + recurrence
        + (by_all,)
        + (by_all_rows,) * 3
        + (tokens_spec,),
        out_specs=(tokens_spec, tokens_spec, by_all)
        + (by_all_rows,) * 3
        + recurrence
        + (by_all,)
        + (by_all_rows,) * 3,
        check_vma=False,
    )
```

```python
import functools

import jax
import jax.numpy as jnp
from jax import lax
from jax.experimental import pallas as pl
from jax.experimental.pallas import tpu as pltpu
from jax.sharding import PartitionSpec as P

epsilon = 1e-06
scale_c = 8.0
bf16 = jnp.bfloat16
f32 = jnp.float32
chunk = 64
gain_rows = 16
vmem_limit = 60 * 1024 * 1024


def rms_scale(values):
    return lax.rsqrt(jnp.mean(values * values, axis=-1, keepdims=True) + epsilon)


def gelu_tanh(values):
    return jax.nn.gelu(values, approximate=True)


def gelu_parts(values):
    slope, cubic = 0.7978845608028654, 0.044715
    square = values * values
    bend = jnp.tanh(slope * values * (1.0 + cubic * square))
    lift = 0.5 + 0.5 * bend
    turn = 0.5 * values * (1.0 - bend * bend) * (slope * (1.0 + 3.0 * cubic * square))
    return values * lift, lift + turn


def mm(left, right, dims):
    return lax.dot_general(left, right, (dims, ((), ())), preferred_element_type=f32)


def split_bf16(value):
    high = value.astype(bf16)
    return high, (value - high.astype(f32)).astype(bf16)


def tie(*values):
    return lax.optimization_barrier(values)


def flip(size, bit):
    return [(place, place ^ bit) for place in range(size)]


def bits_of(size):
    found, bit = [], 1
    while bit < size:
        found.append(bit)
        bit *= 2
    return found


def swap_blk(parts):
    return lax.all_to_all(parts, "blk", split_axis=0, concat_axis=0, tiled=True)


def ring_blk(part, size):
    me, rows = lax.axis_index("blk"), part.shape[0]
    whole = jnp.zeros((size * rows,) + part.shape[1:], part.dtype)
    whole = lax.dynamic_update_slice_in_dim(whole, part, me * rows, axis=0)
    for step in range(1, size):
        part = lax.ppermute(part, "blk", [(place, (place + 1) % size) for place in range(size)])
        place = (me - step) % size
        whole = lax.dynamic_update_slice_in_dim(whole, part, place * rows, axis=0)
    return whole


def for_all(part, size):
    return jnp.broadcast_to(part[None], (size,) + part.shape)


def add_from(value, size, bit, wire=f32):
    return value + lax.ppermute(value.astype(wire), "rows", flip(size, bit)).astype(f32)


def sum_rows(value, size):
    for bit in bits_of(size):
        value = add_from(value, size, bit)
    return value


def split_columns_kernel(
    width, wide, input_ref, branch_ref, output_ref, mixer_ref, mlp_ref, both_ref
):
    parts = both_ref.shape[0]
    both_ref[...] = jnp.zeros_like(both_ref)
    for part in range(parts):
        cut = slice(part * width, (part + 1) * width)
        both_ref[part, :, :width] = input_ref[:, cut]
        both_ref[part, :, wide : wide + width] = branch_ref[:, cut]
        both_ref[part, :, 2 * wide : 2 * wide + width] = output_ref[:, cut]
        both_ref[part, :, width : width + 1] = mixer_ref[...]
        both_ref[part, :, width + 1 : width + 2] = mlp_ref[...]


def join_columns_kernel(width, parts_ref, *out_refs):
    for part in range(parts_ref.shape[0]):
        cut = slice(part * width, (part + 1) * width)
        for number, out_ref in enumerate(out_refs):
            out_ref[:, cut] = parts_ref[part, number, :, :width].astype(f32)


def mixer_in_kernel(width, tokens_ref, columns_ref, normed_ref, pre_ref, gains_ref):
    step = 256
    begin = width // 128 * 128
    turned = columns_ref[:, begin : begin + 128].astype(f32).T
    gains_ref[...] = turned[width - begin : width - begin + 2, :]
    gain = gains_ref[0:1, :]

    def rows_step(index, carry):
        here = pl.ds(pl.multiple_of(index * step, step), step)
        values = tokens_ref[here, :].astype(f32)
        normed_ref[here, :] = (values * rms_scale(values) * gain).astype(bf16)
        pre_ref[here, :] = mm(normed_ref[here, :], columns_ref[...], ((1,), (0,)))
        return carry

    lax.fori_loop(0, tokens_ref.shape[0] // step, rows_step, 0)


def sum_parts(parts_ref, here):
    total = parts_ref[0, here, :].astype(f32)
    for part in range(1, parts_ref.shape[0]):
        total = total + parts_ref[part, here, :].astype(f32)
    return total


def mid_norm_kernel(gain_ref, tokens_ref, parts_ref, mid_ref, normed_ref):
    step = 32

    def rows_step(index, carry):
        here = pl.ds(pl.multiple_of(index * step, step), step)
        values = tokens_ref[here, :].astype(f32) + sum_parts(parts_ref, here)
        mid_ref[here, :] = values
        normed = (values * rms_scale(values) * gain_ref[...]).astype(bf16)
        normed_ref[here, :] = normed
        return carry

    lax.fori_loop(0, tokens_ref.shape[0] // step, rows_step, 0)


def fold8(value):
    return value.reshape(value.shape[0] // 8, 8, value.shape[1]).sum(axis=0)


def norm_back(grad, values, gain):
    scale = rms_scale(values)
    product = grad * values
    factor = scale * scale * scale * jnp.mean(product * gain, axis=-1, keepdims=True)
    return scale * (grad * gain) - values * factor, product * scale


def mid_grad_kernel(gain_ref, mid_ref, cotangent_ref, parts_ref, grad_ref, sent_ref, sums_ref):
    step = 32
    sums_ref[...] = jnp.zeros_like(sums_ref)

    def rows_step(index, carry):
        here = pl.ds(pl.multiple_of(index * step, step), step)
        change, terms = norm_back(sum_parts(parts_ref, here), mid_ref[here, :], gain_ref[...])
        sums_ref[...] += fold8(terms)
        result = cotangent_ref[here, :].astype(f32) + change
        grad_ref[here, :] = result
        sent = result.astype(bf16)
        sent_ref[here, :] = sent
        return carry

    lax.fori_loop(0, mid_ref.shape[0] // step, rows_step, 0)


def token_grad_kernel(gain_ref, tokens_ref, mid_grad_ref, parts_ref, grad_ref, gains_ref):
    step = 32
    rows = tokens_ref.shape[0]
    terms = sum_parts(parts_ref, slice(rows, rows + gain_rows))
    gains_ref[0:1, :] = terms[0:1, :] + terms[1:2, :]
    gains_ref[1:2, :] = terms[2:3, :] + terms[3:4, :]

    def rows_step(index, carry):
        here = pl.ds(pl.multiple_of(index * step, step), step)
        values = tokens_ref[here, :].astype(f32)
        change, _ = norm_back(sum_parts(parts_ref, here), values, gain_ref[...])
        grad_ref[here, :] = mid_grad_ref[here, :] + change
        return carry

    lax.fori_loop(0, tokens_ref.shape[0] // step, rows_step, 0)


def vmem_specs(count):
    return [pl.BlockSpec(memory_space=pltpu.VMEM)] * count


def local_kernel(kernel, name, operands, outs, scratch=()):
    return pl.pallas_call(
        kernel,
        out_shape=[jax.ShapeDtypeStruct(shape, kind) for shape, kind in outs],
        in_specs=[pl.BlockSpec(memory_space=pltpu.VMEM)] * len(operands),
        out_specs=[pl.BlockSpec(memory_space=pltpu.VMEM)] * len(outs),
        scratch_shapes=list(scratch),
        compiler_params=pltpu.CompilerParams(vmem_limit_bytes=vmem_limit),
        name=name,
    )(*operands)


def round_up(value):
    return -(-value // 128) * 128


def column_tiles(width, wide, block):
    tiles = []
    for start in range(0, wide, 256):
        stop = min(start + 256, wide)
        low = (start // block) * block
        high = ((min(stop, width) - 1) // block + 1) * block
        tiles.append((start, stop, low // 128 * 128, min(round_up(high), wide)))
    return tiles


def one_minus_exp(value):
    series = 1.0 + value * (1.0 / 8.0)
    for term in (7.0, 6.0, 5.0, 4.0, 3.0, 2.0):
        series = 1.0 + value * (1.0 / term) * series
    return jnp.where(value > -0.3, -value * series, 1.0 - jnp.exp(value))


def shift_down(tile, count, fill):
    moved = pltpu.roll(tile, count, 0)
    row = lax.broadcasted_iota(jnp.int32, tile.shape, 0)
    return jnp.where(row < count, fill, moved)


def shift_up(tile, count, fill):
    moved = pltpu.roll(tile, tile.shape[0] - count, 0)
    row = lax.broadcasted_iota(jnp.int32, tile.shape, 0)
    return jnp.where(row >= tile.shape[0] - count, fill, moved)


def blocked_product(first, second, weights, tiles, store, length, turned=False):
    step = 256

    def rows_step(index, carry):
        rows = pl.ds(pl.multiple_of(index * step, step), step)
        for start, stop, low, high in tiles:
            total = None
            for (high_ref, low_ref), (w_high, w_low) in zip((first, second), weights):
                if high_ref is None:
                    continue
                a_high = high_ref[rows, low:high]
                a_low = low_ref[rows, low:high]
                cut = (slice(start, stop), slice(low, high))
                cut = cut if turned else cut[::-1]
                b_high, b_low = w_high[cut], w_low[cut]
                dims = ((1,), (1,)) if turned else ((1,), (0,))
                part = mm(a_high, b_high, dims) + mm(a_high, b_low, dims) + mm(a_low, b_high, dims)
                total = part if total is None else total + part
            store(rows, slice(start, stop), total)
        return carry

    lax.fori_loop(0, length // step, rows_step, 0)


def recur_forward_kernel(
    tiles,
    signal_ref,
    masks_ref,
    vectors_ref,
    decay_high,
    decay_low,
    input_high,
    input_low,
    states_ref,
    values_ref,
    conv_ref,
    decay_rate_ref,
    input_rate_ref,
    padded,
    conv_high,
    conv_low,
):
    length, width = signal_ref.shape
    count = length // chunk
    padded[0:8, :] = jnp.zeros((8, width), f32)

    def pad_step(index, carry):
        begin = pl.multiple_of(index * chunk, chunk)
        here = pl.ds(begin, chunk)
        padded[pl.ds(begin + 8, chunk), :] = signal_ref[here, :].astype(f32)
        return carry

    lax.fori_loop(0, count, pad_step, 0)

    def conv_step(index, carry):
        begin = pl.multiple_of(index * chunk, chunk)
        rows = pl.ds(begin, chunk)
        window = padded[pl.ds(begin, chunk + 8), :]
        total = vectors_ref[4:5, :] + vectors_ref[0:1, :] * window[8:, :]
        for tap in range(1, 4):
            total = total + vectors_ref[tap : tap + 1, :] * (
                window[8 - tap : 8 - tap + chunk, :] * masks_ref[rows, tap : tap + 1]
            )
        conv_ref[rows, :] = total
        high, low = split_bf16(total)
        conv_high[rows, :] = high
        conv_low[rows, :] = low
        return carry

    lax.fori_loop(0, count, conv_step, 0)

    def store_decay(rows, columns, value):
        decay_rate_ref[rows, columns] = jax.nn.sigmoid(value + vectors_ref[5:6, columns])

    def store_input(rows, columns, value):
        input_rate_ref[rows, columns] = jax.nn.sigmoid(value + vectors_ref[6:7, columns])

    nothing = (None, None)
    blocked_product(
        (conv_high, conv_low), nothing, ((decay_high, decay_low), nothing), tiles, store_decay, length
    )
    blocked_product(
        (conv_high, conv_low), nothing, ((input_high, input_low), nothing), tiles, store_input, length
    )

    def scan_step(index, state):
        begin = pl.multiple_of(index * 8, 8)
        rows = pl.ds(begin, 8)
        restart = masks_ref[rows, 4:5]
        keep = 1.0 - restart
        log_decay = -vectors_ref[7:8, :] * decay_rate_ref[rows, :]
        mult = restart + keep * jnp.sqrt(one_minus_exp(2.0 * log_decay))
        carried = keep * jnp.exp(log_decay)
        total = mult * input_rate_ref[rows, :] * conv_ref[rows, :]
        for count_rows in (1, 2, 4):
            total = total + carried * shift_down(total, count_rows, 0.0)
            carried = carried * shift_down(carried, count_rows, 1.0)
        total = total + carried * state
        states_ref[rows, :] = total
        return total[7:8, :]

    lax.fori_loop(0, length // 8, scan_step, jnp.zeros((1, width), f32), unroll=4)

    def values_step(index, carry):
        begin = pl.multiple_of(index * chunk, chunk)
        here = pl.ds(begin, chunk)
        values_ref[here, :] = states_ref[pl.ds(begin, chunk), :].astype(bf16)
        return carry

    lax.fori_loop(0, count, values_step, 0)


def mixer_backward_kernel(
    tiles,
    state_grad_ref,
    branch_grad_ref,
    masks_ref,
    vectors_ref,
    mlp_ref,
    signal_any,
    states_any,
    conv_any,
    decay_rate_any,
    input_rate_any,
    decay_high_any,
    decay_low_any,
    input_high_any,
    input_low_any,
    both_any,
    tokens_any,
    both_grad_ref,
    decay_pre_ref,
    input_pre_ref,
    sums_ref,
    token_ref,
    signal_ref,
    states_ref,
    conv_ref,
    decay_rate_ref,
    input_rate_ref,
    decay_high,
    decay_low,
    input_high,
    input_low,
    both_ref,
    tokens_ref,
    padded,
    grads,
    earlier,
    decay_pre_high,
    decay_pre_low,
    input_pre_high,
    input_pre_low,
    gain_sums,
    arrived,
):
    fetched = [
        (signal_any, signal_ref),
        (states_any, states_ref),
        (conv_any, conv_ref),
        (decay_rate_any, decay_rate_ref),
        (input_rate_any, input_rate_ref),
        (decay_high_any, decay_high),
        (decay_low_any, decay_low),
        (input_high_any, input_high),
        (input_low_any, input_low),
        (both_any, both_ref),
    ]
    copies = [
        pltpu.make_async_copy(source, target, arrived.at[number])
        for number, (source, target) in enumerate(fetched)
    ]
    for copy in copies:
        copy.start()
    length, width = grads.shape[0] - 8, grads.shape[1]
    count = length // chunk
    padded[0:8, :] = jnp.zeros((8, width), f32)
    earlier[0:8, :] = jnp.zeros((8, width), f32)
    grads[length:, :] = jnp.zeros((8, width), f32)
    sums_ref[...] = jnp.zeros_like(sums_ref)

    for copy in copies[:5]:
        copy.wait()

    def pad_step(index, carry):
        begin = pl.multiple_of(index * chunk, chunk)
        here = pl.ds(begin, chunk)
        padded[pl.ds(begin + 8, chunk), :] = signal_ref[here, :].astype(f32)
        earlier[pl.ds(begin + 8, chunk), :] = states_ref[here, :]
        grads[here, :] = state_grad_ref[here, :].astype(f32)
        both_grad_ref[here, width:] = branch_grad_ref[here, :]
        return carry

    lax.fori_loop(0, count, pad_step, 0)

    def scan_step(index, later):
        begin = pl.multiple_of(length - 8 - index * 8, 8)
        rows = pl.ds(begin, 8)
        restart = masks_ref[rows, 4:5]
        keep = 1.0 - restart
        decay_rate = decay_rate_ref[rows, :]
        input_rate = input_rate_ref[rows, :]
        conv_out = conv_ref[rows, :]
        log_decay = -vectors_ref[7:8, :] * decay_rate
        decay = jnp.exp(log_decay)
        root = jnp.sqrt(one_minus_exp(2.0 * log_decay))
        mult = restart + keep * root
        carried = keep * decay
        flow = grads[rows, :]
        reach = shift_up(carried, 1, 1.0)
        for count_rows in (1, 2, 4):
            flow = flow + reach * shift_up(flow, count_rows, 0.0)
            reach = reach * shift_up(reach, count_rows, 1.0)
        flow = flow + reach * later
        window = earlier[pl.ds(begin, 16), :]
        before = window[7:15, :]
        flow_rate = flow * input_rate
        mult_grad = flow_rate * conv_out
        log_grad = keep * (flow * before * decay - mult_grad * decay * decay / root)
        rate_log = decay_rate * log_grad
        decay_pre = -vectors_ref[7:8, :] * rate_log * (1.0 - decay_rate)
        input_pre = mult_grad * mult * (1.0 - input_rate)
        grads[rows, :] = flow_rate * mult
        decay_pre_ref[rows, :] = decay_pre
        input_pre_ref[rows, :] = input_pre
        sums_ref[0:8, :] += rate_log
        sums_ref[8:16, :] += decay_pre
        sums_ref[16:24, :] += input_pre
        return carried[0:1, :] * flow[0:1, :]

    lax.fori_loop(0, length // 8, scan_step, jnp.zeros((1, width), f32), unroll=4)

    for copy in copies[5:9]:
        copy.wait()

    def split_step(index, carry):
        rows = pl.ds(pl.multiple_of(index * chunk, chunk), chunk)
        decay_pre_high[rows, :], decay_pre_low[rows, :] = split_bf16(decay_pre_ref[rows, :])
        input_pre_high[rows, :], input_pre_low[rows, :] = split_bf16(input_pre_ref[rows, :])
        return carry

    lax.fori_loop(0, count, split_step, 0)

    def store(rows, columns, value):
        grads[rows, columns] += value

    blocked_product(
        (decay_pre_high, decay_pre_low),
        (input_pre_high, input_pre_low),
        ((decay_high, decay_low), (input_high, input_low)),
        tiles,
        store,
        length,
        True,
    )

    def conv_step(index, carry):
        begin = pl.multiple_of(index * chunk, chunk)
        rows = pl.ds(begin, chunk)
        grad_window = grads[pl.ds(begin, chunk + 8), :]
        mask_window = masks_ref[pl.ds(begin, chunk + 8), :]
        signal_window = padded[pl.ds(begin, chunk + 8), :]
        here = grad_window[:chunk, :]
        result = vectors_ref[0:1, :] * here
        sums_ref[24:32, :] += fold8(here)
        sums_ref[32:40, :] += fold8(here * signal_window[8:, :])
        for tap in range(1, 4):
            masked = grad_window * mask_window[:, tap : tap + 1]
            result = result + vectors_ref[tap : tap + 1, :] * masked[tap : tap + chunk, :]
            sums_ref[32 + 8 * tap : 40 + 8 * tap, :] += fold8(
                masked[:chunk, :] * signal_window[8 - tap : 8 - tap + chunk, :]
            )
        here = pl.ds(begin, chunk)
        both_grad_ref[here, :width] = result.astype(bf16)
        return carry

    lax.fori_loop(0, count, conv_step, 0)
    copies[9].wait()
    parts, rows, model_width = token_ref.shape
    rows = rows - gain_rows
    gain_sums[...] = jnp.zeros_like(gain_sums)

    def token_step(index, carry):
        here = pl.ds(pl.multiple_of(index * rows, rows), rows)
        copy = pltpu.make_async_copy(tokens_any.at[here, :], tokens_ref, arrived.at[len(fetched)])
        copy.start()
        grad = mm(both_grad_ref[here, :], both_ref[...], ((1,), (1,)))
        copy.wait()
        values = tokens_ref[...].astype(f32)
        gain_sums[...] += fold8(values * rms_scale(values) * grad)
        token_ref[index, :rows, :] = grad.astype(bf16)
        return carry

    lax.fori_loop(0, parts, token_step, 0)
    terms = []
    for total in (gain_sums[...], mlp_ref[...]):
        terms += split_bf16(total.sum(axis=0, keepdims=True))
    terms.append(jnp.zeros((gain_rows - len(terms), model_width), bf16))
    terms = jnp.concatenate([term.astype(f32) for term in terms], axis=0).astype(bf16)
    for part in range(parts):
        token_ref[part, rows:, :] = terms


def recur_forward(signal, masks, vectors, weights, tiles):
    length, width = signal.shape
    whole = ((length, width), f32)
    return local_kernel(
        functools.partial(recur_forward_kernel, tiles),
        "recur_forward",
        (signal, masks, vectors, *weights),
        [whole, ((length, width), bf16), whole, whole, whole],
        [
            pltpu.VMEM((length + 8, width), f32),
            pltpu.VMEM((length, width), bf16),
            pltpu.VMEM((length, width), bf16),
        ],
    )


def mixer_backward(resident, fetched, parts, tiles):
    length, wide = resident[0].shape
    model_width = fetched[-1].shape[1]
    whole = ((length, wide), f32)
    outs = [
        ((length, 2 * wide), bf16),
        whole,
        whole,
        ((64, wide), f32),
        ((parts, length // parts + gain_rows, model_width), bf16),
    ]
    padded = pltpu.VMEM((length + 8, wide), f32)
    return pl.pallas_call(
        functools.partial(mixer_backward_kernel, tiles),
        out_shape=[jax.ShapeDtypeStruct(shape, kind) for shape, kind in outs],
        in_specs=vmem_specs(len(resident)) + [pl.BlockSpec(memory_space=pl.ANY)] * len(fetched),
        out_specs=vmem_specs(len(outs)),
        scratch_shapes=[pltpu.VMEM(value.shape, value.dtype) for value in fetched[:-1]]
        + [pltpu.VMEM((length // parts, model_width), bf16)]
        + [padded] * 3
        + [pltpu.VMEM((length, wide), bf16)] * 4
        + [pltpu.VMEM((8, model_width), f32), pltpu.SemaphoreType.DMA((len(fetched),))],
        compiler_params=pltpu.CompilerParams(vmem_limit_bytes=vmem_limit),
        name="mixer_backward",
    )(*resident, *fetched)


def column_grads_kernel(count, *refs):
    for number in range(count):
        value = mm(refs[number][...], refs[count + number][...], ((0,), (0,)))
        value = value.astype(bf16)
        refs[-1][0, :, number] = value.reshape(refs[-1].shape[1], *refs[-1].shape[3:])


def column_grads(lefts, rights, size, parts):
    length, model_width = lefts[0].shape
    wide = rights[0].shape[1]
    each, count = model_width // size, len(lefts)
    block = (1, parts, count, each // parts, wide)
    total = pl.pallas_call(
        functools.partial(column_grads_kernel, count),
        grid=(size,),
        in_specs=[pl.BlockSpec((length, each), lambda i: (0, i))] * count
        + [pl.BlockSpec((length, wide), lambda i: (0, 0))] * count,
        out_specs=pl.BlockSpec(block, lambda i: (i, 0, 0, 0, 0)),
        out_shape=jax.ShapeDtypeStruct((size,) + block[1:], bf16),
        compiler_params=pltpu.CompilerParams(vmem_limit_bytes=vmem_limit),
        name="column_grads",
    )(*lefts, *rights)
    total = total.reshape(size * count * each, wide)
    total = lax.psum_scatter(total, "rows", scatter_dimension=0, tiled=True)
    return total.reshape(parts, count, each // parts, wide)


def gate_grads_kernel(tiles, conv_ref, decay_pre_ref, input_pre_ref, gates_ref, dense, pairs):
    heads, block = gates_ref.shape[1:3]
    pairs[0], pairs[1] = split_bf16(conv_ref[...])
    for gate, ref in enumerate((decay_pre_ref, input_pre_ref)):
        pairs[2], pairs[3] = split_bf16(ref[...])
        for start, stop, low, high in tiles:
            total = None
            for left, right in ((0, 2), (0, 3), (1, 2)):
                part = mm(pairs[left, :, low:high], pairs[right, :, start:stop], ((0,), (0,)))
                total = part if total is None else total + part
            dense[low:high, start:stop] = total
        for head in range(heads):
            cut = slice(head * block, (head + 1) * block)
            gates_ref[gate, head] = dense[cut, cut]


def dense_kernel(decay_ref, input_ref, decay_high, decay_low, input_high, input_low):
    heads, block, _ = decay_ref.shape
    for ref, high, low in (
        (decay_ref, decay_high, decay_low),
        (input_ref, input_high, input_low),
    ):
        high[...] = jnp.zeros_like(high)
        low[...] = jnp.zeros_like(low)
        for head in range(heads):
            cut = slice(head * block, (head + 1) * block)
            high[cut, cut], low[cut, cut] = split_bf16(ref[head])


def mlp_kernel(
    normed_ref,
    cotangent_ref,
    hidden_grad_ref,
    gate_ref,
    up_ref,
    down_ref,
    normed_grad_ref,
    out_ref,
    units_any,
    normed_total,
    out_total,
    gate_grads,
    up_grads,
    hidden_all,
    units,
    sent,
):
    step, steps = pl.program_id(0), pl.num_programs(0)
    length = normed_ref.shape[0]
    group = units.shape[1]
    gate_units = lambda: gate_ref[...].reshape(down_ref.shape)
    up_units = lambda: up_ref[...].reshape(down_ref.shape)

    @pl.when(step == 0)
    def _():
        normed_total[...] = jnp.zeros_like(normed_total)
        out_total[...] = jnp.zeros_like(out_total)

    def rows_step(index, carry):
        here = pl.ds(pl.multiple_of(index * 256, 256), 256)
        normed = normed_ref[here, :]
        gate_act, slope = gelu_parts(mm(normed, gate_units(), ((1,), (1,))))
        up_vals = mm(normed, up_units(), ((1,), (1,)))
        hidden_grad = hidden_grad_ref[here, :]
        gate_grads[here, :] = (hidden_grad * up_vals * slope).astype(bf16)
        up_grads[here, :] = (hidden_grad * gate_act).astype(bf16)
        hidden_all[here, :] = (gate_act * up_vals).astype(bf16)
        normed_total[here, :] += mm(gate_grads[here, :], gate_units(), ((1,), (0,))) + mm(
            up_grads[here, :], up_units(), ((1,), (0,))
        )
        out_total[here, :] += mm(hidden_all[here, :], down_ref[...], ((1,), (0,)))
        return carry

    lax.fori_loop(0, length // 256, rows_step, 0)

    def copy_of(number):
        return pltpu.make_async_copy(
            units.at[number], units_any.at[pl.ds(step * group, group), number], sent.at[number]
        )

    products = ((gate_grads, normed_ref), (up_grads, normed_ref), (hidden_all, cotangent_ref))
    for number, (left, right) in enumerate(products):

        @pl.when(step > 0)
        def _():
            copy_of(number).wait()

        value = mm(left[...], right[...], ((0,), (0,))).astype(bf16)
        units[number] = value.reshape(units.shape[1:])
        copy_of(number).start()

    @pl.when(step == steps - 1)
    def _():
        normed_grad_ref[...] = normed_total[...].astype(bf16)
        out_ref[...] = out_total[...].astype(bf16)
        for number in range(len(products)):
            copy_of(number).wait()


def mlp(normed, cotangent, hidden_grad, first_units, down_units):
    length, model_width = normed.shape
    parts, _, units, _ = first_units.shape
    total = parts * units
    group = 1
    while group * units % 128 or (group < parts and 2 * group * units * length <= 768 * 512):
        group *= 2
    tile = group * units
    first = lambda which: pl.BlockSpec(
        (group, 1, units, model_width), lambda i: (i, which, 0, 0)
    )
    weights = [first(0), first(1), pl.BlockSpec((tile, model_width), lambda i: (i, 0))]
    whole = jax.ShapeDtypeStruct((length, model_width), bf16)
    return pl.pallas_call(
        mlp_kernel,
        grid=(total // tile,),
        out_shape=[
            whole,
            whole,
            jax.ShapeDtypeStruct((parts, 3, units, model_width), bf16),
        ],
        in_specs=vmem_specs(2) + [pl.BlockSpec((length, tile), lambda i: (0, i))] + weights,
        out_specs=vmem_specs(2) + [pl.BlockSpec(memory_space=pl.ANY)],
        scratch_shapes=[pltpu.VMEM((length, model_width), f32)] * 2
        + [pltpu.VMEM((length, tile), bf16)] * 3
        + [pltpu.VMEM((3, group, units, model_width), bf16), pltpu.SemaphoreType.DMA((3,))],
        compiler_params=pltpu.CompilerParams(vmem_limit_bytes=vmem_limit),
        name="mlp",
    )(normed, cotangent, hidden_grad, first_units, first_units, down_units)


def body(
    sizes,
    tokens,
    segment_ids,
    mixer_gain,
    branch_weight,
    input_weight,
    output_weight,
    conv_weight,
    conv_bias,
    decay_gate,
    decay_bias,
    input_gate,
    input_bias,
    decay_param,
    mlp_gain,
    hidden_gate,
    hidden_up,
    hidden_down,
    cotangent,
):
    n_rows, n_blk = sizes
    own_tokens, own_grad = tokens[0], cotangent[0]
    segments = segment_ids[0]
    tok_count, model_width = own_tokens.shape
    width = conv_weight.shape[1]
    wide = round_up(width + 2)
    heads, block, _ = decay_gate.shape
    tiles = column_tiles(width, wide, block)
    row, blk = lax.axis_index("rows"), lax.axis_index("blk")
    square = (tok_count, model_width)
    shard = branch_weight.shape[0]
    units = hidden_gate.shape[0]

    (column_parts,) = local_kernel(
        functools.partial(split_columns_kernel, width, wide),
        "split_columns",
        (input_weight, branch_weight, output_weight, mixer_gain[:, None], mlp_gain[:, None]),
        [((n_blk, shard, 3 * wide), bf16)],
    )
    columns = swap_blk(column_parts).reshape(n_blk * shard, 3 * wide)
    columns, token_own = tie(columns, own_tokens)
    both_columns = lax.all_gather(columns[:, : 2 * wide], "rows", axis=0, tiled=True)
    output_columns = lax.all_gather(columns[:, 2 * wide :], "rows", axis=0, tiled=True)
    tokens_all = ring_blk(token_own, n_blk)
    tokens_all, grad_own, hidden_gate, hidden_up, hidden_down = tie(
        tokens_all, for_all(own_grad, n_blk), hidden_gate, hidden_up, hidden_down
    )
    out_grad = swap_blk(grad_own).reshape(n_blk * tok_count, model_width)
    down_units = lax.all_gather(hidden_down, "rows", axis=0, tiled=True)
    first_units = lax.all_gather(
        jnp.concatenate([hidden_gate, hidden_up], axis=0), "rows", axis=0, tiled=True
    ).reshape(n_rows, 2, units, model_width)

    masks = [jnp.ones_like(segments, dtype=f32)]
    for tap in range(1, 4):
        masks.append(
            jnp.concatenate(
                [jnp.zeros((tap,), f32), (segments[tap:] == segments[:-tap]).astype(f32)]
            )
        )
    masks.append(1.0 - masks[1])
    masks = jnp.pad(jnp.stack(masks, axis=1), ((0, 8), (0, 3)))
    vectors = jnp.concatenate(
        [
            conv_weight,
            conv_bias[None],
            decay_bias[None],
            input_bias[None],
            scale_c * jax.nn.softplus(-decay_param)[None],
        ],
        axis=0,
    )
    vectors = jnp.pad(vectors, ((0, 0), (0, wide - width)), constant_values=1.0)
    weights = local_kernel(
        dense_kernel, "dense_gates", (decay_gate, input_gate), [((wide, wide), bf16)] * 4
    )
    mixer_normed, both_pre, gains = local_kernel(
        functools.partial(mixer_in_kernel, width),
        "mixer_in",
        (tokens_all, both_columns),
        [
            (tokens_all.shape, bf16),
            ((n_blk * tok_count, 2 * wide), f32),
            ((2, model_width), f32),
        ],
    )
    mixer_gains, mlp_gains = gains[0:1], gains[1:2]
    signal, branch_pre = both_pre[:, :wide].astype(bf16), both_pre[:, wide:]
    states, state_values, conv_out, decay_rate, input_rate = recur_forward(
        signal, masks, vectors, weights, tiles
    )
    mixed = (gelu_tanh(branch_pre) * state_values.astype(f32)).astype(bf16)
    mixed, out_grad = tie(mixed, out_grad)

    def scatter_blk(partial):
        return swap_blk(partial.astype(bf16).reshape(n_blk, tok_count, model_width))

    mid_parts = scatter_blk(mm(mixed, output_columns, ((1,), (1,))))
    residual_mid, own_normed = local_kernel(
        mid_norm_kernel,
        "mid_norm",
        (mlp_gains, own_tokens, mid_parts),
        [(square, f32), (square, bf16)],
    )

    mlp_normed = ring_blk(own_normed, n_blk)
    hidden_grad = mm(out_grad, down_units, ((1,), (1,)))
    normed_partial, out_partial, unit_sums = mlp(
        mlp_normed, out_grad, hidden_grad, first_units, down_units
    )
    normed_parts = scatter_blk(normed_partial)
    unit_sums = lax.psum_scatter(
        unit_sums.reshape(n_rows * 3 * units, model_width),
        "rows",
        scatter_dimension=0,
        tiled=True,
    )

    mid_grad, own_sent, mlp_gain_part = local_kernel(
        mid_grad_kernel,
        "mid_grad",
        (mlp_gains, residual_mid, own_grad, normed_parts),
        [(square, f32), (square, bf16), ((8, model_width), f32)],
    )
    mid_sent = ring_blk(own_sent, n_blk)

    mid_sent, out_partial = tie(mid_sent, out_partial)
    out_parts = scatter_blk(out_partial)
    mixed_grad = mm(mid_sent, output_columns, ((1,), (0,)))
    branch_act, branch_slope = gelu_parts(branch_pre)
    state_grad = (mixed_grad * branch_act).astype(bf16)
    branch_grad = (mixed_grad * state_values.astype(f32) * branch_slope).astype(bf16)
    early_sum = column_grads((mid_sent, mixer_normed), (mixed, branch_grad), n_rows, n_blk)
    both_grad, decay_pre_grad, input_pre_grad, sums, token_sent = mixer_backward(
        (state_grad, branch_grad, masks, vectors, mlp_gain_part),
        (
            signal,
            states,
            conv_out,
            decay_rate,
            input_rate,
            *weights,
            both_columns,
            tokens_all,
        ),
        n_blk,
        tiles,
    )
    token_sent, out_parts, unit_sums, both_grad, decay_pre_grad, input_pre_grad, sums = tie(
        token_sent, out_parts, unit_sums, both_grad, decay_pre_grad, input_pre_grad, sums
    )
    token_parts = swap_blk(token_sent)
    late_sum = column_grads((mixer_normed,), (both_grad[:, :wide],), n_rows, n_blk)
    (gate_sums,) = local_kernel(
        functools.partial(gate_grads_kernel, tiles),
        "gate_grads",
        (conv_out, decay_pre_grad, input_pre_grad),
        [((2, heads, block, block), f32)],
        [pltpu.VMEM((wide, wide), f32), pltpu.VMEM((4,) + signal.shape, bf16)],
    )
    gate_sums, token_parts = tie(gate_sums, token_parts)
    gate_sums = [gate_sums[0], gate_sums[1]]
    one_way = bits_of(n_rows)
    other_way = one_way[:1] + one_way[:0:-1]
    vector_sums = sums.reshape(8, 8, wide).sum(axis=1)
    for at, bit in enumerate(bits_of(n_rows)):
        for number, order in enumerate((one_way, other_way)):
            gate_sums[number] = add_from(gate_sums[number], n_rows, order[at], bf16)
        vector_sums = add_from(vector_sums, n_rows, bit)
        vector_sums, *gate_sums = tie(vector_sums, *gate_sums)
    token_parts, early_sum = tie(token_parts, early_sum)
    vector_sums = vector_sums[:, :width]
    token_grad, gain_sums = local_kernel(
        token_grad_kernel,
        "token_grad",
        (mixer_gains, own_tokens, mid_grad, token_parts),
        [(square, f32), ((2, model_width), f32)],
    )
    gain_sums = sum_rows(gain_sums, n_rows)

    column_sums = swap_blk(jnp.concatenate([early_sum, late_sum], axis=1))
    output_weight_grad, branch_weight_grad, input_weight_grad = local_kernel(
        functools.partial(join_columns_kernel, width),
        "join_columns",
        (column_sums,),
        [((shard, n_blk * width), f32)] * 3,
    )
    block_out = (residual_mid + out_parts.astype(f32).sum(axis=0)).astype(bf16)

    gain_sums = lax.dynamic_slice_in_dim(
        gain_sums, (row * n_blk + blk) * mixer_gain.shape[0], mixer_gain.shape[0], axis=1
    )

    return (
        block_out[None],
        token_grad[None],
        gain_sums[0],
        branch_weight_grad,
        input_weight_grad,
        output_weight_grad,
        vector_sums[4:8],
        vector_sums[3],
        gate_sums[0],
        vector_sums[1],
        gate_sums[1],
        vector_sums[2],
        scale_c * jax.nn.sigmoid(-decay_param) * vector_sums[0],
        gain_sums[1],
        unit_sums[:units].astype(f32),
        unit_sums[units : 2 * units].astype(f32),
        unit_sums[2 * units :].astype(f32),
    )


def solution(mesh):
    by_all = P(("rows", "blk"))
    by_all_rows = P(("rows", "blk"), None)
    tokens_spec = P("rows", "blk", None)
    by_blk = P("blk")
    by_blk_heads = P("blk", None, None)
    taps = P(None, "blk")
    recurrence = (taps, by_blk, by_blk_heads, by_blk, by_blk_heads, by_blk, by_blk)
    return jax.shard_map(
        functools.partial(body, (mesh.shape["rows"], mesh.shape["blk"])),
        mesh=mesh,
        in_specs=(tokens_spec, P("rows", None), by_all)
        + (by_all_rows,) * 3
        + recurrence
        + (by_all,)
        + (by_all_rows,) * 3
        + (tokens_spec,),
        out_specs=(tokens_spec, tokens_spec, by_all)
        + (by_all_rows,) * 3
        + recurrence
        + (by_all,)
        + (by_all_rows,) * 3,
        check_vma=False,
    )
```

```python
import functools

import jax
import jax.numpy as jnp
from jax import lax
from jax.experimental import pallas as pl
from jax.experimental.pallas import tpu as pltpu
from jax.sharding import PartitionSpec as P

epsilon = 1e-06
scale_c = 8.0
bf16 = jnp.bfloat16
f32 = jnp.float32
chunk = 64
gain_rows = 16
vmem_limit = 60 * 1024 * 1024


def rms_scale(values):
    return lax.rsqrt(jnp.mean(values * values, axis=-1, keepdims=True) + epsilon)


def gelu_tanh(values):
    return jax.nn.gelu(values, approximate=True)


def gelu_parts(values):
    slope, cubic = 0.7978845608028654, 0.044715
    square = values * values
    bend = jnp.tanh(slope * values * (1.0 + cubic * square))
    lift = 0.5 + 0.5 * bend
    turn = 0.5 * values * (1.0 - bend * bend) * (slope * (1.0 + 3.0 * cubic * square))
    return values * lift, lift + turn


def mm(left, right, dims):
    return lax.dot_general(left, right, (dims, ((), ())), preferred_element_type=f32)


def split_bf16(value):
    high = value.astype(bf16)
    return high, (value - high.astype(f32)).astype(bf16)


def tie(*values):
    return lax.optimization_barrier(values)


def flip(size, bit):
    return [(place, place ^ bit) for place in range(size)]


def bits_of(size):
    found, bit = [], 1
    while bit < size:
        found.append(bit)
        bit *= 2
    return found


def swap_blk(parts):
    return lax.all_to_all(parts, "blk", split_axis=0, concat_axis=0, tiled=True)


def ring_blk(part, size, beside=None):
    me, rows = lax.axis_index("blk"), part.shape[0]
    whole = jnp.zeros((size * rows,) + part.shape[1:], part.dtype)
    whole = lax.dynamic_update_slice_in_dim(whole, part, me * rows, axis=0)
    for step in range(1, size):
        part = lax.ppermute(part, "blk", [(place, (place + 1) % size) for place in range(size)])
        if step == 1 and beside is not None:
            part, beside = tie(part, beside)
        place = (me - step) % size
        whole = lax.dynamic_update_slice_in_dim(whole, part, place * rows, axis=0)
    return whole if beside is None else (whole, beside)


def ring_sum(partial, size):
    me, rows = lax.axis_index("blk"), partial.shape[0] // size
    pick = lambda place: lax.dynamic_slice_in_dim(partial, place % size * rows, rows, axis=0)
    total = pick(me - 1 + size)
    for step in range(1, size):
        total = lax.ppermute(total, "blk", [(place, (place + 1) % size) for place in range(size)])
        if step < size - 1:
            total = (total.astype(f32) + pick(me - 1 - step + size).astype(f32)).astype(bf16)
    return total, pick(me)


def for_all(part, size):
    return jnp.broadcast_to(part[None], (size,) + part.shape)


def halve(total, size, bit, left):
    axis = left.index(bit)
    left.remove(bit)
    mine = (lax.axis_index("rows") // bit) % 2
    away = lax.dynamic_index_in_dim(total, 1 - mine, axis, keepdims=False)
    keep = lax.dynamic_index_in_dim(total, mine, axis, keepdims=False)
    got = lax.ppermute(away, "rows", flip(size, bit))
    return (keep.astype(f32) + got.astype(f32)).astype(bf16)


def sum_columns(total, size):
    left = list(reversed(bits_of(size)))
    total = total.reshape((2,) * len(left) + total.shape[1:])
    total = halve(total, size, 1, left)
    half, order = total.shape[-1] // 2, bits_of(size)[1:]
    found = []
    for cut, bits in ((total[..., :half], order), (total[..., half:], order[::-1])):
        rest = list(left)
        found.append([cut, bits, rest])
    for at in range(len(order)):
        for piece in found:
            piece[0] = halve(piece[0], size, piece[1][at], piece[2])
        found[0][0], found[1][0] = tie(found[0][0], found[1][0])
    return jnp.concatenate([found[0][0], found[1][0]], axis=-1)


def add_from(value, size, bit, wire=f32):
    return value + lax.ppermute(value.astype(wire), "rows", flip(size, bit)).astype(f32)


def sum_rows(value, size):
    for bit in bits_of(size):
        value = add_from(value, size, bit)
    return value


def split_columns_kernel(
    width, wide, input_ref, branch_ref, output_ref, mixer_ref, mlp_ref, both_ref
):
    parts = both_ref.shape[0]
    both_ref[...] = jnp.zeros_like(both_ref)
    for part in range(parts):
        cut = slice(part * width, (part + 1) * width)
        both_ref[part, :, :width] = input_ref[:, cut]
        both_ref[part, :, wide : wide + width] = branch_ref[:, cut]
        both_ref[part, :, 2 * wide : 2 * wide + width] = output_ref[:, cut]
        both_ref[part, :, width : width + 1] = mixer_ref[...]
        both_ref[part, :, width + 1 : width + 2] = mlp_ref[...]


def join_columns_kernel(width, parts_ref, *out_refs):
    for part in range(parts_ref.shape[0]):
        cut = slice(part * width, (part + 1) * width)
        for number, out_ref in enumerate(out_refs):
            out_ref[:, cut] = parts_ref[part, number, :, :width].astype(f32)


def mixer_in_kernel(width, tokens_ref, columns_ref, normed_ref, signal_ref, branch_ref, gains_ref):
    step = 256
    begin = width // 128 * 128
    turned = columns_ref[:, begin : begin + 128].astype(f32).T
    gains_ref[...] = turned[width - begin : width - begin + 2, :]
    gain = gains_ref[0:1, :]

    def rows_step(index, carry):
        here = pl.ds(pl.multiple_of(index * step, step), step)
        values = tokens_ref[here, :].astype(f32)
        normed_ref[here, :] = (values * rms_scale(values) * gain).astype(bf16)
        value = mm(normed_ref[here, :], columns_ref[...], ((1,), (0,)))
        wide = signal_ref.shape[1]
        signal_ref[here, :] = value[:, :wide].astype(bf16)
        branch_ref[here, :] = value[:, wide:]
        return carry

    lax.fori_loop(0, tokens_ref.shape[0] // step, rows_step, 0)


def sum_parts(parts_ref, here):
    total = parts_ref[0, here, :].astype(f32)
    for part in range(1, parts_ref.shape[0]):
        total = total + parts_ref[part, here, :].astype(f32)
    return total


def mid_norm_kernel(gain_ref, tokens_ref, one_ref, two_ref, mid_ref, normed_ref):
    step = 32

    def rows_step(index, carry):
        here = pl.ds(pl.multiple_of(index * step, step), step)
        values = tokens_ref[here, :].astype(f32) + one_ref[here, :].astype(f32)
        values = values + two_ref[here, :].astype(f32)
        mid_ref[here, :] = values
        normed = (values * rms_scale(values) * gain_ref[...]).astype(bf16)
        normed_ref[here, :] = normed
        return carry

    lax.fori_loop(0, tokens_ref.shape[0] // step, rows_step, 0)


def fold8(value):
    return value.reshape(value.shape[0] // 8, 8, value.shape[1]).sum(axis=0)


def norm_back(grad, values, gain):
    scale = rms_scale(values)
    product = grad * values
    factor = scale * scale * scale * jnp.mean(product * gain, axis=-1, keepdims=True)
    return scale * (grad * gain) - values * factor, product * scale


def mid_grad_kernel(
    gain_ref, mid_ref, cotangent_ref, one_ref, two_ref, grad_ref, sent_ref, sums_ref
):
    step = 32
    sums_ref[...] = jnp.zeros_like(sums_ref)

    def rows_step(index, carry):
        here = pl.ds(pl.multiple_of(index * step, step), step)
        grad = one_ref[here, :].astype(f32) + two_ref[here, :].astype(f32)
        change, terms = norm_back(grad, mid_ref[here, :], gain_ref[...])
        sums_ref[...] += fold8(terms)
        result = cotangent_ref[here, :].astype(f32) + change
        grad_ref[here, :] = result
        sent = result.astype(bf16)
        sent_ref[here, :] = sent
        return carry

    lax.fori_loop(0, mid_ref.shape[0] // step, rows_step, 0)


def token_grad_kernel(gain_ref, tokens_ref, mid_grad_ref, parts_ref, grad_ref, gains_ref):
    step = 32
    rows = tokens_ref.shape[0]
    terms = sum_parts(parts_ref, slice(rows, rows + gain_rows))
    gains_ref[0:1, :] = terms[0:1, :] + terms[1:2, :]
    gains_ref[1:2, :] = terms[2:3, :] + terms[3:4, :]

    def rows_step(index, carry):
        here = pl.ds(pl.multiple_of(index * step, step), step)
        values = tokens_ref[here, :].astype(f32)
        change, _ = norm_back(sum_parts(parts_ref, here), values, gain_ref[...])
        grad_ref[here, :] = mid_grad_ref[here, :] + change
        return carry

    lax.fori_loop(0, tokens_ref.shape[0] // step, rows_step, 0)


def vmem_specs(count):
    return [pl.BlockSpec(memory_space=pltpu.VMEM)] * count


def local_kernel(kernel, name, operands, outs, scratch=()):
    return pl.pallas_call(
        kernel,
        out_shape=[jax.ShapeDtypeStruct(shape, kind) for shape, kind in outs],
        in_specs=[pl.BlockSpec(memory_space=pltpu.VMEM)] * len(operands),
        out_specs=[pl.BlockSpec(memory_space=pltpu.VMEM)] * len(outs),
        scratch_shapes=list(scratch),
        compiler_params=pltpu.CompilerParams(vmem_limit_bytes=vmem_limit),
        name=name,
    )(*operands)


def round_up(value):
    return -(-value // 128) * 128


def column_tiles(width, wide, block):
    tiles = []
    for start in range(0, wide, 256):
        stop = min(start + 256, wide)
        low = (start // block) * block
        high = ((min(stop, width) - 1) // block + 1) * block
        tiles.append((start, stop, low // 128 * 128, min(round_up(high), wide)))
    return tiles


def one_minus_exp(value):
    series = 1.0 + value * (1.0 / 8.0)
    for term in (7.0, 6.0, 5.0, 4.0, 3.0, 2.0):
        series = 1.0 + value * (1.0 / term) * series
    return jnp.where(value > -0.3, -value * series, 1.0 - jnp.exp(value))


def shift_down(tile, count, fill):
    moved = pltpu.roll(tile, count, 0)
    row = lax.broadcasted_iota(jnp.int32, tile.shape, 0)
    return jnp.where(row < count, fill, moved)


def shift_up(tile, count, fill):
    moved = pltpu.roll(tile, tile.shape[0] - count, 0)
    row = lax.broadcasted_iota(jnp.int32, tile.shape, 0)
    return jnp.where(row >= tile.shape[0] - count, fill, moved)


def blocked_product(first, second, weights, tiles, store, length, turned=False):
    step = 256

    def rows_step(index, carry):
        rows = pl.ds(pl.multiple_of(index * step, step), step)
        for start, stop, low, high in tiles:
            total = None
            for (high_ref, low_ref), (w_high, w_low) in zip((first, second), weights):
                if high_ref is None:
                    continue
                a_high = high_ref[rows, low:high]
                a_low = low_ref[rows, low:high]
                cut = (slice(start, stop), slice(low, high))
                cut = cut if turned else cut[::-1]
                b_high, b_low = w_high[cut], w_low[cut]
                dims = ((1,), (1,)) if turned else ((1,), (0,))
                part = mm(a_high, b_high, dims) + mm(a_high, b_low, dims) + mm(a_low, b_high, dims)
                total = part if total is None else total + part
            store(rows, slice(start, stop), total)
        return carry

    lax.fori_loop(0, length // step, rows_step, 0)


def recur_forward_kernel(
    tiles,
    signal_ref,
    masks_ref,
    vectors_ref,
    decay_high,
    decay_low,
    input_high,
    input_low,
    states_ref,
    values_ref,
    conv_ref,
    decay_rate_ref,
    input_rate_ref,
    padded,
    conv_high,
    conv_low,
):
    length, width = signal_ref.shape
    count = length // chunk
    padded[0:8, :] = jnp.zeros((8, width), f32)

    def pad_step(index, carry):
        begin = pl.multiple_of(index * chunk, chunk)
        here = pl.ds(begin, chunk)
        padded[pl.ds(begin + 8, chunk), :] = signal_ref[here, :].astype(f32)
        return carry

    lax.fori_loop(0, count, pad_step, 0)

    def conv_step(index, carry):
        begin = pl.multiple_of(index * chunk, chunk)
        rows = pl.ds(begin, chunk)
        window = padded[pl.ds(begin, chunk + 8), :]
        total = vectors_ref[4:5, :] + vectors_ref[0:1, :] * window[8:, :]
        for tap in range(1, 4):
            total = total + vectors_ref[tap : tap + 1, :] * (
                window[8 - tap : 8 - tap + chunk, :] * masks_ref[rows, tap : tap + 1]
            )
        conv_ref[rows, :] = total
        high, low = split_bf16(total)
        conv_high[rows, :] = high
        conv_low[rows, :] = low
        return carry

    lax.fori_loop(0, count, conv_step, 0)

    def store_decay(rows, columns, value):
        decay_rate_ref[rows, columns] = jax.nn.sigmoid(value + vectors_ref[5:6, columns])

    def store_input(rows, columns, value):
        input_rate_ref[rows, columns] = jax.nn.sigmoid(value + vectors_ref[6:7, columns])

    nothing = (None, None)
    blocked_product(
        (conv_high, conv_low), nothing, ((decay_high, decay_low), nothing), tiles, store_decay, length
    )
    blocked_product(
        (conv_high, conv_low), nothing, ((input_high, input_low), nothing), tiles, store_input, length
    )

    def scan_step(index, state):
        begin = pl.multiple_of(index * 8, 8)
        rows = pl.ds(begin, 8)
        restart = masks_ref[rows, 4:5]
        keep = 1.0 - restart
        log_decay = -vectors_ref[7:8, :] * decay_rate_ref[rows, :]
        mult = restart + keep * jnp.sqrt(one_minus_exp(2.0 * log_decay))
        carried = keep * jnp.exp(log_decay)
        total = mult * input_rate_ref[rows, :] * conv_ref[rows, :]
        for count_rows in (1, 2, 4):
            total = total + carried * shift_down(total, count_rows, 0.0)
            carried = carried * shift_down(carried, count_rows, 1.0)
        total = total + carried * state
        states_ref[rows, :] = total
        return total[7:8, :]

    lax.fori_loop(0, length // 8, scan_step, jnp.zeros((1, width), f32), unroll=4)

    def values_step(index, carry):
        begin = pl.multiple_of(index * chunk, chunk)
        here = pl.ds(begin, chunk)
        values_ref[here, :] = states_ref[pl.ds(begin, chunk), :].astype(bf16)
        return carry

    lax.fori_loop(0, count, values_step, 0)


def mixer_backward_kernel(
    tiles,
    state_grad_ref,
    branch_grad_ref,
    masks_ref,
    vectors_ref,
    mlp_ref,
    signal_any,
    states_any,
    conv_any,
    decay_rate_any,
    input_rate_any,
    decay_high_any,
    decay_low_any,
    input_high_any,
    input_low_any,
    both_any,
    normed_any,
    tokens_any,
    late_ref,
    decay_pre_ref,
    input_pre_ref,
    sums_ref,
    token_ref,
    signal_ref,
    states_ref,
    conv_ref,
    decay_rate_ref,
    input_rate_ref,
    decay_high,
    decay_low,
    input_high,
    input_low,
    both_ref,
    normed_ref,
    tokens_ref,
    both_grad_ref,
    padded,
    grads,
    earlier,
    decay_pre_high,
    decay_pre_low,
    input_pre_high,
    input_pre_low,
    gain_sums,
    arrived,
):
    fetched = [
        (signal_any, signal_ref),
        (states_any, states_ref),
        (conv_any, conv_ref),
        (decay_rate_any, decay_rate_ref),
        (input_rate_any, input_rate_ref),
        (decay_high_any, decay_high),
        (decay_low_any, decay_low),
        (input_high_any, input_high),
        (input_low_any, input_low),
        (both_any, both_ref),
        (normed_any, normed_ref),
    ]
    copies = [
        pltpu.make_async_copy(source, target, arrived.at[number])
        for number, (source, target) in enumerate(fetched)
    ]
    for copy in copies:
        copy.start()
    length, width = grads.shape[0] - 8, grads.shape[1]
    count = length // chunk
    padded[0:8, :] = jnp.zeros((8, width), f32)
    earlier[0:8, :] = jnp.zeros((8, width), f32)
    grads[length:, :] = jnp.zeros((8, width), f32)
    sums_ref[...] = jnp.zeros_like(sums_ref)

    for copy in copies[:5]:
        copy.wait()

    def pad_step(index, carry):
        begin = pl.multiple_of(index * chunk, chunk)
        here = pl.ds(begin, chunk)
        padded[pl.ds(begin + 8, chunk), :] = signal_ref[here, :].astype(f32)
        earlier[pl.ds(begin + 8, chunk), :] = states_ref[here, :]
        grads[here, :] = state_grad_ref[here, :].astype(f32)
        both_grad_ref[here, width:] = branch_grad_ref[here, :]
        return carry

    lax.fori_loop(0, count, pad_step, 0)

    def scan_step(index, later):
        begin = pl.multiple_of(length - 8 - index * 8, 8)
        rows = pl.ds(begin, 8)
        restart = masks_ref[rows, 4:5]
        keep = 1.0 - restart
        decay_rate = decay_rate_ref[rows, :]
        input_rate = input_rate_ref[rows, :]
        conv_out = conv_ref[rows, :]
        log_decay = -vectors_ref[7:8, :] * decay_rate
        decay = jnp.exp(log_decay)
        root = jnp.sqrt(one_minus_exp(2.0 * log_decay))
        mult = restart + keep * root
        carried = keep * decay
        flow = grads[rows, :]
        reach = shift_up(carried, 1, 1.0)
        for count_rows in (1, 2, 4):
            flow = flow + reach * shift_up(flow, count_rows, 0.0)
            reach = reach * shift_up(reach, count_rows, 1.0)
        flow = flow + reach * later
        window = earlier[pl.ds(begin, 16), :]
        before = window[7:15, :]
        flow_rate = flow * input_rate
        mult_grad = flow_rate * conv_out
        log_grad = keep * (flow * before * decay - mult_grad * decay * decay / root)
        rate_log = decay_rate * log_grad
        decay_pre = -vectors_ref[7:8, :] * rate_log * (1.0 - decay_rate)
        input_pre = mult_grad * mult * (1.0 - input_rate)
        grads[rows, :] = flow_rate * mult
        decay_pre_ref[rows, :] = decay_pre
        input_pre_ref[rows, :] = input_pre
        sums_ref[0:8, :] += rate_log
        sums_ref[8:16, :] += decay_pre
        sums_ref[16:24, :] += input_pre
        return carried[0:1, :] * flow[0:1, :]

    lax.fori_loop(0, length // 8, scan_step, jnp.zeros((1, width), f32), unroll=4)

    for copy in copies[5:9]:
        copy.wait()

    def split_step(index, carry):
        rows = pl.ds(pl.multiple_of(index * chunk, chunk), chunk)
        decay_pre_high[rows, :], decay_pre_low[rows, :] = split_bf16(decay_pre_ref[rows, :])
        input_pre_high[rows, :], input_pre_low[rows, :] = split_bf16(input_pre_ref[rows, :])
        return carry

    lax.fori_loop(0, count, split_step, 0)

    def store(rows, columns, value):
        grads[rows, columns] += value

    blocked_product(
        (decay_pre_high, decay_pre_low),
        (input_pre_high, input_pre_low),
        ((decay_high, decay_low), (input_high, input_low)),
        tiles,
        store,
        length,
        True,
    )

    def conv_step(index, carry):
        begin = pl.multiple_of(index * chunk, chunk)
        rows = pl.ds(begin, chunk)
        grad_window = grads[pl.ds(begin, chunk + 8), :]
        mask_window = masks_ref[pl.ds(begin, chunk + 8), :]
        signal_window = padded[pl.ds(begin, chunk + 8), :]
        here = grad_window[:chunk, :]
        result = vectors_ref[0:1, :] * here
        sums_ref[24:32, :] += fold8(here)
        sums_ref[32:40, :] += fold8(here * signal_window[8:, :])
        for tap in range(1, 4):
            masked = grad_window * mask_window[:, tap : tap + 1]
            result = result + vectors_ref[tap : tap + 1, :] * masked[tap : tap + chunk, :]
            sums_ref[32 + 8 * tap : 40 + 8 * tap, :] += fold8(
                masked[:chunk, :] * signal_window[8 - tap : 8 - tap + chunk, :]
            )
        here = pl.ds(begin, chunk)
        both_grad_ref[here, :width] = result.astype(bf16)
        return carry

    lax.fori_loop(0, count, conv_step, 0)
    copies[9].wait()
    copies[10].wait()
    each = late_ref.shape[1] * late_ref.shape[3]

    def late_step(index, carry):
        rows = pl.ds(pl.multiple_of(index * each, each), each)
        value = mm(normed_ref[:, rows], both_grad_ref[:, :width], ((0,), (0,))).astype(bf16)
        late_ref[index, :, 0] = value.reshape(late_ref.shape[1], *late_ref.shape[3:])
        return carry

    lax.fori_loop(0, late_ref.shape[0], late_step, 0)
    parts, rows, model_width = token_ref.shape
    rows = rows - gain_rows
    gain_sums[...] = jnp.zeros_like(gain_sums)

    def token_step(index, carry):
        here = pl.ds(pl.multiple_of(index * rows, rows), rows)
        copy = pltpu.make_async_copy(tokens_any.at[here, :], tokens_ref, arrived.at[len(fetched)])
        copy.start()
        grad = mm(both_grad_ref[here, :], both_ref[...], ((1,), (1,)))
        copy.wait()
        values = tokens_ref[...].astype(f32)
        gain_sums[...] += fold8(values * rms_scale(values) * grad)
        token_ref[index, :rows, :] = grad.astype(bf16)
        return carry

    lax.fori_loop(0, parts, token_step, 0)
    terms = []
    for total in (gain_sums[...], mlp_ref[...]):
        terms += split_bf16(total.sum(axis=0, keepdims=True))
    terms.append(jnp.zeros((gain_rows - len(terms), model_width), bf16))
    terms = jnp.concatenate([term.astype(f32) for term in terms], axis=0).astype(bf16)
    for part in range(parts):
        token_ref[part, rows:, :] = terms


def recur_forward(signal, masks, vectors, weights, tiles):
    length, width = signal.shape
    whole = ((length, width), f32)
    return local_kernel(
        functools.partial(recur_forward_kernel, tiles),
        "recur_forward",
        (signal, masks, vectors, *weights),
        [whole, ((length, width), bf16), whole, whole, whole],
        [
            pltpu.VMEM((length + 8, width), f32),
            pltpu.VMEM((length, width), bf16),
            pltpu.VMEM((length, width), bf16),
        ],
    )


def mixer_backward(resident, fetched, size, parts, tiles):
    length, wide = resident[0].shape
    model_width = fetched[-1].shape[1]
    whole = ((length, wide), f32)
    outs = [
        ((size, parts, 1, model_width // size // parts, wide), bf16),
        whole,
        whole,
        ((64, wide), f32),
        ((parts, length // parts + gain_rows, model_width), bf16),
    ]
    padded = pltpu.VMEM((length + 8, wide), f32)
    return pl.pallas_call(
        functools.partial(mixer_backward_kernel, tiles),
        out_shape=[jax.ShapeDtypeStruct(shape, kind) for shape, kind in outs],
        in_specs=vmem_specs(len(resident)) + [pl.BlockSpec(memory_space=pl.ANY)] * len(fetched),
        out_specs=vmem_specs(len(outs)),
        scratch_shapes=[pltpu.VMEM(value.shape, value.dtype) for value in fetched[:-1]]
        + [pltpu.VMEM((length // parts, model_width), bf16)]
        + [pltpu.VMEM((length, 2 * wide), bf16)]
        + [padded] * 3
        + [pltpu.VMEM((length, wide), bf16)] * 4
        + [pltpu.VMEM((8, model_width), f32), pltpu.SemaphoreType.DMA((len(fetched),))],
        compiler_params=pltpu.CompilerParams(vmem_limit_bytes=vmem_limit),
        name="mixer_backward",
    )(*resident, *fetched)


def column_grads_kernel(count, *refs):
    for number in range(count):
        value = mm(refs[number][...], refs[count + number][...], ((0,), (0,)))
        value = value.astype(bf16)
        refs[-1][0, :, number] = value.reshape(refs[-1].shape[1], *refs[-1].shape[3:])


def column_grads(lefts, rights, size, parts):
    length, model_width = lefts[0].shape
    wide = rights[0].shape[1]
    each, count = model_width // size, len(lefts)
    block = (1, parts, count, each // parts, wide)
    total = pl.pallas_call(
        functools.partial(column_grads_kernel, count),
        grid=(size,),
        in_specs=[pl.BlockSpec((length, each), lambda i: (0, i))] * count
        + [pl.BlockSpec((length, wide), lambda i: (0, 0))] * count,
        out_specs=pl.BlockSpec(block, lambda i: (i, 0, 0, 0, 0)),
        out_shape=jax.ShapeDtypeStruct((size,) + block[1:], bf16),
        compiler_params=pltpu.CompilerParams(vmem_limit_bytes=vmem_limit),
        name="column_grads",
    )(*lefts, *rights)
    return total


def gate_grads_kernel(tiles, conv_ref, decay_pre_ref, input_pre_ref, gates_ref, dense, pairs):
    heads, block = gates_ref.shape[1:3]
    pairs[0], pairs[1] = split_bf16(conv_ref[...])
    for gate, ref in enumerate((decay_pre_ref, input_pre_ref)):
        pairs[2], pairs[3] = split_bf16(ref[...])
        for start, stop, low, high in tiles:
            total = None
            for left, right in ((0, 2), (0, 3), (1, 2)):
                part = mm(pairs[left, :, low:high], pairs[right, :, start:stop], ((0,), (0,)))
                total = part if total is None else total + part
            dense[low:high, start:stop] = total
        for head in range(heads):
            cut = slice(head * block, (head + 1) * block)
            gates_ref[gate, head] = dense[cut, cut]


def dense_kernel(decay_ref, input_ref, decay_high, decay_low, input_high, input_low):
    heads, block, _ = decay_ref.shape
    for ref, high, low in (
        (decay_ref, decay_high, decay_low),
        (input_ref, input_high, input_low),
    ):
        high[...] = jnp.zeros_like(high)
        low[...] = jnp.zeros_like(low)
        for head in range(heads):
            cut = slice(head * block, (head + 1) * block)
            high[cut, cut], low[cut, cut] = split_bf16(ref[head])


def mlp_kernel(
    normed_ref,
    cotangent_ref,
    hidden_grad_ref,
    gate_ref,
    up_ref,
    down_ref,
    normed_grad_ref,
    out_ref,
    units_any,
    normed_total,
    out_total,
    gate_grads,
    up_grads,
    hidden_all,
    units,
    sent,
):
    step, steps = pl.program_id(0), pl.num_programs(0)
    length = normed_ref.shape[0]
    group = units.shape[1]
    gate_units = lambda: gate_ref[...].reshape(down_ref.shape)
    up_units = lambda: up_ref[...].reshape(down_ref.shape)

    @pl.when(step == 0)
    def _():
        normed_total[...] = jnp.zeros_like(normed_total)
        out_total[...] = jnp.zeros_like(out_total)

    def rows_step(index, carry):
        here = pl.ds(pl.multiple_of(index * 256, 256), 256)
        normed = normed_ref[here, :]
        gate_act, slope = gelu_parts(mm(normed, gate_units(), ((1,), (1,))))
        up_vals = mm(normed, up_units(), ((1,), (1,)))
        hidden_grad = hidden_grad_ref[here, :]
        gate_grads[here, :] = (hidden_grad * up_vals * slope).astype(bf16)
        up_grads[here, :] = (hidden_grad * gate_act).astype(bf16)
        hidden_all[here, :] = (gate_act * up_vals).astype(bf16)
        normed_total[here, :] += mm(gate_grads[here, :], gate_units(), ((1,), (0,))) + mm(
            up_grads[here, :], up_units(), ((1,), (0,))
        )
        out_total[here, :] += mm(hidden_all[here, :], down_ref[...], ((1,), (0,)))
        return carry

    lax.fori_loop(0, length // 256, rows_step, 0)

    def copy_of(number):
        return pltpu.make_async_copy(
            units.at[number], units_any.at[pl.ds(step * group, group), number], sent.at[number]
        )

    products = ((gate_grads, normed_ref), (up_grads, normed_ref), (hidden_all, cotangent_ref))
    for number, (left, right) in enumerate(products):

        @pl.when(step > 0)
        def _():
            copy_of(number).wait()

        value = mm(left[...], right[...], ((0,), (0,))).astype(bf16)
        units[number] = value.reshape(units.shape[1:])
        copy_of(number).start()

    @pl.when(step == steps - 1)
    def _():
        normed_grad_ref[...] = normed_total[...].astype(bf16)
        out_ref[...] = out_total[...].astype(bf16)
        for number in range(len(products)):
            copy_of(number).wait()


def mlp(normed, cotangent, hidden_grad, first_units, down_units):
    length, model_width = normed.shape
    parts, _, units, _ = first_units.shape
    total = parts * units
    group = 1
    while group * units % 128 or (group < parts and 2 * group * units * length <= 768 * 512):
        group *= 2
    tile = group * units
    first = lambda which: pl.BlockSpec(
        (group, 1, units, model_width), lambda i: (i, which, 0, 0)
    )
    weights = [first(0), first(1), pl.BlockSpec((tile, model_width), lambda i: (i, 0))]
    whole = jax.ShapeDtypeStruct((length, model_width), bf16)
    return pl.pallas_call(
        mlp_kernel,
        grid=(total // tile,),
        out_shape=[
            whole,
            whole,
            jax.ShapeDtypeStruct((parts, 3, units, model_width), bf16),
        ],
        in_specs=vmem_specs(2) + [pl.BlockSpec((length, tile), lambda i: (0, i))] + weights,
        out_specs=vmem_specs(2) + [pl.BlockSpec(memory_space=pl.ANY)],
        scratch_shapes=[pltpu.VMEM((length, model_width), f32)] * 2
        + [pltpu.VMEM((length, tile), bf16)] * 3
        + [pltpu.VMEM((3, group, units, model_width), bf16), pltpu.SemaphoreType.DMA((3,))],
        compiler_params=pltpu.CompilerParams(vmem_limit_bytes=vmem_limit),
        name="mlp",
    )(normed, cotangent, hidden_grad, first_units, first_units, down_units)


def body(
    sizes,
    tokens,
    segment_ids,
    mixer_gain,
    branch_weight,
    input_weight,
    output_weight,
    conv_weight,
    conv_bias,
    decay_gate,
    decay_bias,
    input_gate,
    input_bias,
    decay_param,
    mlp_gain,
    hidden_gate,
    hidden_up,
    hidden_down,
    cotangent,
):
    n_rows, n_blk = sizes
    own_tokens, own_grad = tokens[0], cotangent[0]
    segments = segment_ids[0]
    tok_count, model_width = own_tokens.shape
    width = conv_weight.shape[1]
    wide = round_up(width + 2)
    heads, block, _ = decay_gate.shape
    tiles = column_tiles(width, wide, block)
    row, blk = lax.axis_index("rows"), lax.axis_index("blk")
    square = (tok_count, model_width)
    shard = branch_weight.shape[0]
    units = hidden_gate.shape[0]

    (column_parts,) = local_kernel(
        functools.partial(split_columns_kernel, width, wide),
        "split_columns",
        (input_weight, branch_weight, output_weight, mixer_gain[:, None], mlp_gain[:, None]),
        [((n_blk, shard, 3 * wide), bf16)],
    )
    columns = swap_blk(column_parts).reshape(n_blk * shard, 3 * wide)
    weights = local_kernel(
        dense_kernel, "dense_gates", (decay_gate, input_gate), [((wide, wide), bf16)] * 4
    )
    down_units = lax.all_gather(hidden_down, "rows", axis=0, tiled=True)
    columns, token_own, grad_own, first_own, *weights = tie(
        columns,
        own_tokens,
        for_all(own_grad, n_blk),
        jnp.concatenate([hidden_gate, hidden_up], axis=0),
        *weights,
    )
    both_columns = lax.all_gather(columns[:, : 2 * wide], "rows", axis=0, tiled=True)
    output_columns = lax.all_gather(columns[:, 2 * wide :], "rows", axis=0, tiled=True)
    tokens_all, down_units = ring_blk(token_own, n_blk, down_units)
    tokens_all, grad_own, first_own = tie(tokens_all, grad_own, first_own)
    out_grad = swap_blk(grad_own).reshape(n_blk * tok_count, model_width)
    first_units = lax.all_gather(first_own, "rows", axis=0, tiled=True)
    first_units = first_units.reshape(n_rows, 2, units, model_width)

    masks = [jnp.ones_like(segments, dtype=f32)]
    for tap in range(1, 4):
        masks.append(
            jnp.concatenate(
                [jnp.zeros((tap,), f32), (segments[tap:] == segments[:-tap]).astype(f32)]
            )
        )
    masks.append(1.0 - masks[1])
    masks = jnp.pad(jnp.stack(masks, axis=1), ((0, 8), (0, 3)))
    vectors = jnp.concatenate(
        [
            conv_weight,
            conv_bias[None],
            decay_bias[None],
            input_bias[None],
            scale_c * jax.nn.softplus(-decay_param)[None],
        ],
        axis=0,
    )
    vectors = jnp.pad(vectors, ((0, 0), (0, wide - width)), constant_values=1.0)
    mixer_normed, signal, branch_pre, gains = local_kernel(
        functools.partial(mixer_in_kernel, width),
        "mixer_in",
        (tokens_all, both_columns),
        [
            (tokens_all.shape, bf16),
            ((n_blk * tok_count, wide), bf16),
            ((n_blk * tok_count, wide), f32),
            ((2, model_width), f32),
        ],
    )
    mixer_gains, mlp_gains = gains[0:1], gains[1:2]
    states, state_values, conv_out, decay_rate, input_rate = recur_forward(
        signal, masks, vectors, weights, tiles
    )
    mixed = (gelu_tanh(branch_pre) * state_values.astype(f32)).astype(bf16)
    mid_partial = mm(mixed, output_columns, ((1,), (1,))).astype(bf16)
    mid_partial, out_grad = tie(mid_partial, out_grad)
    mid_parts = ring_sum(mid_partial, n_blk)
    residual_mid, own_normed = local_kernel(
        mid_norm_kernel,
        "mid_norm",
        (mlp_gains, own_tokens, *mid_parts),
        [(square, f32), (square, bf16)],
    )

    mlp_normed = ring_blk(own_normed, n_blk)
    hidden_grad = mm(out_grad, down_units, ((1,), (1,)))
    normed_partial, out_partial, unit_sums = mlp(
        mlp_normed, out_grad, hidden_grad, first_units, down_units
    )
    normed_parts = ring_sum(normed_partial, n_blk)
    unit_sums = lax.psum_scatter(
        unit_sums.reshape(n_rows * 3 * units, model_width),
        "rows",
        scatter_dimension=0,
        tiled=True,
    )

    mid_grad, own_sent, mlp_gain_part = local_kernel(
        mid_grad_kernel,
        "mid_grad",
        (mlp_gains, residual_mid, own_grad, *normed_parts),
        [(square, f32), (square, bf16), ((8, model_width), f32)],
    )
    mid_sent = ring_blk(own_sent, n_blk)

    mid_sent, out_partial = tie(mid_sent, out_partial)
    out_parts = swap_blk(out_partial.reshape(n_blk, tok_count, model_width))
    mixed_grad = mm(mid_sent, output_columns, ((1,), (0,)))
    branch_act, branch_slope = gelu_parts(branch_pre)
    state_grad = (mixed_grad * branch_act).astype(bf16)
    branch_grad = (mixed_grad * state_values.astype(f32) * branch_slope).astype(bf16)
    early_sum = column_grads((mid_sent, mixer_normed), (mixed, branch_grad), n_rows, n_blk)
    early_shape = early_sum.shape[1:]
    early_sum = lax.psum_scatter(
        early_sum.reshape(-1, wide), "rows", scatter_dimension=0, tiled=True
    ).reshape(early_shape)
    late_sum, decay_pre_grad, input_pre_grad, sums, token_sent = mixer_backward(
        (state_grad, branch_grad, masks, vectors, mlp_gain_part),
        (
            signal,
            states,
            conv_out,
            decay_rate,
            input_rate,
            *weights,
            both_columns,
            mixer_normed,
            tokens_all,
        ),
        n_rows,
        n_blk,
        tiles,
    )
    token_sent, out_parts, unit_sums, late_sum, decay_pre_grad, input_pre_grad, sums = tie(
        token_sent, out_parts, unit_sums, late_sum, decay_pre_grad, input_pre_grad, sums
    )
    token_parts = swap_blk(token_sent)
    late_sum = sum_columns(late_sum, n_rows)
    (gate_sums,) = local_kernel(
        functools.partial(gate_grads_kernel, tiles),
        "gate_grads",
        (conv_out, decay_pre_grad, input_pre_grad),
        [((2, heads, block, block), f32)],
        [pltpu.VMEM((wide, wide), f32), pltpu.VMEM((4,) + signal.shape, bf16)],
    )
    gate_sums, token_parts = tie(gate_sums, token_parts)
    gate_sums = [gate_sums[0], gate_sums[1]]
    one_way = bits_of(n_rows)
    other_way = one_way[:1] + one_way[:0:-1]
    vector_sums = sums.reshape(8, 8, wide).sum(axis=1)
    for at, bit in enumerate(bits_of(n_rows)):
        for number, order in enumerate((one_way, other_way)):
            gate_sums[number] = add_from(gate_sums[number], n_rows, order[at], bf16)
        vector_sums = add_from(vector_sums, n_rows, bit)
        vector_sums, *gate_sums = tie(vector_sums, *gate_sums)
    token_parts, early_sum, late_sum = tie(token_parts, early_sum, late_sum)
    vector_sums = vector_sums[:, :width]
    token_grad, gain_sums = local_kernel(
        token_grad_kernel,
        "token_grad",
        (mixer_gains, own_tokens, mid_grad, token_parts),
        [(square, f32), ((2, model_width), f32)],
    )
    gain_sums = sum_rows(gain_sums, n_rows)

    column_sums = swap_blk(jnp.concatenate([early_sum, late_sum], axis=1))
    output_weight_grad, branch_weight_grad, input_weight_grad = local_kernel(
        functools.partial(join_columns_kernel, width),
        "join_columns",
        (column_sums,),
        [((shard, n_blk * width), f32)] * 3,
    )
    block_out = (residual_mid + out_parts.astype(f32).sum(axis=0)).astype(bf16)

    gain_sums = lax.dynamic_slice_in_dim(
        gain_sums, (row * n_blk + blk) * mixer_gain.shape[0], mixer_gain.shape[0], axis=1
    )

    return (
        block_out[None],
        token_grad[None],
        gain_sums[0],
        branch_weight_grad,
        input_weight_grad,
        output_weight_grad,
        vector_sums[4:8],
        vector_sums[3],
        gate_sums[0],
        vector_sums[1],
        gate_sums[1],
        vector_sums[2],
        scale_c * jax.nn.sigmoid(-decay_param) * vector_sums[0],
        gain_sums[1],
        unit_sums[:units].astype(f32),
        unit_sums[units : 2 * units].astype(f32),
        unit_sums[2 * units :].astype(f32),
    )


def solution(mesh):
    by_all = P(("rows", "blk"))
    by_all_rows = P(("rows", "blk"), None)
    tokens_spec = P("rows", "blk", None)
    by_blk = P("blk")
    by_blk_heads = P("blk", None, None)
    taps = P(None, "blk")
    recurrence = (taps, by_blk, by_blk_heads, by_blk, by_blk_heads, by_blk, by_blk)
    return jax.shard_map(
        functools.partial(body, (mesh.shape["rows"], mesh.shape["blk"])),
        mesh=mesh,
        in_specs=(tokens_spec, P("rows", None), by_all)
        + (by_all_rows,) * 3
        + recurrence
        + (by_all,)
        + (by_all_rows,) * 3
        + (tokens_spec,),
        out_specs=(tokens_spec, tokens_spec, by_all)
        + (by_all_rows,) * 3
        + recurrence
        + (by_all,)
        + (by_all_rows,) * 3,
        check_vma=False,
    )
```

```python
import functools

import jax
import jax.numpy as jnp
from jax import lax
from jax.experimental import pallas as pl
from jax.experimental.pallas import tpu as pltpu
from jax.sharding import PartitionSpec as P

epsilon = 1e-06
scale_c = 8.0
bf16 = jnp.bfloat16
f32 = jnp.float32
chunk = 64
vmem_limit = 60 * 1024 * 1024


def rms_scale(values):
    return lax.rsqrt(jnp.mean(values * values, axis=-1, keepdims=True) + epsilon)


def gelu_tanh(values):
    return jax.nn.gelu(values, approximate=True)


def gelu_parts(values):
    slope, cubic = 0.7978845608028654, 0.044715
    square = values * values
    bend = jnp.tanh(slope * values * (1.0 + cubic * square))
    lift = 0.5 + 0.5 * bend
    turn = 0.5 * values * (1.0 - bend * bend) * (slope * (1.0 + 3.0 * cubic * square))
    return values * lift, lift + turn


def mm(left, right, dims):
    return lax.dot_general(left, right, (dims, ((), ())), preferred_element_type=f32)


def split_bf16(value):
    high = value.astype(bf16)
    return high, (value - high.astype(f32)).astype(bf16)


def tie(*values):
    return lax.optimization_barrier(values)


def flip(size, bit):
    return [(place, place ^ bit) for place in range(size)]


def bits_of(size):
    found, bit = [], 1
    while bit < size:
        found.append(bit)
        bit *= 2
    return found


def swap_blk(parts):
    return lax.all_to_all(parts, "blk", split_axis=0, concat_axis=0, tiled=True)


def ring_blk(part, size, beside=None):
    me, rows = lax.axis_index("blk"), part.shape[0]
    whole = jnp.zeros((size * rows,) + part.shape[1:], part.dtype)
    whole = lax.dynamic_update_slice_in_dim(whole, part, me * rows, axis=0)
    for step in range(1, size):
        part = lax.ppermute(part, "blk", [(place, (place + 1) % size) for place in range(size)])
        if step == 1 and beside is not None:
            part, beside = tie(part, beside)
        place = (me - step) % size
        whole = lax.dynamic_update_slice_in_dim(whole, part, place * rows, axis=0)
    return whole if beside is None else (whole, beside)


def ring_sum(partial, size):
    me, rows = lax.axis_index("blk"), partial.shape[0] // size
    pick = lambda place: lax.dynamic_slice_in_dim(partial, place % size * rows, rows, axis=0)
    total = pick(me - 1 + size)
    for step in range(1, size):
        total = lax.ppermute(total, "blk", [(place, (place + 1) % size) for place in range(size)])
        if step < size - 1:
            total = (total.astype(f32) + pick(me - 1 - step + size).astype(f32)).astype(bf16)
    return total, pick(me)


def for_all(part, size):
    return jnp.broadcast_to(part[None], (size,) + part.shape)


def halve(total, size, bit, left):
    axis = left.index(bit)
    left.remove(bit)
    mine = (lax.axis_index("rows") // bit) % 2
    away = lax.dynamic_index_in_dim(total, 1 - mine, axis, keepdims=False)
    keep = lax.dynamic_index_in_dim(total, mine, axis, keepdims=False)
    got = lax.ppermute(away, "rows", flip(size, bit))
    return (keep.astype(f32) + got.astype(f32)).astype(bf16)


def sum_columns(total, size, beside):
    left = list(reversed(bits_of(size)))
    total = total.reshape((2,) * len(left) + total.shape[1:])
    total = halve(total, size, 1, left)
    beside = [add_from(value, size, 1) for value in beside]
    half, order = total.shape[-1] // 2, bits_of(size)[1:]
    found = []
    for cut, bits in ((total[..., :half], order), (total[..., half:], order[::-1])):
        rest = list(left)
        found.append([cut, bits, rest])
    for at in range(len(order)):
        for piece in found:
            piece[0] = halve(piece[0], size, piece[1][at], piece[2])
        beside = [add_from(value, size, order[at]) for value in beside]
        found[0][0], found[1][0], *beside = tie(found[0][0], found[1][0], *beside)
    return jnp.concatenate([found[0][0], found[1][0]], axis=-1), beside


def add_from(value, size, bit, wire=f32):
    return value + lax.ppermute(value.astype(wire), "rows", flip(size, bit)).astype(f32)


def split_columns_kernel(
    width, wide, input_ref, branch_ref, output_ref, mixer_ref, mlp_ref, both_ref
):
    parts = both_ref.shape[0]
    both_ref[...] = jnp.zeros_like(both_ref)
    for part in range(parts):
        cut = slice(part * width, (part + 1) * width)
        both_ref[part, :, :width] = input_ref[:, cut]
        both_ref[part, :, wide : wide + width] = branch_ref[:, cut]
        both_ref[part, :, 2 * wide : 2 * wide + width] = output_ref[:, cut]
        both_ref[part, :, width : width + 1] = mixer_ref[...]
        both_ref[part, :, width + 1 : width + 2] = mlp_ref[...]


def join_columns_kernel(width, parts_ref, *out_refs):
    for part in range(parts_ref.shape[0]):
        cut = slice(part * width, (part + 1) * width)
        for number, out_ref in enumerate(out_refs):
            out_ref[:, cut] = parts_ref[part, number, :, :width].astype(f32)


def mixer_in_kernel(width, tokens_ref, columns_ref, normed_ref, signal_ref, branch_ref, gains_ref):
    step = 256
    begin = width // 128 * 128
    turned = columns_ref[:, begin : begin + 128].astype(f32).T
    gains_ref[...] = turned[width - begin : width - begin + 2, :]
    gain = gains_ref[0:1, :]

    def rows_step(index, carry):
        here = pl.ds(pl.multiple_of(index * step, step), step)
        values = tokens_ref[here, :].astype(f32)
        normed_ref[here, :] = (values * rms_scale(values) * gain).astype(bf16)
        value = mm(normed_ref[here, :], columns_ref[...], ((1,), (0,)))
        wide = signal_ref.shape[1]
        signal_ref[here, :] = value[:, :wide].astype(bf16)
        branch_ref[here, :] = value[:, wide:]
        return carry

    lax.fori_loop(0, tokens_ref.shape[0] // step, rows_step, 0)


def sum_parts(parts_ref, here):
    total = parts_ref[0, here, :].astype(f32)
    for part in range(1, parts_ref.shape[0]):
        total = total + parts_ref[part, here, :].astype(f32)
    return total


def mid_norm_kernel(gain_ref, tokens_ref, one_ref, two_ref, mid_ref, normed_ref):
    step = 32

    def rows_step(index, carry):
        here = pl.ds(pl.multiple_of(index * step, step), step)
        values = tokens_ref[here, :].astype(f32) + one_ref[here, :].astype(f32)
        values = values + two_ref[here, :].astype(f32)
        mid_ref[here, :] = values
        normed = (values * rms_scale(values) * gain_ref[...]).astype(bf16)
        normed_ref[here, :] = normed
        return carry

    lax.fori_loop(0, tokens_ref.shape[0] // step, rows_step, 0)


def fold8(value):
    return value.reshape(value.shape[0] // 8, 8, value.shape[1]).sum(axis=0)


def norm_back(grad, values, gain):
    scale = rms_scale(values)
    product = grad * values
    factor = scale * scale * scale * jnp.mean(product * gain, axis=-1, keepdims=True)
    return scale * (grad * gain) - values * factor, product * scale


def mid_grad_kernel(
    gain_ref, mid_ref, cotangent_ref, one_ref, two_ref, grad_ref, sent_ref, sums_ref
):
    step = 32
    sums_ref[...] = jnp.zeros_like(sums_ref)

    def rows_step(index, carry):
        here = pl.ds(pl.multiple_of(index * step, step), step)
        grad = one_ref[here, :].astype(f32) + two_ref[here, :].astype(f32)
        change, terms = norm_back(grad, mid_ref[here, :], gain_ref[...])
        sums_ref[...] += fold8(terms)
        result = cotangent_ref[here, :].astype(f32) + change
        grad_ref[here, :] = result
        sent = result.astype(bf16)
        sent_ref[here, :] = sent
        return carry

    lax.fori_loop(0, mid_ref.shape[0] // step, rows_step, 0)


def token_grad_kernel(gain_ref, tokens_ref, mid_grad_ref, parts_ref, grad_ref):
    step = 32

    def rows_step(index, carry):
        here = pl.ds(pl.multiple_of(index * step, step), step)
        values = tokens_ref[here, :].astype(f32)
        change, _ = norm_back(sum_parts(parts_ref, here), values, gain_ref[...])
        grad_ref[here, :] = mid_grad_ref[here, :] + change
        return carry

    lax.fori_loop(0, tokens_ref.shape[0] // step, rows_step, 0)


def vmem_specs(count):
    return [pl.BlockSpec(memory_space=pltpu.VMEM)] * count


def local_kernel(kernel, name, operands, outs, scratch=()):
    return pl.pallas_call(
        kernel,
        out_shape=[jax.ShapeDtypeStruct(shape, kind) for shape, kind in outs],
        in_specs=[pl.BlockSpec(memory_space=pltpu.VMEM)] * len(operands),
        out_specs=[pl.BlockSpec(memory_space=pltpu.VMEM)] * len(outs),
        scratch_shapes=list(scratch),
        compiler_params=pltpu.CompilerParams(vmem_limit_bytes=vmem_limit),
        name=name,
    )(*operands)


def round_up(value):
    return -(-value // 128) * 128


def column_tiles(width, wide, block):
    tiles = []
    for start in range(0, wide, 256):
        stop = min(start + 256, wide)
        low = (start // block) * block
        high = ((min(stop, width) - 1) // block + 1) * block
        tiles.append((start, stop, low // 128 * 128, min(round_up(high), wide)))
    return tiles


def one_minus_exp(value):
    series = 1.0 + value * (1.0 / 8.0)
    for term in (7.0, 6.0, 5.0, 4.0, 3.0, 2.0):
        series = 1.0 + value * (1.0 / term) * series
    return jnp.where(value > -0.3, -value * series, 1.0 - jnp.exp(value))


def shift_down(tile, count, fill):
    moved = pltpu.roll(tile, count, 0)
    row = lax.broadcasted_iota(jnp.int32, tile.shape, 0)
    return jnp.where(row < count, fill, moved)


def shift_up(tile, count, fill):
    moved = pltpu.roll(tile, tile.shape[0] - count, 0)
    row = lax.broadcasted_iota(jnp.int32, tile.shape, 0)
    return jnp.where(row >= tile.shape[0] - count, fill, moved)


def blocked_product(first, second, weights, tiles, store, length, turned=False):
    step = 256

    def rows_step(index, carry):
        rows = pl.ds(pl.multiple_of(index * step, step), step)
        for start, stop, low, high in tiles:
            total = None
            for (high_ref, low_ref), (w_high, w_low) in zip((first, second), weights):
                if high_ref is None:
                    continue
                a_high = high_ref[rows, low:high]
                a_low = low_ref[rows, low:high]
                cut = (slice(start, stop), slice(low, high))
                cut = cut if turned else cut[::-1]
                b_high, b_low = w_high[cut], w_low[cut]
                dims = ((1,), (1,)) if turned else ((1,), (0,))
                part = mm(a_high, b_high, dims) + mm(a_high, b_low, dims) + mm(a_low, b_high, dims)
                total = part if total is None else total + part
            store(rows, slice(start, stop), total)
        return carry

    lax.fori_loop(0, length // step, rows_step, 0)


def recur_forward_kernel(
    tiles,
    signal_ref,
    masks_ref,
    vectors_ref,
    decay_high,
    decay_low,
    input_high,
    input_low,
    states_ref,
    values_ref,
    conv_ref,
    decay_rate_ref,
    input_rate_ref,
    padded,
    conv_high,
    conv_low,
):
    length, width = signal_ref.shape
    count = length // chunk
    padded[0:8, :] = jnp.zeros((8, width), f32)

    def pad_step(index, carry):
        begin = pl.multiple_of(index * chunk, chunk)
        here = pl.ds(begin, chunk)
        padded[pl.ds(begin + 8, chunk), :] = signal_ref[here, :].astype(f32)
        return carry

    lax.fori_loop(0, count, pad_step, 0)

    def conv_step(index, carry):
        begin = pl.multiple_of(index * chunk, chunk)
        rows = pl.ds(begin, chunk)
        window = padded[pl.ds(begin, chunk + 8), :]
        total = vectors_ref[4:5, :] + vectors_ref[0:1, :] * window[8:, :]
        for tap in range(1, 4):
            total = total + vectors_ref[tap : tap + 1, :] * (
                window[8 - tap : 8 - tap + chunk, :] * masks_ref[rows, tap : tap + 1]
            )
        conv_ref[rows, :] = total
        high, low = split_bf16(total)
        conv_high[rows, :] = high
        conv_low[rows, :] = low
        return carry

    lax.fori_loop(0, count, conv_step, 0)

    def store_decay(rows, columns, value):
        decay_rate_ref[rows, columns] = jax.nn.sigmoid(value + vectors_ref[5:6, columns])

    def store_input(rows, columns, value):
        input_rate_ref[rows, columns] = jax.nn.sigmoid(value + vectors_ref[6:7, columns])

    nothing = (None, None)
    blocked_product(
        (conv_high, conv_low), nothing, ((decay_high, decay_low), nothing), tiles, store_decay, length
    )
    blocked_product(
        (conv_high, conv_low), nothing, ((input_high, input_low), nothing), tiles, store_input, length
    )

    def scan_step(index, state):
        begin = pl.multiple_of(index * 8, 8)
        rows = pl.ds(begin, 8)
        restart = masks_ref[rows, 4:5]
        keep = 1.0 - restart
        log_decay = -vectors_ref[7:8, :] * decay_rate_ref[rows, :]
        mult = restart + keep * jnp.sqrt(one_minus_exp(2.0 * log_decay))
        carried = keep * jnp.exp(log_decay)
        total = mult * input_rate_ref[rows, :] * conv_ref[rows, :]
        for count_rows in (1, 2, 4):
            total = total + carried * shift_down(total, count_rows, 0.0)
            carried = carried * shift_down(carried, count_rows, 1.0)
        total = total + carried * state
        states_ref[rows, :] = total
        return total[7:8, :]

    lax.fori_loop(0, length // 8, scan_step, jnp.zeros((1, width), f32), unroll=4)

    def values_step(index, carry):
        begin = pl.multiple_of(index * chunk, chunk)
        here = pl.ds(begin, chunk)
        values_ref[here, :] = states_ref[pl.ds(begin, chunk), :].astype(bf16)
        return carry

    lax.fori_loop(0, count, values_step, 0)


def mixer_backward_kernel(
    tiles,
    state_grad_ref,
    branch_grad_ref,
    masks_ref,
    vectors_ref,
    mlp_ref,
    signal_any,
    states_any,
    conv_any,
    decay_rate_any,
    input_rate_any,
    decay_high_any,
    decay_low_any,
    input_high_any,
    input_low_any,
    both_any,
    normed_any,
    tokens_any,
    late_ref,
    sums_ref,
    gains_ref,
    gates_ref,
    token_ref,
    signal_ref,
    states_ref,
    conv_ref,
    decay_rate_ref,
    input_rate_ref,
    decay_high,
    decay_low,
    input_high,
    input_low,
    both_ref,
    normed_ref,
    tokens_ref,
    both_grad_ref,
    padded,
    grads,
    earlier,
    decay_pre_ref,
    input_pre_ref,
    decay_pre_high,
    decay_pre_low,
    input_pre_high,
    input_pre_low,
    conv_high,
    conv_low,
    dense,
    gain_sums,
    arrived,
):
    fetched = [
        (signal_any, signal_ref),
        (states_any, states_ref),
        (conv_any, conv_ref),
        (decay_rate_any, decay_rate_ref),
        (input_rate_any, input_rate_ref),
        (decay_high_any, decay_high),
        (decay_low_any, decay_low),
        (input_high_any, input_high),
        (input_low_any, input_low),
        (both_any, both_ref),
        (normed_any, normed_ref),
    ]
    copies = [
        pltpu.make_async_copy(source, target, arrived.at[number])
        for number, (source, target) in enumerate(fetched)
    ]
    for copy in copies:
        copy.start()
    length, width = grads.shape[0] - 8, grads.shape[1]
    count = length // chunk
    padded[0:8, :] = jnp.zeros((8, width), f32)
    earlier[0:8, :] = jnp.zeros((8, width), f32)
    grads[length:, :] = jnp.zeros((8, width), f32)
    sums_ref[...] = jnp.zeros_like(sums_ref)

    for copy in copies[:5]:
        copy.wait()

    def pad_step(index, carry):
        begin = pl.multiple_of(index * chunk, chunk)
        here = pl.ds(begin, chunk)
        padded[pl.ds(begin + 8, chunk), :] = signal_ref[here, :].astype(f32)
        earlier[pl.ds(begin + 8, chunk), :] = states_ref[here, :]
        grads[here, :] = state_grad_ref[here, :].astype(f32)
        both_grad_ref[here, width:] = branch_grad_ref[here, :]
        return carry

    lax.fori_loop(0, count, pad_step, 0)

    def scan_step(index, later):
        begin = pl.multiple_of(length - 8 - index * 8, 8)
        rows = pl.ds(begin, 8)
        restart = masks_ref[rows, 4:5]
        keep = 1.0 - restart
        decay_rate = decay_rate_ref[rows, :]
        input_rate = input_rate_ref[rows, :]
        conv_out = conv_ref[rows, :]
        log_decay = -vectors_ref[7:8, :] * decay_rate
        decay = jnp.exp(log_decay)
        root = jnp.sqrt(one_minus_exp(2.0 * log_decay))
        mult = restart + keep * root
        carried = keep * decay
        flow = grads[rows, :]
        reach = shift_up(carried, 1, 1.0)
        for count_rows in (1, 2, 4):
            flow = flow + reach * shift_up(flow, count_rows, 0.0)
            reach = reach * shift_up(reach, count_rows, 1.0)
        flow = flow + reach * later
        window = earlier[pl.ds(begin, 16), :]
        before = window[7:15, :]
        flow_rate = flow * input_rate
        mult_grad = flow_rate * conv_out
        log_grad = keep * (flow * before * decay - mult_grad * decay * decay / root)
        rate_log = decay_rate * log_grad
        decay_pre = -vectors_ref[7:8, :] * rate_log * (1.0 - decay_rate)
        input_pre = mult_grad * mult * (1.0 - input_rate)
        grads[rows, :] = flow_rate * mult
        decay_pre_ref[rows, :] = decay_pre
        input_pre_ref[rows, :] = input_pre
        sums_ref[0:8, :] += rate_log
        sums_ref[8:16, :] += decay_pre
        sums_ref[16:24, :] += input_pre
        return carried[0:1, :] * flow[0:1, :]

    lax.fori_loop(0, length // 8, scan_step, jnp.zeros((1, width), f32), unroll=4)

    for copy in copies[5:9]:
        copy.wait()

    def split_step(index, carry):
        rows = pl.ds(pl.multiple_of(index * chunk, chunk), chunk)
        decay_pre_high[rows, :], decay_pre_low[rows, :] = split_bf16(decay_pre_ref[rows, :])
        input_pre_high[rows, :], input_pre_low[rows, :] = split_bf16(input_pre_ref[rows, :])
        conv_high[rows, :], conv_low[rows, :] = split_bf16(conv_ref[rows, :])
        return carry

    lax.fori_loop(0, count, split_step, 0)

    def store(rows, columns, value):
        grads[rows, columns] += value

    blocked_product(
        (decay_pre_high, decay_pre_low),
        (input_pre_high, input_pre_low),
        ((decay_high, decay_low), (input_high, input_low)),
        tiles,
        store,
        length,
        True,
    )

    def conv_step(index, carry):
        begin = pl.multiple_of(index * chunk, chunk)
        rows = pl.ds(begin, chunk)
        grad_window = grads[pl.ds(begin, chunk + 8), :]
        mask_window = masks_ref[pl.ds(begin, chunk + 8), :]
        signal_window = padded[pl.ds(begin, chunk + 8), :]
        here = grad_window[:chunk, :]
        result = vectors_ref[0:1, :] * here
        sums_ref[24:32, :] += fold8(here)
        sums_ref[32:40, :] += fold8(here * signal_window[8:, :])
        for tap in range(1, 4):
            masked = grad_window * mask_window[:, tap : tap + 1]
            result = result + vectors_ref[tap : tap + 1, :] * masked[tap : tap + chunk, :]
            sums_ref[32 + 8 * tap : 40 + 8 * tap, :] += fold8(
                masked[:chunk, :] * signal_window[8 - tap : 8 - tap + chunk, :]
            )
        here = pl.ds(begin, chunk)
        both_grad_ref[here, :width] = result.astype(bf16)
        return carry

    lax.fori_loop(0, count, conv_step, 0)
    copies[9].wait()
    copies[10].wait()
    each = late_ref.shape[1] * late_ref.shape[3]

    def late_step(index, carry):
        rows = pl.ds(pl.multiple_of(index * each, each), each)
        value = mm(normed_ref[:, rows], both_grad_ref[:, :width], ((0,), (0,))).astype(bf16)
        late_ref[index, :, 0] = value.reshape(late_ref.shape[1], *late_ref.shape[3:])
        return carry

    lax.fori_loop(0, late_ref.shape[0], late_step, 0)
    parts, rows, _ = token_ref.shape
    gain_sums[...] = jnp.zeros_like(gain_sums)

    def token_step(index, carry):
        here = pl.ds(pl.multiple_of(index * rows, rows), rows)
        copy = pltpu.make_async_copy(tokens_any.at[here, :], tokens_ref, arrived.at[len(fetched)])
        copy.start()
        grad = mm(both_grad_ref[here, :], both_ref[...], ((1,), (1,)))
        copy.wait()
        values = tokens_ref[...].astype(f32)
        gain_sums[...] += fold8(values * rms_scale(values) * grad)
        token_ref[index] = grad.astype(bf16)
        return carry

    lax.fori_loop(0, parts, token_step, 0)
    heads, block = gates_ref.shape[1:3]
    for gate, (high, low) in enumerate(
        ((decay_pre_high, decay_pre_low), (input_pre_high, input_pre_low))
    ):
        for start, stop, first, last in tiles:
            total = None
            for left, right in ((conv_high, high), (conv_high, low), (conv_low, high)):
                part = mm(left[:, first:last], right[:, start:stop], ((0,), (0,)))
                total = part if total is None else total + part
            dense[first:last, start:stop] = total
        for head in range(heads):
            cut = slice(head * block, (head + 1) * block)
            gates_ref[gate, head] = dense[cut, cut]
    for row, total in enumerate((gain_sums, mlp_ref)):
        gains_ref[row : row + 1, :] = total[...].sum(axis=0, keepdims=True)


def recur_forward(signal, masks, vectors, weights, tiles):
    length, width = signal.shape
    whole = ((length, width), f32)
    return local_kernel(
        functools.partial(recur_forward_kernel, tiles),
        "recur_forward",
        (signal, masks, vectors, *weights),
        [whole, ((length, width), bf16), whole, whole, whole],
        [
            pltpu.VMEM((length + 8, width), f32),
            pltpu.VMEM((length, width), bf16),
            pltpu.VMEM((length, width), bf16),
        ],
    )


def mixer_backward(resident, fetched, size, parts, tiles, gates_shape):
    length, wide = resident[0].shape
    model_width = fetched[-1].shape[1]
    outs = [
        ((size, parts, 1, model_width // size // parts, wide), bf16),
        ((64, wide), f32),
        ((2, model_width), f32),
        (gates_shape, f32),
        ((parts, length // parts, model_width), bf16),
    ]
    padded = pltpu.VMEM((length + 8, wide), f32)
    return pl.pallas_call(
        functools.partial(mixer_backward_kernel, tiles),
        out_shape=[jax.ShapeDtypeStruct(shape, kind) for shape, kind in outs],
        in_specs=vmem_specs(len(resident)) + [pl.BlockSpec(memory_space=pl.ANY)] * len(fetched),
        out_specs=vmem_specs(len(outs)),
        scratch_shapes=[pltpu.VMEM(value.shape, value.dtype) for value in fetched[:-1]]
        + [pltpu.VMEM((length // parts, model_width), bf16)]
        + [pltpu.VMEM((length, 2 * wide), bf16)]
        + [padded] * 3
        + [pltpu.VMEM((length, wide), f32)] * 2
        + [pltpu.VMEM((length, wide), bf16)] * 6
        + [pltpu.VMEM((wide, wide), f32), pltpu.VMEM((8, model_width), f32), pltpu.SemaphoreType.DMA((len(fetched),))],
        compiler_params=pltpu.CompilerParams(vmem_limit_bytes=vmem_limit),
        name="mixer_backward",
    )(*resident, *fetched)


def column_grads_kernel(count, *refs):
    for number in range(count):
        value = mm(refs[number][...], refs[count + number][...], ((0,), (0,)))
        value = value.astype(bf16)
        refs[-1][0, :, number] = value.reshape(refs[-1].shape[1], *refs[-1].shape[3:])


def column_grads(lefts, rights, size, parts):
    length, model_width = lefts[0].shape
    wide = rights[0].shape[1]
    each, count = model_width // size, len(lefts)
    block = (1, parts, count, each // parts, wide)
    total = pl.pallas_call(
        functools.partial(column_grads_kernel, count),
        grid=(size,),
        in_specs=[pl.BlockSpec((length, each), lambda i: (0, i))] * count
        + [pl.BlockSpec((length, wide), lambda i: (0, 0))] * count,
        out_specs=pl.BlockSpec(block, lambda i: (i, 0, 0, 0, 0)),
        out_shape=jax.ShapeDtypeStruct((size,) + block[1:], bf16),
        compiler_params=pltpu.CompilerParams(vmem_limit_bytes=vmem_limit),
        name="column_grads",
    )(*lefts, *rights)
    return total


def dense_kernel(decay_ref, input_ref, decay_high, decay_low, input_high, input_low):
    heads, block, _ = decay_ref.shape
    for ref, high, low in (
        (decay_ref, decay_high, decay_low),
        (input_ref, input_high, input_low),
    ):
        high[...] = jnp.zeros_like(high)
        low[...] = jnp.zeros_like(low)
        for head in range(heads):
            cut = slice(head * block, (head + 1) * block)
            high[cut, cut], low[cut, cut] = split_bf16(ref[head])


def mlp_kernel(
    normed_ref,
    cotangent_ref,
    hidden_grad_ref,
    gate_ref,
    up_ref,
    down_ref,
    normed_grad_ref,
    out_ref,
    units_any,
    normed_total,
    out_total,
    gate_grads,
    up_grads,
    hidden_all,
    units,
    sent,
):
    step, steps = pl.program_id(0), pl.num_programs(0)
    length = normed_ref.shape[0]
    group = units.shape[1]
    gate_units = lambda: gate_ref[...].reshape(down_ref.shape)
    up_units = lambda: up_ref[...].reshape(down_ref.shape)

    @pl.when(step == 0)
    def _():
        normed_total[...] = jnp.zeros_like(normed_total)
        out_total[...] = jnp.zeros_like(out_total)

    def rows_step(index, carry):
        here = pl.ds(pl.multiple_of(index * 256, 256), 256)
        normed = normed_ref[here, :]
        gate_act, slope = gelu_parts(mm(normed, gate_units(), ((1,), (1,))))
        up_vals = mm(normed, up_units(), ((1,), (1,)))
        hidden_grad = hidden_grad_ref[here, :]
        gate_grads[here, :] = (hidden_grad * up_vals * slope).astype(bf16)
        up_grads[here, :] = (hidden_grad * gate_act).astype(bf16)
        hidden_all[here, :] = (gate_act * up_vals).astype(bf16)
        normed_total[here, :] += mm(gate_grads[here, :], gate_units(), ((1,), (0,))) + mm(
            up_grads[here, :], up_units(), ((1,), (0,))
        )
        out_total[here, :] += mm(hidden_all[here, :], down_ref[...], ((1,), (0,)))
        return carry

    lax.fori_loop(0, length // 256, rows_step, 0)

    def copy_of(number):
        return pltpu.make_async_copy(
            units.at[number], units_any.at[pl.ds(step * group, group), number], sent.at[number]
        )

    products = ((gate_grads, normed_ref), (up_grads, normed_ref), (hidden_all, cotangent_ref))
    for number, (left, right) in enumerate(products):

        @pl.when(step > 0)
        def _():
            copy_of(number).wait()

        value = mm(left[...], right[...], ((0,), (0,))).astype(bf16)
        units[number] = value.reshape(units.shape[1:])
        copy_of(number).start()

    @pl.when(step == steps - 1)
    def _():
        normed_grad_ref[...] = normed_total[...].astype(bf16)
        out_ref[...] = out_total[...].astype(bf16)
        for number in range(len(products)):
            copy_of(number).wait()


def mlp(normed, cotangent, hidden_grad, first_units, down_units):
    length, model_width = normed.shape
    parts, _, units, _ = first_units.shape
    total = parts * units
    group = 1
    while group * units % 128 or (group < parts and 2 * group * units * length <= 768 * 512):
        group *= 2
    tile = group * units
    first = lambda which: pl.BlockSpec(
        (group, 1, units, model_width), lambda i: (i, which, 0, 0)
    )
    weights = [first(0), first(1), pl.BlockSpec((tile, model_width), lambda i: (i, 0))]
    whole = jax.ShapeDtypeStruct((length, model_width), bf16)
    return pl.pallas_call(
        mlp_kernel,
        grid=(total // tile,),
        out_shape=[
            whole,
            whole,
            jax.ShapeDtypeStruct((parts, 3, units, model_width), bf16),
        ],
        in_specs=vmem_specs(2) + [pl.BlockSpec((length, tile), lambda i: (0, i))] + weights,
        out_specs=vmem_specs(2) + [pl.BlockSpec(memory_space=pl.ANY)],
        scratch_shapes=[pltpu.VMEM((length, model_width), f32)] * 2
        + [pltpu.VMEM((length, tile), bf16)] * 3
        + [pltpu.VMEM((3, group, units, model_width), bf16), pltpu.SemaphoreType.DMA((3,))],
        compiler_params=pltpu.CompilerParams(vmem_limit_bytes=vmem_limit),
        name="mlp",
    )(normed, cotangent, hidden_grad, first_units, first_units, down_units)


def body(
    sizes,
    tokens,
    segment_ids,
    mixer_gain,
    branch_weight,
    input_weight,
    output_weight,
    conv_weight,
    conv_bias,
    decay_gate,
    decay_bias,
    input_gate,
    input_bias,
    decay_param,
    mlp_gain,
    hidden_gate,
    hidden_up,
    hidden_down,
    cotangent,
):
    n_rows, n_blk = sizes
    own_tokens, own_grad = tokens[0], cotangent[0]
    segments = segment_ids[0]
    tok_count, model_width = own_tokens.shape
    width = conv_weight.shape[1]
    wide = round_up(width + 2)
    heads, block, _ = decay_gate.shape
    tiles = column_tiles(width, wide, block)
    row, blk = lax.axis_index("rows"), lax.axis_index("blk")
    square = (tok_count, model_width)
    shard = branch_weight.shape[0]
    units = hidden_gate.shape[0]

    (column_parts,) = local_kernel(
        functools.partial(split_columns_kernel, width, wide),
        "split_columns",
        (input_weight, branch_weight, output_weight, mixer_gain[:, None], mlp_gain[:, None]),
        [((n_blk, shard, 3 * wide), bf16)],
    )
    columns = swap_blk(column_parts).reshape(n_blk * shard, 3 * wide)
    weights = local_kernel(
        dense_kernel, "dense_gates", (decay_gate, input_gate), [((wide, wide), bf16)] * 4
    )
    down_units = lax.all_gather(hidden_down, "rows", axis=0, tiled=True)
    columns, token_own, grad_own, first_own, *weights = tie(
        columns,
        own_tokens,
        for_all(own_grad, n_blk),
        jnp.concatenate([hidden_gate, hidden_up], axis=0),
        *weights,
    )
    both_columns = lax.all_gather(columns[:, : 2 * wide], "rows", axis=0, tiled=True)
    output_columns = lax.all_gather(columns[:, 2 * wide :], "rows", axis=0, tiled=True)
    tokens_all, down_units = ring_blk(token_own, n_blk, down_units)
    tokens_all, grad_own, first_own = tie(tokens_all, grad_own, first_own)
    out_grad = swap_blk(grad_own).reshape(n_blk * tok_count, model_width)
    first_units = lax.all_gather(first_own, "rows", axis=0, tiled=True)
    first_units = first_units.reshape(n_rows, 2, units, model_width)

    masks = [jnp.ones_like(segments, dtype=f32)]
    for tap in range(1, 4):
        masks.append(
            jnp.concatenate(
                [jnp.zeros((tap,), f32), (segments[tap:] == segments[:-tap]).astype(f32)]
            )
        )
    masks.append(1.0 - masks[1])
    masks = jnp.pad(jnp.stack(masks, axis=1), ((0, 8), (0, 3)))
    vectors = jnp.concatenate(
        [
            conv_weight,
            conv_bias[None],
            decay_bias[None],
            input_bias[None],
            scale_c * jax.nn.softplus(-decay_param)[None],
        ],
        axis=0,
    )
    vectors = jnp.pad(vectors, ((0, 0), (0, wide - width)), constant_values=1.0)
    mixer_normed, signal, branch_pre, gains = local_kernel(
        functools.partial(mixer_in_kernel, width),
        "mixer_in",
        (tokens_all, both_columns),
        [
            (tokens_all.shape, bf16),
            ((n_blk * tok_count, wide), bf16),
            ((n_blk * tok_count, wide), f32),
            ((2, model_width), f32),
        ],
    )
    mixer_gains, mlp_gains = gains[0:1], gains[1:2]
    states, state_values, conv_out, decay_rate, input_rate = recur_forward(
        signal, masks, vectors, weights, tiles
    )
    mixed = (gelu_tanh(branch_pre) * state_values.astype(f32)).astype(bf16)
    mid_partial = mm(mixed, output_columns, ((1,), (1,))).astype(bf16)
    mid_partial, out_grad = tie(mid_partial, out_grad)
    mid_parts = ring_sum(mid_partial, n_blk)
    residual_mid, own_normed = local_kernel(
        mid_norm_kernel,
        "mid_norm",
        (mlp_gains, own_tokens, *mid_parts),
        [(square, f32), (square, bf16)],
    )

    mlp_normed = ring_blk(own_normed, n_blk)
    hidden_grad = mm(out_grad, down_units, ((1,), (1,)))
    normed_partial, out_partial, unit_sums = mlp(
        mlp_normed, out_grad, hidden_grad, first_units, down_units
    )
    normed_parts = ring_sum(normed_partial, n_blk)
    unit_sums = lax.psum_scatter(
        unit_sums.reshape(n_rows * 3 * units, model_width),
        "rows",
        scatter_dimension=0,
        tiled=True,
    )

    mid_grad, own_sent, mlp_gain_part = local_kernel(
        mid_grad_kernel,
        "mid_grad",
        (mlp_gains, residual_mid, own_grad, *normed_parts),
        [(square, f32), (square, bf16), ((8, model_width), f32)],
    )
    mid_sent = ring_blk(own_sent, n_blk)

    mid_sent, out_partial = tie(mid_sent, out_partial)
    out_parts = swap_blk(out_partial.reshape(n_blk, tok_count, model_width))
    mixed_grad = mm(mid_sent, output_columns, ((1,), (0,)))
    branch_act, branch_slope = gelu_parts(branch_pre)
    state_grad = (mixed_grad * branch_act).astype(bf16)
    branch_grad = (mixed_grad * state_values.astype(f32) * branch_slope).astype(bf16)
    early_sum = column_grads((mid_sent, mixer_normed), (mixed, branch_grad), n_rows, n_blk)
    early_shape = early_sum.shape[1:]
    early_sum = lax.psum_scatter(
        early_sum.reshape(-1, wide), "rows", scatter_dimension=0, tiled=True
    ).reshape(early_shape)
    late_sum, sums, gain_sums, gate_sums, token_sent = mixer_backward(
        (state_grad, branch_grad, masks, vectors, mlp_gain_part),
        (
            signal,
            states,
            conv_out,
            decay_rate,
            input_rate,
            *weights,
            both_columns,
            mixer_normed,
            tokens_all,
        ),
        n_rows,
        n_blk,
        tiles,
        (2, heads, block, block),
    )
    token_sent, out_parts, unit_sums, late_sum, sums, gain_sums, gate_sums = tie(
        token_sent, out_parts, unit_sums, late_sum, sums, gain_sums, gate_sums
    )
    token_parts = swap_blk(token_sent)
    vector_sums = sums.reshape(8, 8, wide).sum(axis=1)
    late_sum, (vector_sums, gain_sums) = sum_columns(late_sum, n_rows, [vector_sums, gain_sums])
    column_sums = jnp.concatenate([early_sum, late_sum], axis=1)
    gate_sums = [add_from(gate_sums[number], n_rows, 1, bf16) for number in range(2)]
    *gate_sums, token_parts, column_sums, gain_sums = tie(
        *gate_sums, token_parts, column_sums, gain_sums
    )
    one_way = bits_of(n_rows)[1:]
    over_blk = bits_of(n_blk)
    for at in range(max(len(one_way), len(over_blk))):
        if at < len(one_way):
            for number, order in enumerate((one_way, one_way[::-1])):
                gate_sums[number] = add_from(gate_sums[number], n_rows, order[at], bf16)
        if at < len(over_blk):
            moved = lax.ppermute(gain_sums, "blk", flip(n_blk, over_blk[at]))
            gain_sums = gain_sums + moved
        *gate_sums, gain_sums = tie(*gate_sums, gain_sums)
    vector_sums = vector_sums[:, :width]
    (token_grad,) = local_kernel(
        token_grad_kernel,
        "token_grad",
        (mixer_gains, own_tokens, mid_grad, token_parts),
        [(square, f32)],
    )
    output_weight_grad, branch_weight_grad, input_weight_grad = local_kernel(
        functools.partial(join_columns_kernel, width),
        "join_columns",
        (swap_blk(column_sums),),
        [((shard, n_blk * width), f32)] * 3,
    )
    block_out = (residual_mid + out_parts.astype(f32).sum(axis=0)).astype(bf16)

    gain_sums = lax.dynamic_slice_in_dim(
        gain_sums, (row * n_blk + blk) * mixer_gain.shape[0], mixer_gain.shape[0], axis=1
    )

    return (
        block_out[None],
        token_grad[None],
        gain_sums[0],
        branch_weight_grad,
        input_weight_grad,
        output_weight_grad,
        vector_sums[4:8],
        vector_sums[3],
        gate_sums[0],
        vector_sums[1],
        gate_sums[1],
        vector_sums[2],
        scale_c * jax.nn.sigmoid(-decay_param) * vector_sums[0],
        gain_sums[1],
        unit_sums[:units].astype(f32),
        unit_sums[units : 2 * units].astype(f32),
        unit_sums[2 * units :].astype(f32),
    )


def solution(mesh):
    by_all = P(("rows", "blk"))
    by_all_rows = P(("rows", "blk"), None)
    tokens_spec = P("rows", "blk", None)
    by_blk = P("blk")
    by_blk_heads = P("blk", None, None)
    taps = P(None, "blk")
    recurrence = (taps, by_blk, by_blk_heads, by_blk, by_blk_heads, by_blk, by_blk)
    return jax.shard_map(
        functools.partial(body, (mesh.shape["rows"], mesh.shape["blk"])),
        mesh=mesh,
        in_specs=(tokens_spec, P("rows", None), by_all)
        + (by_all_rows,) * 3
        + recurrence
        + (by_all,)
        + (by_all_rows,) * 3
        + (tokens_spec,),
        out_specs=(tokens_spec, tokens_spec, by_all)
        + (by_all_rows,) * 3
        + recurrence
        + (by_all,)
        + (by_all_rows,) * 3,
        check_vma=False,
    )
```

```python
import functools

import jax
import jax.numpy as jnp
from jax import lax
from jax.experimental import pallas as pl
from jax.experimental.pallas import tpu as pltpu
from jax.sharding import PartitionSpec as P

epsilon = 1e-06
scale_c = 8.0
bf16 = jnp.bfloat16
f32 = jnp.float32
chunk = 64
vmem_limit = 60 * 1024 * 1024


def rms_scale(values):
    return lax.rsqrt(jnp.mean(values * values, axis=-1, keepdims=True) + epsilon)


def gelu_tanh(values):
    return jax.nn.gelu(values, approximate=True)


def gelu_parts(values):
    slope, cubic = 0.7978845608028654, 0.044715
    square = values * values
    bend = jnp.tanh(slope * values * (1.0 + cubic * square))
    lift = 0.5 + 0.5 * bend
    turn = 0.5 * values * (1.0 - bend * bend) * (slope * (1.0 + 3.0 * cubic * square))
    return values * lift, lift + turn


def mm(left, right, dims):
    return lax.dot_general(left, right, (dims, ((), ())), preferred_element_type=f32)


def split_bf16(value):
    high = value.astype(bf16)
    return high, (value - high.astype(f32)).astype(bf16)


def tie(*values):
    return lax.optimization_barrier(values)


def flip(size, bit):
    return [(place, place ^ bit) for place in range(size)]


def bits_of(size):
    found, bit = [], 1
    while bit < size:
        found.append(bit)
        bit *= 2
    return found


def swap_blk(parts):
    return lax.all_to_all(parts, "blk", split_axis=0, concat_axis=0, tiled=True)


def ring_blk(part, size, beside=None):
    me, rows = lax.axis_index("blk"), part.shape[0]
    whole = jnp.zeros((size * rows,) + part.shape[1:], part.dtype)
    whole = lax.dynamic_update_slice_in_dim(whole, part, me * rows, axis=0)
    for step in range(1, size):
        part = lax.ppermute(part, "blk", [(place, (place + 1) % size) for place in range(size)])
        if step == 1 and beside is not None:
            part, beside = tie(part, beside)
        place = (me - step) % size
        whole = lax.dynamic_update_slice_in_dim(whole, part, place * rows, axis=0)
    return whole if beside is None else (whole, beside)


def ring_sum(partial, size, first=None):
    me, rows = lax.axis_index("blk"), partial.shape[0] // size
    pick = lambda place: lax.dynamic_slice_in_dim(partial, place % size * rows, rows, axis=0)
    total = pick(me - 1 + size) if first is None else first
    for step in range(1, size):
        total = lax.ppermute(total, "blk", [(place, (place + 1) % size) for place in range(size)])
        if step < size - 1:
            total = (total.astype(f32) + pick(me - 1 - step + size).astype(f32)).astype(bf16)
    return total, pick(me)


def for_all(part, size):
    return jnp.broadcast_to(part[None], (size,) + part.shape)


def halve(total, size, bit, left):
    axis = left.index(bit)
    left.remove(bit)
    mine = (lax.axis_index("rows") // bit) % 2
    away = lax.dynamic_index_in_dim(total, 1 - mine, axis, keepdims=False)
    keep = lax.dynamic_index_in_dim(total, mine, axis, keepdims=False)
    got = lax.ppermute(away, "rows", flip(size, bit))
    return (keep.astype(f32) + got.astype(f32)).astype(bf16)


def sum_columns(away, keep, size, beside):
    left = list(reversed(bits_of(size)))[:-1]
    got = lax.ppermute(away, "rows", flip(size, 1))
    total = (keep.astype(f32) + got.astype(f32)).astype(bf16)
    total = total.reshape((2,) * len(left) + total.shape[1:])
    beside = [add_from(value, size, 1) for value in beside]
    half, order = total.shape[-1] // 2, bits_of(size)[1:]
    found = []
    for cut, bits in ((total[..., :half], order), (total[..., half:], order[::-1])):
        rest = list(left)
        found.append([cut, bits, rest])
    for at in range(len(order)):
        for piece in found:
            piece[0] = halve(piece[0], size, piece[1][at], piece[2])
        beside = [add_from(value, size, order[at]) for value in beside]
        found[0][0], found[1][0], *beside = tie(found[0][0], found[1][0], *beside)
    return jnp.concatenate([found[0][0], found[1][0]], axis=-1), beside


def add_from(value, size, bit, wire=f32):
    return value + lax.ppermute(value.astype(wire), "rows", flip(size, bit)).astype(f32)


def split_columns_kernel(
    width, wide, input_ref, branch_ref, output_ref, mixer_ref, mlp_ref, both_ref
):
    parts, shard, _ = both_ref.shape
    both_ref[...] = jnp.zeros_like(both_ref)
    turn = lax.broadcasted_iota(jnp.int32, (shard, shard), 0) == lax.broadcasted_iota(
        jnp.int32, (shard, shard), 1
    )

    def column(ref):
        value = jnp.where(turn, ref[...].astype(f32), 0.0)
        return jnp.sum(value, axis=1, keepdims=True).astype(bf16)

    mixer_column, mlp_column = column(mixer_ref), column(mlp_ref)
    for part in range(parts):
        cut = slice(part * width, (part + 1) * width)
        both_ref[part, :, :width] = input_ref[:, cut]
        both_ref[part, :, wide : wide + width] = branch_ref[:, cut]
        both_ref[part, :, 2 * wide : 2 * wide + width] = output_ref[:, cut]
        both_ref[part, :, width : width + 1] = mixer_column
        both_ref[part, :, width + 1 : width + 2] = mlp_column


def join_columns_kernel(width, parts_ref, *out_refs):
    for part in range(parts_ref.shape[0]):
        cut = slice(part * width, (part + 1) * width)
        for number, out_ref in enumerate(out_refs):
            out_ref[:, cut] = parts_ref[part, number, :, :width].astype(f32)


def mixer_in_kernel(width, tokens_ref, columns_ref, normed_ref, signal_ref, branch_ref, gains_ref):
    step = 256
    begin = width // 128 * 128
    turned = columns_ref[:, begin : begin + 128].astype(f32).T
    gains_ref[...] = turned[width - begin : width - begin + 2, :]
    gain = gains_ref[0:1, :]

    def rows_step(index, carry):
        here = pl.ds(pl.multiple_of(index * step, step), step)
        values = tokens_ref[here, :].astype(f32)
        normed_ref[here, :] = (values * rms_scale(values) * gain).astype(bf16)
        value = mm(normed_ref[here, :], columns_ref[...], ((1,), (0,)))
        wide = signal_ref.shape[1]
        signal_ref[here, :] = value[:, :wide].astype(bf16)
        branch_ref[here, :] = value[:, wide:]
        return carry

    lax.fori_loop(0, tokens_ref.shape[0] // step, rows_step, 0)


def sum_parts(parts_ref, here):
    total = parts_ref[0, here, :].astype(f32)
    for part in range(1, parts_ref.shape[0]):
        total = total + parts_ref[part, here, :].astype(f32)
    return total


def mid_norm_kernel(gain_ref, tokens_ref, one_ref, two_ref, mid_ref, normed_ref):
    step = 128

    def rows_step(index, carry):
        here = pl.ds(pl.multiple_of(index * step, step), step)
        values = tokens_ref[here, :].astype(f32) + one_ref[here, :].astype(f32)
        values = values + two_ref[here, :].astype(f32)
        mid_ref[here, :] = values
        normed = (values * rms_scale(values) * gain_ref[...]).astype(bf16)
        normed_ref[here, :] = normed
        return carry

    lax.fori_loop(0, tokens_ref.shape[0] // step, rows_step, 0)


def fold8(value):
    return value.reshape(value.shape[0] // 8, 8, value.shape[1]).sum(axis=0)


def norm_back(grad, values, gain):
    scale = rms_scale(values)
    product = grad * values
    factor = scale * scale * scale * jnp.mean(product * gain, axis=-1, keepdims=True)
    return scale * (grad * gain) - values * factor, product * scale


def mid_grad_kernel(
    gain_ref, mid_ref, cotangent_ref, one_ref, two_ref, grad_ref, sent_ref, sums_ref
):
    step = 128
    sums_ref[...] = jnp.zeros_like(sums_ref)

    def rows_step(index, carry):
        here = pl.ds(pl.multiple_of(index * step, step), step)
        grad = one_ref[here, :].astype(f32) + two_ref[here, :].astype(f32)
        change, terms = norm_back(grad, mid_ref[here, :], gain_ref[...])
        sums_ref[...] += fold8(terms)
        result = cotangent_ref[here, :].astype(f32) + change
        grad_ref[here, :] = result
        sent = result.astype(bf16)
        sent_ref[here, :] = sent
        return carry

    lax.fori_loop(0, mid_ref.shape[0] // step, rows_step, 0)


def token_grad_kernel(gain_ref, tokens_ref, mid_grad_ref, parts_ref, grad_ref):
    step = 32

    def rows_step(index, carry):
        here = pl.ds(pl.multiple_of(index * step, step), step)
        values = tokens_ref[here, :].astype(f32)
        change, _ = norm_back(sum_parts(parts_ref, here), values, gain_ref[...])
        grad_ref[here, :] = mid_grad_ref[here, :] + change
        return carry

    lax.fori_loop(0, tokens_ref.shape[0] // step, rows_step, 0)


def vmem_specs(count):
    return [pl.BlockSpec(memory_space=pltpu.VMEM)] * count


def local_kernel(kernel, name, operands, outs, scratch=()):
    return pl.pallas_call(
        kernel,
        out_shape=[jax.ShapeDtypeStruct(shape, kind) for shape, kind in outs],
        in_specs=[pl.BlockSpec(memory_space=pltpu.VMEM)] * len(operands),
        out_specs=[pl.BlockSpec(memory_space=pltpu.VMEM)] * len(outs),
        scratch_shapes=list(scratch),
        compiler_params=pltpu.CompilerParams(vmem_limit_bytes=vmem_limit),
        name=name,
    )(*operands)


def round_up(value):
    return -(-value // 128) * 128


def column_tiles(width, wide, block):
    tiles = []
    for start in range(0, wide, 256):
        stop = min(start + 256, wide)
        low = (start // block) * block
        high = ((min(stop, width) - 1) // block + 1) * block
        tiles.append((start, stop, low // 128 * 128, min(round_up(high), wide)))
    return tiles


def one_minus_exp(value):
    series = 1.0 + value * (1.0 / 8.0)
    for term in (7.0, 6.0, 5.0, 4.0, 3.0, 2.0):
        series = 1.0 + value * (1.0 / term) * series
    return jnp.where(value > -0.3, -value * series, 1.0 - jnp.exp(value))


def shift_down(tile, count, fill):
    moved = pltpu.roll(tile, count, 0)
    row = lax.broadcasted_iota(jnp.int32, tile.shape, 0)
    return jnp.where(row < count, fill, moved)


def shift_up(tile, count, fill):
    moved = pltpu.roll(tile, tile.shape[0] - count, 0)
    row = lax.broadcasted_iota(jnp.int32, tile.shape, 0)
    return jnp.where(row >= tile.shape[0] - count, fill, moved)


def blocked_product(first, second, weights, tiles, store, length, turned=False):
    step = 256

    def rows_step(index, carry):
        rows = pl.ds(pl.multiple_of(index * step, step), step)
        for start, stop, low, high in tiles:
            total = None
            for (high_ref, low_ref), (w_high, w_low) in zip((first, second), weights):
                if high_ref is None:
                    continue
                a_high = high_ref[rows, low:high]
                a_low = low_ref[rows, low:high]
                cut = (slice(start, stop), slice(low, high))
                cut = cut if turned else cut[::-1]
                b_high, b_low = w_high[cut], w_low[cut]
                dims = ((1,), (1,)) if turned else ((1,), (0,))
                part = mm(a_high, b_high, dims) + mm(a_high, b_low, dims) + mm(a_low, b_high, dims)
                total = part if total is None else total + part
            store(rows, slice(start, stop), total)
        return carry

    lax.fori_loop(0, length // step, rows_step, 0)


def recur_forward_kernel(
    tiles,
    signal_ref,
    masks_ref,
    vectors_ref,
    decay_high,
    decay_low,
    input_high,
    input_low,
    states_ref,
    values_ref,
    conv_ref,
    decay_rate_ref,
    input_rate_ref,
    padded,
    conv_high,
    conv_low,
):
    length, width = signal_ref.shape
    count = length // chunk
    padded[0:8, :] = jnp.zeros((8, width), f32)

    def pad_step(index, carry):
        begin = pl.multiple_of(index * chunk, chunk)
        here = pl.ds(begin, chunk)
        padded[pl.ds(begin + 8, chunk), :] = signal_ref[here, :].astype(f32)
        return carry

    lax.fori_loop(0, count, pad_step, 0)

    def conv_step(index, carry):
        begin = pl.multiple_of(index * chunk, chunk)
        rows = pl.ds(begin, chunk)
        window = padded[pl.ds(begin, chunk + 8), :]
        total = vectors_ref[4:5, :] + vectors_ref[0:1, :] * window[8:, :]
        for tap in range(1, 4):
            total = total + vectors_ref[tap : tap + 1, :] * (
                window[8 - tap : 8 - tap + chunk, :] * masks_ref[rows, tap : tap + 1]
            )
        conv_ref[rows, :] = total
        high, low = split_bf16(total)
        conv_high[rows, :] = high
        conv_low[rows, :] = low
        return carry

    lax.fori_loop(0, count, conv_step, 0)

    def store_decay(rows, columns, value):
        decay_rate_ref[rows, columns] = jax.nn.sigmoid(value + vectors_ref[5:6, columns])

    def store_input(rows, columns, value):
        input_rate_ref[rows, columns] = jax.nn.sigmoid(value + vectors_ref[6:7, columns])

    nothing = (None, None)
    blocked_product(
        (conv_high, conv_low), nothing, ((decay_high, decay_low), nothing), tiles, store_decay, length
    )
    blocked_product(
        (conv_high, conv_low), nothing, ((input_high, input_low), nothing), tiles, store_input, length
    )

    def scan_step(index, state):
        begin = pl.multiple_of(index * 8, 8)
        rows = pl.ds(begin, 8)
        restart = masks_ref[rows, 4:5]
        keep = 1.0 - restart
        log_decay = -vectors_ref[7:8, :] * decay_rate_ref[rows, :]
        mult = restart + keep * jnp.sqrt(one_minus_exp(2.0 * log_decay))
        carried = keep * jnp.exp(log_decay)
        total = mult * input_rate_ref[rows, :] * conv_ref[rows, :]
        for count_rows in (1, 2, 4):
            total = total + carried * shift_down(total, count_rows, 0.0)
            carried = carried * shift_down(carried, count_rows, 1.0)
        total = total + carried * state
        states_ref[rows, :] = total
        return total[7:8, :]

    lax.fori_loop(0, length // 8, scan_step, jnp.zeros((1, width), f32), unroll=4)

    def values_step(index, carry):
        begin = pl.multiple_of(index * chunk, chunk)
        here = pl.ds(begin, chunk)
        values_ref[here, :] = states_ref[pl.ds(begin, chunk), :].astype(bf16)
        return carry

    lax.fori_loop(0, count, values_step, 0)


def mixer_backward_kernel(
    tiles,
    core_ref,
    state_grad_ref,
    branch_grad_ref,
    masks_ref,
    vectors_ref,
    mlp_ref,
    signal_any,
    states_any,
    conv_any,
    decay_rate_any,
    input_rate_any,
    decay_high_any,
    decay_low_any,
    input_high_any,
    input_low_any,
    both_any,
    normed_any,
    tokens_any,
    away_ref,
    keep_ref,
    totals_ref,
    gains_ref,
    gates_ref,
    token_ref,
    signal_ref,
    states_ref,
    conv_ref,
    decay_rate_ref,
    input_rate_ref,
    decay_high,
    decay_low,
    input_high,
    input_low,
    both_ref,
    normed_ref,
    tokens_ref,
    both_grad_ref,
    padded,
    grads,
    earlier,
    decay_pre_ref,
    input_pre_ref,
    decay_pre_high,
    decay_pre_low,
    input_pre_high,
    input_pre_low,
    conv_high,
    conv_low,
    dense,
    sums_ref,
    gain_sums,
    arrived,
):
    fetched = [
        (signal_any, signal_ref),
        (states_any, states_ref),
        (conv_any, conv_ref),
        (decay_rate_any, decay_rate_ref),
        (input_rate_any, input_rate_ref),
        (decay_high_any, decay_high),
        (decay_low_any, decay_low),
        (input_high_any, input_high),
        (input_low_any, input_low),
        (both_any, both_ref),
        (normed_any, normed_ref),
    ]
    copies = [
        pltpu.make_async_copy(source, target, arrived.at[number])
        for number, (source, target) in enumerate(fetched)
    ]
    for copy in copies:
        copy.start()
    length, width = grads.shape[0] - 8, grads.shape[1]
    count = length // chunk
    padded[0:8, :] = jnp.zeros((8, width), f32)
    earlier[0:8, :] = jnp.zeros((8, width), f32)
    grads[length:, :] = jnp.zeros((8, width), f32)
    sums_ref[...] = jnp.zeros_like(sums_ref)

    for copy in copies[:5]:
        copy.wait()

    def pad_step(index, carry):
        begin = pl.multiple_of(index * chunk, chunk)
        here = pl.ds(begin, chunk)
        padded[pl.ds(begin + 8, chunk), :] = signal_ref[here, :].astype(f32)
        earlier[pl.ds(begin + 8, chunk), :] = states_ref[here, :]
        grads[here, :] = state_grad_ref[here, :].astype(f32)
        both_grad_ref[here, width:] = branch_grad_ref[here, :]
        return carry

    lax.fori_loop(0, count, pad_step, 0)

    def scan_step(index, later):
        begin = pl.multiple_of(length - 8 - index * 8, 8)
        rows = pl.ds(begin, 8)
        restart = masks_ref[rows, 4:5]
        keep = 1.0 - restart
        decay_rate = decay_rate_ref[rows, :]
        input_rate = input_rate_ref[rows, :]
        conv_out = conv_ref[rows, :]
        log_decay = -vectors_ref[7:8, :] * decay_rate
        decay = jnp.exp(log_decay)
        root = jnp.sqrt(one_minus_exp(2.0 * log_decay))
        mult = restart + keep * root
        carried = keep * decay
        flow = grads[rows, :]
        reach = shift_up(carried, 1, 1.0)
        for count_rows in (1, 2, 4):
            flow = flow + reach * shift_up(flow, count_rows, 0.0)
            reach = reach * shift_up(reach, count_rows, 1.0)
        flow = flow + reach * later
        window = earlier[pl.ds(begin, 16), :]
        before = window[7:15, :]
        flow_rate = flow * input_rate
        mult_grad = flow_rate * conv_out
        log_grad = keep * (flow * before * decay - mult_grad * decay * decay / root)
        rate_log = decay_rate * log_grad
        decay_pre = -vectors_ref[7:8, :] * rate_log * (1.0 - decay_rate)
        input_pre = mult_grad * mult * (1.0 - input_rate)
        grads[rows, :] = flow_rate * mult
        decay_pre_ref[rows, :] = decay_pre
        input_pre_ref[rows, :] = input_pre
        sums_ref[0:8, :] += rate_log
        sums_ref[8:16, :] += decay_pre
        sums_ref[16:24, :] += input_pre
        return carried[0:1, :] * flow[0:1, :]

    lax.fori_loop(0, length // 8, scan_step, jnp.zeros((1, width), f32), unroll=4)

    for copy in copies[5:9]:
        copy.wait()

    def split_step(index, carry):
        rows = pl.ds(pl.multiple_of(index * chunk, chunk), chunk)
        decay_pre_high[rows, :], decay_pre_low[rows, :] = split_bf16(decay_pre_ref[rows, :])
        input_pre_high[rows, :], input_pre_low[rows, :] = split_bf16(input_pre_ref[rows, :])
        conv_high[rows, :], conv_low[rows, :] = split_bf16(conv_ref[rows, :])
        return carry

    lax.fori_loop(0, count, split_step, 0)

    def store(rows, columns, value):
        grads[rows, columns] += value

    blocked_product(
        (decay_pre_high, decay_pre_low),
        (input_pre_high, input_pre_low),
        ((decay_high, decay_low), (input_high, input_low)),
        tiles,
        store,
        length,
        True,
    )

    def conv_step(index, carry):
        begin = pl.multiple_of(index * chunk, chunk)
        rows = pl.ds(begin, chunk)
        grad_window = grads[pl.ds(begin, chunk + 8), :]
        mask_window = masks_ref[pl.ds(begin, chunk + 8), :]
        signal_window = padded[pl.ds(begin, chunk + 8), :]
        here = grad_window[:chunk, :]
        result = vectors_ref[0:1, :] * here
        sums_ref[24:32, :] += fold8(here)
        sums_ref[32:40, :] += fold8(here * signal_window[8:, :])
        for tap in range(1, 4):
            masked = grad_window * mask_window[:, tap : tap + 1]
            result = result + vectors_ref[tap : tap + 1, :] * masked[tap : tap + chunk, :]
            sums_ref[32 + 8 * tap : 40 + 8 * tap, :] += fold8(
                masked[:chunk, :] * signal_window[8 - tap : 8 - tap + chunk, :]
            )
        here = pl.ds(begin, chunk)
        both_grad_ref[here, :width] = result.astype(bf16)
        return carry

    lax.fori_loop(0, count, conv_step, 0)
    copies[9].wait()
    copies[10].wait()
    each = keep_ref.shape[1] * keep_ref.shape[3]

    def late_step(index, carry):
        for side, out_ref in enumerate((keep_ref, away_ref)):
            place = 2 * index + (core_ref[0] ^ side)
            rows = pl.ds(pl.multiple_of(place * each, each), each)
            value = mm(normed_ref[:, rows], both_grad_ref[:, :width], ((0,), (0,))).astype(bf16)
            out_ref[index, :, 0] = value.reshape(out_ref.shape[1], *out_ref.shape[3:])
        return carry

    lax.fori_loop(0, keep_ref.shape[0], late_step, 0)
    parts, rows, _ = token_ref.shape
    gain_sums[...] = jnp.zeros_like(gain_sums)

    def token_step(index, carry):
        here = pl.ds(pl.multiple_of(index * rows, rows), rows)
        copy = pltpu.make_async_copy(tokens_any.at[here, :], tokens_ref, arrived.at[len(fetched)])
        copy.start()
        grad = mm(both_grad_ref[here, :], both_ref[...], ((1,), (1,)))
        copy.wait()
        values = tokens_ref[...].astype(f32)
        gain_sums[...] += fold8(values * rms_scale(values) * grad)
        token_ref[index] = grad.astype(bf16)
        return carry

    lax.fori_loop(0, parts, token_step, 0)
    heads, block = gates_ref.shape[1:3]
    for gate, (high, low) in enumerate(
        ((decay_pre_high, decay_pre_low), (input_pre_high, input_pre_low))
    ):
        for start, stop, first, last in tiles:
            total = None
            for left, right in ((conv_high, high), (conv_high, low), (conv_low, high)):
                part = mm(left[:, first:last], right[:, start:stop], ((0,), (0,)))
                total = part if total is None else total + part
            dense[first:last, start:stop] = total
        for head in range(heads):
            cut = slice(head * block, (head + 1) * block)
            gates_ref[gate, head] = dense[cut, cut]
    for row in range(totals_ref.shape[0]):
        total = sums_ref[8 * row : 8 * row + 8, :].sum(axis=0, keepdims=True)
        totals_ref[row : row + 1, :] = total
    for row, total in enumerate((gain_sums, mlp_ref)):
        gains_ref[row : row + 1, :] = total[...].sum(axis=0, keepdims=True)


def recur_forward(signal, masks, vectors, weights, tiles):
    length, width = signal.shape
    whole = ((length, width), f32)
    return local_kernel(
        functools.partial(recur_forward_kernel, tiles),
        "recur_forward",
        (signal, masks, vectors, *weights),
        [whole, ((length, width), bf16), whole, whole, whole],
        [
            pltpu.VMEM((length + 8, width), f32),
            pltpu.VMEM((length, width), bf16),
            pltpu.VMEM((length, width), bf16),
        ],
    )


def mixer_backward(core, resident, fetched, size, parts, tiles, gates_shape):
    length, wide = resident[0].shape
    model_width = fetched[-1].shape[1]
    outs = [
        ((size // 2, parts, 1, model_width // size // parts, wide), bf16),
        ((size // 2, parts, 1, model_width // size // parts, wide), bf16),
        ((8, wide), f32),
        ((2, model_width), f32),
        (gates_shape, f32),
        ((parts, length // parts, model_width), bf16),
    ]
    padded = pltpu.VMEM((length + 8, wide), f32)
    return pl.pallas_call(
        functools.partial(mixer_backward_kernel, tiles),
        out_shape=[jax.ShapeDtypeStruct(shape, kind) for shape, kind in outs],
        in_specs=[pl.BlockSpec(memory_space=pltpu.SMEM)]
        + vmem_specs(len(resident))
        + [pl.BlockSpec(memory_space=pl.ANY)] * len(fetched),
        out_specs=vmem_specs(len(outs)),
        scratch_shapes=[pltpu.VMEM(value.shape, value.dtype) for value in fetched[:-1]]
        + [pltpu.VMEM((length // parts, model_width), bf16)]
        + [pltpu.VMEM((length, 2 * wide), bf16)]
        + [padded] * 3
        + [pltpu.VMEM((length, wide), f32)] * 2
        + [pltpu.VMEM((length, wide), bf16)] * 6
        + [pltpu.VMEM((wide, wide), f32), pltpu.VMEM((64, wide), f32)]
        + [pltpu.VMEM((8, model_width), f32), pltpu.SemaphoreType.DMA((len(fetched),))],
        compiler_params=pltpu.CompilerParams(vmem_limit_bytes=vmem_limit),
        name="mixer_backward",
    )(core, *resident, *fetched)


def column_grads_kernel(count, *refs):
    for number in range(count):
        value = mm(refs[number][...], refs[count + number][...], ((0,), (0,)))
        shape = refs[-1].shape[:2] + refs[-1].shape[3:]
        refs[-1][:, :, number] = value.astype(bf16).reshape(shape)


def column_grads(lefts, rights, size, parts):
    length, model_width = lefts[0].shape
    wide = rights[0].shape[1]
    each, count = model_width // size, len(lefts)
    block = (2, parts, count, each // parts, wide)
    total = pl.pallas_call(
        functools.partial(column_grads_kernel, count),
        grid=(size // 2,),
        in_specs=[pl.BlockSpec((length, 2 * each), lambda i: (0, i))] * count
        + [pl.BlockSpec((length, wide), lambda i: (0, 0))] * count,
        out_specs=pl.BlockSpec(block, lambda i: (i, 0, 0, 0, 0)),
        out_shape=jax.ShapeDtypeStruct((size,) + block[1:], bf16),
        compiler_params=pltpu.CompilerParams(vmem_limit_bytes=vmem_limit),
        name="column_grads",
    )(*lefts, *rights)
    return total


def dense_kernel(decay_ref, input_ref, decay_high, decay_low, input_high, input_low):
    heads, block, _ = decay_ref.shape
    for ref, high, low in (
        (decay_ref, decay_high, decay_low),
        (input_ref, input_high, input_low),
    ):
        high[...] = jnp.zeros_like(high)
        low[...] = jnp.zeros_like(low)
        for head in range(heads):
            cut = slice(head * block, (head + 1) * block)
            high[cut, cut], low[cut, cut] = split_bf16(ref[head])


def mlp_kernel(
    normed_ref,
    cotangent_any,
    hidden_grad_ref,
    first_any,
    down_any,
    normed_grad_ref,
    out_ref,
    units_any,
    normed_total,
    out_total,
    gate_grads,
    up_grads,
    hidden_all,
    units,
    gate_all,
    up_all,
    down_all,
    cotangent_ref,
    sent,
    arrived,
    cotangent_arrived,
):
    step, steps = pl.program_id(0), pl.num_programs(0)
    length = normed_ref.shape[0]
    group = units.shape[1]
    tile = group * units.shape[2]

    def fetch(at):
        here = pl.ds(at * group, group)
        rows = pl.ds(pl.multiple_of(at * tile, tile), tile)
        return [
            pltpu.make_async_copy(source, target, arrived.at[number, at])
            for number, (source, target) in enumerate(
                (
                    (first_any.at[here, 0], gate_all.at[here]),
                    (first_any.at[here, 1], up_all.at[here]),
                    (down_any.at[rows, :], down_all.at[rows, :]),
                )
            )
        ]

    cotangent_copy = pltpu.make_async_copy(cotangent_any, cotangent_ref, cotangent_arrived)

    @pl.when(step == 0)
    def _():
        for at in range(gate_all.shape[0] // group):
            for copy in fetch(at):
                copy.start()
            if at == 0:
                cotangent_copy.start()
        normed_total[...] = jnp.zeros_like(normed_total)
        out_total[...] = jnp.zeros_like(out_total)

    mine = pl.ds(step * group, group)
    gate_units = lambda: gate_all[mine].reshape(tile, gate_all.shape[2])
    up_units = lambda: up_all[mine].reshape(tile, up_all.shape[2])
    coming = fetch(step)
    coming[0].wait()
    coming[1].wait()

    def rows_step(index, carry):
        here = pl.ds(pl.multiple_of(index * 256, 256), 256)
        normed = normed_ref[here, :]
        gate_act, slope = gelu_parts(mm(normed, gate_units(), ((1,), (1,))))
        up_vals = mm(normed, up_units(), ((1,), (1,)))
        hidden_grad = hidden_grad_ref[here, :]
        gate_grads[here, :] = (hidden_grad * up_vals * slope).astype(bf16)
        up_grads[here, :] = (hidden_grad * gate_act).astype(bf16)
        hidden_all[here, :] = (gate_act * up_vals).astype(bf16)
        normed_total[here, :] += mm(gate_grads[here, :], gate_units(), ((1,), (0,))) + mm(
            up_grads[here, :], up_units(), ((1,), (0,))
        )
        return carry

    lax.fori_loop(0, length // 256, rows_step, 0)
    coming[2].wait()

    def out_step(index, carry):
        here = pl.ds(pl.multiple_of(index * 256, 256), 256)
        down = down_all[pl.ds(pl.multiple_of(step * tile, tile), tile), :]
        out_total[here, :] += mm(hidden_all[here, :], down, ((1,), (0,)))
        return carry

    lax.fori_loop(0, length // 256, out_step, 0)

    @pl.when(step == 0)
    def _():
        cotangent_copy.wait()

    def copy_of(number):
        return pltpu.make_async_copy(
            units.at[number], units_any.at[pl.ds(step * group, group), number], sent.at[number]
        )

    products = ((gate_grads, normed_ref), (up_grads, normed_ref), (hidden_all, cotangent_ref))
    for number, (left, right) in enumerate(products):

        @pl.when(step > 0)
        def _():
            copy_of(number).wait()

        value = mm(left[...], right[...], ((0,), (0,))).astype(bf16)
        units[number] = value.reshape(units.shape[1:])
        copy_of(number).start()

    @pl.when(step == steps - 1)
    def _():
        normed_grad_ref[...] = normed_total[...].astype(bf16)
        out_ref[...] = out_total[...].astype(bf16)
        for number in range(len(products)):
            copy_of(number).wait()


def mlp(normed, cotangent, hidden_grad, first_units, down_units):
    length, model_width = normed.shape
    parts, _, units, _ = first_units.shape
    total = parts * units
    group = 1
    while group * units % 128 or (group < parts and 2 * group * units * length <= 768 * 512):
        group *= 2
    tile = group * units
    whole = jax.ShapeDtypeStruct((length, model_width), bf16)
    return pl.pallas_call(
        mlp_kernel,
        grid=(total // tile,),
        out_shape=[
            whole,
            whole,
            jax.ShapeDtypeStruct((parts, 3, units, model_width), bf16),
        ],
        in_specs=vmem_specs(1)
        + [pl.BlockSpec(memory_space=pl.ANY), pl.BlockSpec((length, tile), lambda i: (0, i))]
        + [pl.BlockSpec(memory_space=pl.ANY)] * 2,
        out_specs=vmem_specs(2) + [pl.BlockSpec(memory_space=pl.ANY)],
        scratch_shapes=[pltpu.VMEM((length, model_width), f32)] * 2
        + [pltpu.VMEM((length, tile), bf16)] * 3
        + [pltpu.VMEM((3, group, units, model_width), bf16)]
        + [pltpu.VMEM((parts, units, model_width), bf16)] * 2
        + [pltpu.VMEM((total, model_width), bf16), pltpu.VMEM((length, model_width), bf16)]
        + [pltpu.SemaphoreType.DMA((3,)), pltpu.SemaphoreType.DMA((3, total // tile))]
        + [pltpu.SemaphoreType.DMA],
        compiler_params=pltpu.CompilerParams(vmem_limit_bytes=vmem_limit),
        name="mlp",
    )(normed, cotangent, hidden_grad, first_units, down_units)


def body(
    sizes,
    tokens,
    segment_ids,
    mixer_gain,
    branch_weight,
    input_weight,
    output_weight,
    conv_weight,
    conv_bias,
    decay_gate,
    decay_bias,
    input_gate,
    input_bias,
    decay_param,
    mlp_gain,
    hidden_gate,
    hidden_up,
    hidden_down,
    cotangent,
):
    n_rows, n_blk = sizes
    own_tokens, own_grad = tokens[0], cotangent[0]
    segments = segment_ids[0]
    tok_count, model_width = own_tokens.shape
    width = conv_weight.shape[1]
    wide = round_up(width + 2)
    heads, block, _ = decay_gate.shape
    tiles = column_tiles(width, wide, block)
    row, blk = lax.axis_index("rows"), lax.axis_index("blk")
    square = (tok_count, model_width)
    shard = branch_weight.shape[0]
    units = hidden_gate.shape[0]

    (column_parts,) = local_kernel(
        functools.partial(split_columns_kernel, width, wide),
        "split_columns",
        (input_weight, branch_weight, output_weight, mixer_gain[None], mlp_gain[None]),
        [((n_blk, shard, 3 * wide), bf16)],
    )
    columns = swap_blk(column_parts).reshape(n_blk * shard, 3 * wide)
    weights = local_kernel(
        dense_kernel, "dense_gates", (decay_gate, input_gate), [((wide, wide), bf16)] * 4
    )
    down_units = lax.all_gather(hidden_down, "rows", axis=0, tiled=True)
    columns, token_own, grad_own, first_own, *weights = tie(
        columns,
        own_tokens,
        for_all(own_grad, n_blk),
        jnp.concatenate([hidden_gate, hidden_up], axis=0),
        *weights,
    )
    both_columns = lax.all_gather(columns[:, : 2 * wide], "rows", axis=0, tiled=True)
    output_columns = lax.all_gather(columns[:, 2 * wide :], "rows", axis=0, tiled=True)
    tokens_all, down_units = ring_blk(token_own, n_blk, down_units)
    tokens_all, grad_own, first_own = tie(tokens_all, grad_own, first_own)
    out_grad = swap_blk(grad_own).reshape(n_blk * tok_count, model_width)
    first_units = lax.all_gather(first_own, "rows", axis=0, tiled=True)
    first_units = first_units.reshape(n_rows, 2, units, model_width)

    masks = [jnp.ones_like(segments, dtype=f32)]
    for tap in range(1, 4):
        masks.append(
            jnp.concatenate(
                [jnp.zeros((tap,), f32), (segments[tap:] == segments[:-tap]).astype(f32)]
            )
        )
    masks.append(1.0 - masks[1])
    masks = jnp.pad(jnp.stack(masks, axis=1), ((0, 8), (0, 3)))
    vectors = jnp.concatenate(
        [
            conv_weight,
            conv_bias[None],
            decay_bias[None],
            input_bias[None],
            scale_c * jax.nn.softplus(-decay_param)[None],
        ],
        axis=0,
    )
    vectors = jnp.pad(vectors, ((0, 0), (0, wide - width)), constant_values=1.0)
    mixer_normed, signal, branch_pre, gains = local_kernel(
        functools.partial(mixer_in_kernel, width),
        "mixer_in",
        (tokens_all, both_columns),
        [
            (tokens_all.shape, bf16),
            ((n_blk * tok_count, wide), bf16),
            ((n_blk * tok_count, wide), f32),
            ((2, model_width), f32),
        ],
    )
    mixer_gains, mlp_gains = gains[0:1], gains[1:2]
    states, state_values, conv_out, decay_rate, input_rate = recur_forward(
        signal, masks, vectors, weights, tiles
    )
    mixed = (gelu_tanh(branch_pre) * state_values.astype(f32)).astype(bf16)
    before = (blk + n_blk - 1) % n_blk * tok_count
    first = lax.dynamic_slice_in_dim(mixed, before, tok_count, axis=0)
    first = mm(first, output_columns, ((1,), (1,))).astype(bf16)
    first, mixed_all, out_grad = tie(first, mixed, out_grad)
    mid_partial = mm(mixed_all, output_columns, ((1,), (1,))).astype(bf16)
    mid_parts = ring_sum(mid_partial, n_blk, first)
    residual_mid, own_normed = local_kernel(
        mid_norm_kernel,
        "mid_norm",
        (mlp_gains, own_tokens, *mid_parts),
        [(square, f32), (square, bf16)],
    )

    mlp_normed = ring_blk(own_normed, n_blk)
    hidden_grad = mm(out_grad, down_units, ((1,), (1,)))
    normed_partial, out_partial, unit_sums = mlp(
        mlp_normed, out_grad, hidden_grad, first_units, down_units
    )
    normed_parts = ring_sum(normed_partial, n_blk)
    unit_sums = lax.psum_scatter(
        unit_sums.reshape(n_rows * 3 * units, model_width),
        "rows",
        scatter_dimension=0,
        tiled=True,
    )

    mid_grad, own_sent, mlp_gain_part = local_kernel(
        mid_grad_kernel,
        "mid_grad",
        (mlp_gains, residual_mid, own_grad, *normed_parts),
        [(square, f32), (square, bf16), ((8, model_width), f32)],
    )
    mid_sent = ring_blk(own_sent, n_blk)

    mid_sent, out_partial = tie(mid_sent, out_partial)
    out_parts = swap_blk(out_partial.reshape(n_blk, tok_count, model_width))
    mixed_grad = mm(mid_sent, output_columns, ((1,), (0,)))
    branch_act, branch_slope = gelu_parts(branch_pre)
    state_grad = (mixed_grad * branch_act).astype(bf16)
    branch_grad = (mixed_grad * state_values.astype(f32) * branch_slope).astype(bf16)
    early_sum = column_grads((mid_sent, mixer_normed), (mixed, branch_grad), n_rows, n_blk)
    early_shape = early_sum.shape[1:]
    early_sum = lax.psum_scatter(
        early_sum.reshape(-1, wide), "rows", scatter_dimension=0, tiled=True
    ).reshape(early_shape)
    away, keep, vector_sums, gain_sums, gate_sums, token_sent = mixer_backward(
        (row % 2).astype(jnp.int32)[None],
        (state_grad, branch_grad, masks, vectors, mlp_gain_part),
        (
            signal,
            states,
            conv_out,
            decay_rate,
            input_rate,
            *weights,
            both_columns,
            mixer_normed,
            tokens_all,
        ),
        n_rows,
        n_blk,
        tiles,
        (2, heads, block, block),
    )
    token_sent, out_parts, unit_sums, away, keep, vector_sums, gain_sums, gate_sums = tie(
        token_sent, out_parts, unit_sums, away, keep, vector_sums, gain_sums, gate_sums
    )
    token_parts = swap_blk(token_sent)
    late_sum, (vector_sums, gain_sums) = sum_columns(
        away, keep, n_rows, [vector_sums, gain_sums]
    )
    column_sums = jnp.concatenate([early_sum, late_sum], axis=1)
    gate_sums = [add_from(gate_sums[number], n_rows, 1, bf16) for number in range(2)]
    *gate_sums, token_parts, column_sums, gain_sums = tie(
        *gate_sums, token_parts, column_sums, gain_sums
    )
    one_way = bits_of(n_rows)[1:]
    over_blk = bits_of(n_blk)
    for at in range(max(len(one_way), len(over_blk))):
        if at < len(one_way):
            for number, order in enumerate((one_way, one_way[::-1])):
                gate_sums[number] = add_from(gate_sums[number], n_rows, order[at], bf16)
        if at < len(over_blk):
            moved = lax.ppermute(gain_sums, "blk", flip(n_blk, over_blk[at]))
            gain_sums = gain_sums + moved
        *gate_sums, gain_sums = tie(*gate_sums, gain_sums)
    vector_sums = vector_sums[:, :width]
    (token_grad,) = local_kernel(
        token_grad_kernel,
        "token_grad",
        (mixer_gains, own_tokens, mid_grad, token_parts),
        [(square, f32)],
    )
    output_weight_grad, branch_weight_grad, input_weight_grad = local_kernel(
        functools.partial(join_columns_kernel, width),
        "join_columns",
        (swap_blk(column_sums),),
        [((shard, n_blk * width), f32)] * 3,
    )
    block_out = (residual_mid + out_parts.astype(f32).sum(axis=0)).astype(bf16)

    gain_sums = lax.dynamic_slice_in_dim(
        gain_sums, (row * n_blk + blk) * mixer_gain.shape[0], mixer_gain.shape[0], axis=1
    )

    return (
        block_out[None],
        token_grad[None],
        gain_sums[0],
        branch_weight_grad,
        input_weight_grad,
        output_weight_grad,
        vector_sums[4:8],
        vector_sums[3],
        gate_sums[0],
        vector_sums[1],
        gate_sums[1],
        vector_sums[2],
        scale_c * jax.nn.sigmoid(-decay_param) * vector_sums[0],
        gain_sums[1],
        unit_sums[:units].astype(f32),
        unit_sums[units : 2 * units].astype(f32),
        unit_sums[2 * units :].astype(f32),
    )


def solution(mesh):
    by_all = P(("rows", "blk"))
    by_all_rows = P(("rows", "blk"), None)
    tokens_spec = P("rows", "blk", None)
    by_blk = P("blk")
    by_blk_heads = P("blk", None, None)
    taps = P(None, "blk")
    recurrence = (taps, by_blk, by_blk_heads, by_blk, by_blk_heads, by_blk, by_blk)
    return jax.shard_map(
        functools.partial(body, (mesh.shape["rows"], mesh.shape["blk"])),
        mesh=mesh,
        in_specs=(tokens_spec, P("rows", None), by_all)
        + (by_all_rows,) * 3
        + recurrence
        + (by_all,)
        + (by_all_rows,) * 3
        + (tokens_spec,),
        out_specs=(tokens_spec, tokens_spec, by_all)
        + (by_all_rows,) * 3
        + recurrence
        + (by_all,)
        + (by_all_rows,) * 3,
        check_vma=False,
    )
```
